128 devices in a mesh: tm: 4 (over z), row: 4 (over y), col: 8 (over x, core).
Axes of the slice: x: 4, y: 4, z: 4, core: 2. Of those that a mesh axis runs over, the one named last changes fastest.
Arguments:
- features: bfloat16 [8, 32, 256, 384], P('tm', 'row', 'col'), may hold values from -6 to 6
- conv_first: bfloat16 [3, 3, 3, 384, 192], replicated, may hold values from -0.0625 to 0.0625
- conv_second: bfloat16 [3, 3, 3, 192, 192], replicated, may hold values from -0.078125 to 0.078125
- shortcut_weight: bfloat16 [384, 192], replicated, may hold values from -0.3125 to 0.3125
- head_weight: bfloat16 [192, 3], replicated, may hold values from -0.4375 to 0.4375
- target_frames: float32 [3, 8, 32, 256], P(None, 'tm', 'row', 'col'), may hold values from -4 to 4
Outputs:
- grad_first: float32 [3, 3, 3, 384, 192], replicated
- grad_second: float32 [3, 3, 3, 192, 192], replicated
- grad_shortcut: float32 [384, 192], replicated
- grad_head: float32 [192, 3], replicated
- loss_mean: float32 [], replicated
The draws below stay inside these ranges and needn't reach their ends.
All inputs are finite; a program needn't handle non-finite values.
Results may differ from the reference program's by a relative error of at most 0.0038.
Values may be sent and summed in bfloat16 or wider, within the bound.
A program may use at most 128 MiB of HBM per device.

```python
import jax
import jax.numpy as jnp
from jax import lax

C_IN = 384
C_MID = 192
COLORS = 3
F_DEV = 2
TILE_H = 8
TILE_W = 32
NFRAMES = 8
NH = 32
NW = 256
N_TM = 4
N_ROW = 4
N_COL = 8


def levels(key, extent, shards, smallest, top_value):
    factor_of, own = 1.0, jax.random.fold_in(key, 6)
    for dim, parts in shards:
        steps = jnp.exp(jax.random.uniform(jax.random.fold_in(own, dim), (parts,), jnp.float32, smallest / len(shards), top_value / len(shards)))
        factor_of = factor_of * jnp.repeat(steps, extent[dim] // parts).reshape([-1 if axis == dim else 1 for axis in range(len(extent))])
    return factor_of


def noise(rng, extent, scale, limit, cuts=(), held_as=jnp.bfloat16):
    values = scale * jax.random.normal(rng, extent, jnp.float32)
    if cuts:
        values = values * levels(rng, extent, cuts, -0.22, 0.18)
    return jnp.clip(values, -limit, limit).astype(held_as)


def setup_inputs(seed: int = 0) -> dict:
    seeds = jax.random.split(jax.random.key(seed), 7)
    features = noise(seeds[0], (NFRAMES, NH, NW, C_IN), 1.0, 6.0, ((0, 4), (1, 4), (2, 8)))
    conv_first = noise(seeds[1], (3, 3, 3, C_IN, C_MID), (27 * C_IN) ** -0.5, 0.0625)
    conv_second = noise(seeds[2], (3, 3, 3, C_MID, C_MID), (27 * C_MID) ** -0.5, 0.078125)
    shortcut_weight = noise(seeds[3], (C_IN, C_MID), C_IN ** -0.5, 0.3125)
    head_weight = noise(seeds[4], (C_MID, COLORS), C_MID ** -0.5, 0.4375)
    target_frames = noise(seeds[5], (COLORS, NFRAMES, NH, NW), 1.0, 4.0, ((1, 4), (2, 4), (3, 8)), jnp.float32)
    return dict(features=features, conv_first=conv_first, conv_second=conv_second, shortcut_weight=shortcut_weight, head_weight=head_weight, target_frames=target_frames)


EPSILON = 1e-06
HUBER_BETA = 0.05
SSIM_CONST_A = 0.0004
SSIM_CONST_B = 0.0036

def normed_silu(values):
    inverse = lax.rsqrt(lax.optimization_barrier(jnp.mean(values * values, axis=-1, keepdims=True)) + EPSILON)
    return jax.nn.silu(values * inverse)

def causal_conv(values, kernel):
    result = lax.conv_general_dilated(values[None].astype(jnp.float32), kernel.astype(jnp.float32), (1, 1, 1), ((2, 0), (1, 1), (1, 1)), dimension_numbers=('NDHWC', 'DHWIO', 'NDHWC'), precision=lax.Precision.HIGHEST)
    return result[0]

def gauss_weights():
    offsets = jnp.arange(11, dtype=jnp.float32) - 5.0
    kernel_taps = jnp.exp(-offsets * offsets / 4.5)
    return kernel_taps / jnp.sum(kernel_taps)

def blur_valid(padded, height, tile_width):
    kernel_taps = gauss_weights()
    row_pass = kernel_taps[0] * padded[..., 0:height, :]
    for offset in range(1, 11):
        row_pass = row_pass + kernel_taps[offset] * padded[..., offset:offset + height, :]
    result = kernel_taps[0] * row_pass[..., 0:tile_width]
    for offset in range(1, 11):
        result = result + kernel_taps[offset] * row_pass[..., offset:offset + tile_width]
    return result

def gauss_blur(values):
    padding = [(0, 0)] * (values.ndim - 2) + [(5, 5), (5, 5)]
    return blur_valid(jnp.pad(values, padding), values.shape[-2], values.shape[-1])

def huber_loss(diff):
    magnitude = jnp.abs(diff)
    return jnp.where(magnitude < HUBER_BETA, 0.5 * diff * diff / HUBER_BETA, magnitude - 0.5 * HUBER_BETA)

def pixel_loss(picture, target, pix_dev):
    mean_x = gauss_blur(picture)
    mean_y = gauss_blur(target)
    var_x = gauss_blur(picture * picture) - mean_x * mean_x
    var_y = gauss_blur(target * target) - mean_y * mean_y
    covar = gauss_blur(picture * target) - mean_x * mean_y
    numer_a = 2.0 * mean_x * mean_y + SSIM_CONST_A
    numer_b = 2.0 * covar + SSIM_CONST_B
    denom_a = mean_x * mean_x + mean_y * mean_y + SSIM_CONST_A
    denom_b = var_x + var_y + SSIM_CONST_B
    ssim_map = numer_a * numer_b / (denom_a * denom_b)
    return (jnp.sum(huber_loss(picture - target)) + jnp.sum(1.0 - ssim_map)) / pix_dev

def reference(features, conv_first, conv_second, shortcut_weight, head_weight, target_frames):
    pix_dev = 1.0 * COLORS * F_DEV * TILE_H * TILE_W
    contract = (((0,), (0,)), ((), ()))
    act_zero = normed_silu(features.astype(jnp.float32)).astype(jnp.bfloat16)
    pre_first = causal_conv(act_zero, conv_first)
    act_first = normed_silu(pre_first).astype(jnp.bfloat16)
    pre_second = causal_conv(act_first, conv_second)
    shortcut_out = jnp.dot(features, shortcut_weight, preferred_element_type=jnp.float32)
    block_sum = pre_second + shortcut_out
    act_block = normed_silu(block_sum).astype(jnp.bfloat16)
    image_rgb = jnp.dot(act_block, head_weight, preferred_element_type=jnp.float32)
    image_first = jnp.moveaxis(image_rgb, -1, 0)

    def total_loss(picture):
        return pixel_loss(picture, target_frames, pix_dev)
    loss_sum, backprop = jax.vjp(total_loss, image_first)
    grad_image = jnp.moveaxis(backprop(jnp.ones_like(loss_sum))[0], 0, -1)
    flat_block = act_block.reshape(-1, C_MID).astype(jnp.float32)
    grad_head = lax.dot_general(flat_block, grad_image.reshape(-1, COLORS), contract, precision=lax.Precision.HIGHEST)
    grad_act_block = jnp.dot(grad_image, head_weight.astype(jnp.float32).T, precision=lax.Precision.HIGHEST)
    grad_block = jax.vjp(normed_silu, block_sum)[1](grad_act_block)[0].astype(jnp.bfloat16)
    grad_shortcut = lax.dot_general(features.reshape(-1, C_IN), grad_block.reshape(-1, C_MID), contract, preferred_element_type=jnp.float32)
    conv_back = jax.vjp(causal_conv, act_first.astype(jnp.float32), conv_second.astype(jnp.float32))[1]
    grad_act_first, grad_second = conv_back(grad_block.astype(jnp.float32))
    grad_pre_first = jax.vjp(normed_silu, pre_first)[1](grad_act_first)[0].astype(jnp.bfloat16)
    first_back = jax.vjp(lambda kernel: causal_conv(act_zero, kernel), conv_first.astype(jnp.float32))[1]
    grad_first = first_back(grad_pre_first.astype(jnp.float32))[0]
    loss_mean = loss_sum / (N_TM * N_ROW * N_COL)
    return (grad_first, grad_second, grad_shortcut, grad_head, loss_mean)
```

```python
import functools
import math
import types

import jax
import jax.numpy as jnp
from jax import lax
from jax.experimental import pallas as pl
from jax.experimental.pallas import tpu as pltpu
from jax.sharding import PartitionSpec as P

MESH = pl.DeviceIdType.MESH
F32, BF16 = jnp.float32, jnp.bfloat16
HIGH = lax.Precision.HIGHEST
EPSILON = 1e-06
HUBER_BETA = 0.05
SSIM_CONST_A = 0.0004
SSIM_CONST_B = 0.0036
N_TM, N_ROW, N_COL = 4, 4, 8
FR, TH, TW = 2, 8, 32
VOX = FR * TH * TW
C_IN, C_MID = 384, 192
PIX = 1.0 * 3 * VOX
RAW = [math.exp(-o * o / 4.5) for o in range(6)]
TAPS = [v / (RAW[0] + 2.0 * sum(RAW[1:])) for v in RAW]
NT = (((1,), (1,)), ((), ()))
NN = (((1,), (0,)), ((), ()))
TN = (((0,), (0,)), ((), ()))
HALO = [(0, -1, 0), (0, 1, 0)]
SIDES = [(-1, -1), (0, -1), (1, -1), (-1, 1), (0, 1), (1, 1)]


def band(distance, keep):
    total = jnp.zeros(distance.shape, F32)
    gap = jnp.abs(distance)
    for offset in range(6):
        total = total + jnp.where(gap == offset, TAPS[offset], 0.0)
    return jnp.where(keep, total, 0.0)


def iota(shape, dim):
    return lax.broadcasted_iota(jnp.int32, shape, dim)


def silu_forward(values):
    inverse = lax.rsqrt(jnp.mean(values * values, axis=-1, keepdims=True) + EPSILON)
    unit = values * inverse
    return unit / (1.0 + jnp.exp(-unit))


def silu_backward(values, grad):
    inverse = lax.rsqrt(jnp.mean(values * values, axis=-1, keepdims=True) + EPSILON)
    unit = values * inverse
    gate = 1.0 / (1.0 + jnp.exp(-unit))
    slope = grad * (gate * (1.0 + unit * (1.0 - gate)))
    return inverse * (slope - unit * jnp.mean(slope * unit, axis=-1, keepdims=True))


def wrap(index, step, count):
    return lax.rem(index + (step + count), count)


class Halo:
    def __init__(self, place, ahead, own, other, rims, edges, lines, send, recv):
        self.place, self.ahead = place, ahead
        self.tiles, self.rims, self.edges, self.lines = (own, other), rims, edges, lines
        self.send, self.recv = send, recv

    def copies(self, group):
        t, r, c = self.place
        own, target = self.tiles[0], self.tiles[group]
        there = wrap(t, self.ahead * group, N_TM)
        items = []

        def add(number, src, dst, dr, dc):
            items.append(
                pltpu.make_async_remote_copy(
                    src_ref=src,
                    dst_ref=dst,
                    send_sem=self.send.at[9 * group + number],
                    recv_sem=self.recv.at[9 * group + number],
                    device_id=(there, wrap(r, dr, N_ROW), wrap(c, dc, N_COL)),
                    device_id_type=MESH,
                )
            )

        add(0, own.at[:, 1], target.at[:, 9], -1, 0)
        add(1, own.at[:, 8], target.at[:, 0], 1, 0)
        for number, (dr, dc) in enumerate(SIDES):
            side = 0 if dc == 1 else 1
            add(2 + number, self.edges.at[1 - side], self.rims.at[group, side, 1 - dr], dr, dc)
        if group == 1:
            add(8, own.at[:, pl.ds(1, TH)], target.at[:, pl.ds(1, TH)], 0, 0)
        return items

    def start(self, edges_ref):
        chan = self.edges.shape[-1]
        self.edges[...] = edges_ref[:, :, 0:chan].astype(BF16)
        for group in (0, 1):
            for copy in self.copies(group):
                copy.start()

    def arrived(self, group):
        for copy in self.copies(group):
            copy.wait_recv()

    def sent(self):
        for group in (0, 1):
            for copy in self.copies(group):
                copy.wait_send()

    def shift(self, group, shifted, frame_at):
        t, r, c = self.place
        tile, lines = self.tiles[group], self.lines
        chan = tile.shape[-1]
        for side in (0, 1):
            for frame in range(FR):
                at = slice(frame * TH, frame * TH + TH)
                middle = self.rims[group, side, 1].astype(F32)
                lines[side, frame, 1 : TH + 1] = middle[at]
                lines[side, frame, 0:1] = self.rims[group, side, 0].astype(F32)[frame * TH + TH - 1 : frame * TH + TH]
                lines[side, frame, TH + 1 : TH + 2] = self.rims[group, side, 2].astype(F32)[frame * TH : frame * TH + 1]
        edge_t = jnp.where(self.ahead == 1, t == 0, t == N_TM - 1)
        live = 1.0 if group == 0 else jnp.where(edge_t, 0.0, 1.0)
        top = jnp.where(r == 0, 0.0, 1.0)
        bottom = jnp.where(r == N_ROW - 1, 0.0, 1.0)
        left = jnp.where(c == 0, 0.0, 1.0)
        right = jnp.where(c == N_COL - 1, 0.0, 1.0)
        column = iota((TW, chan), 0)

        def one(step, carry):
            frame, row = step // (TH + 2), lax.rem(step, TH + 2)
            scale = live * jnp.where(row == 0, top, jnp.where(row == TH + 1, bottom, 1.0))
            base = tile[frame, row].astype(F32) * scale
            first = lines[0, frame, pl.ds(row, 1), :] * (scale * left)
            last = lines[1, frame, pl.ds(row, 1), :] * (scale * right)
            shifted[0, frame_at + frame, row] = jnp.where(column == 0, first, pltpu.roll(base, 1, 0)).astype(BF16)
            shifted[1, frame_at + frame, row] = base.astype(BF16)
            shifted[2, frame_at + frame, row] = jnp.where(column == TW - 1, last, pltpu.roll(base, TW - 1, 0)).astype(BF16)
            return carry

        lax.fori_loop(0, FR * (TH + 2), one, 0)


def convolve(shifted, weights, total, full_at, full_tap, half_at, half_out, dims, flip, first):
    half = VOX // FR

    def one(row, carry):
        def tap(time, col):
            if flip:
                return weights[(time * 3 + 2 - row) * 3 + 2 - col]
            return weights[(time * 3 + row) * 3 + col]

        chan = shifted.shape[-1]
        full = None
        part = None
        for col in range(3):
            data = shifted[col, pl.ds(full_at, FR), pl.ds(row, TH)].reshape(VOX, chan)
            term = lax.dot_general(data, tap(full_tap, col), dims, preferred_element_type=F32)
            full = term if full is None else full + term
        total[...] += full
        for col in range(3):
            data = shifted[col, half_at, pl.ds(row, TH)].reshape(half, chan)
            term = lax.dot_general(data, tap(1, col), dims, preferred_element_type=F32)
            part = term if part is None else part + term
        total[pl.ds(half_out * half, half), :] += part
        return carry

    if first:
        total[...] = jnp.zeros(total.shape, F32)
    lax.fori_loop(0, 3, one, 0)


CHUNK = 128


def chunks(body):
    def one(step, carry):
        body(pl.ds(pl.multiple_of(step * CHUNK, CHUNK), CHUNK), step)
        return carry

    lax.fori_loop(0, VOX // CHUNK, one, 0)


def put_tile(tile, edges, step, values):
    rows = CHUNK // TW
    chan = values.shape[-1]
    for at in range(rows):
        edges[0, pl.ds(step * rows + at, 1), 0:chan] = values[at * TW : at * TW + 1]
        edges[1, pl.ds(step * rows + at, 1), 0:chan] = values[at * TW + TW - 1 : at * TW + TW]
    values = values.astype(BF16)
    frame, row = step // (TH // rows), lax.rem(step, TH // rows) * rows
    tile[frame, pl.ds(row + 1, rows)] = values.reshape(rows, TW, values.shape[-1])


def picture_copies(place, tile, field, send, recv):
    t, r, c = place
    items = []
    number = 0
    for dr in range(N_ROW):
        for dc in (-1, 0, 1):
            if dr == 0 and dc == 0:
                continue
            items.append(
                pltpu.make_async_remote_copy(
                    src_ref=tile,
                    dst_ref=field.at[1 - dc, :, pl.ds(pl.multiple_of(r * TH, TH), TH), :],
                    send_sem=send.at[number],
                    recv_sem=recv.at[number],
                    device_id=(t, wrap(r, dr, N_ROW), wrap(c, dc, N_COL)),
                    device_id_type=MESH,
                )
            )
            number += 1
    return items


def canvas(place, tile, field):
    t, r, c = place
    field[1, :, pl.ds(pl.multiple_of(r * TH, TH), TH), :] = tile[...]
    flat = [field[side].reshape(6 * N_ROW * TH, 128) for side in range(3)]
    left = flat[0] * jnp.where(c == 0, 0.0, 1.0)
    right = flat[2] * jnp.where(c == N_COL - 1, 0.0, 1.0)
    return left + pltpu.roll(flat[1], TW, 1) + pltpu.roll(right, 2 * TW, 1)


def high_dot(a, b):
    return jnp.dot(a, b, precision=HIGH, preferred_element_type=F32)


def picture_loss(place, x_tile, y_tile, x_field, y_field, spread):
    t, r, c = place
    rows = 6 * N_ROW * TH
    x, y = canvas(place, x_tile, x_field), canvas(place, y_tile, y_field)
    across = band(iota((128, 128), 0) - iota((128, 128), 1), True)
    row_a, row_b = iota((rows, rows), 0), iota((rows, rows), 1)
    down = band(row_a - row_b, (row_a >> 5) == (row_b >> 5))
    own_a, own_b = iota((48, rows), 0), iota((48, rows), 1)
    down_own = band((own_a & 7) + r * TH - (own_b & 31), (own_a >> 3) == (own_b >> 5))
    wide = high_dot(jnp.concatenate([x, y, x * x, y * y, x * y], axis=0), across)
    mean_x, mean_y, square_x, square_y, cross = [
        high_dot(down, wide[m * rows : (m + 1) * rows]) for m in range(5)
    ]
    var_x = square_x - mean_x * mean_x
    var_y = square_y - mean_y * mean_y
    covar = cross - mean_x * mean_y
    numer_a = 2.0 * mean_x * mean_y + SSIM_CONST_A
    numer_b = 2.0 * covar + SSIM_CONST_B
    denom_a = mean_x * mean_x + mean_y * mean_y + SSIM_CONST_A
    denom_b = var_x + var_y + SSIM_CONST_B
    denom_all = denom_a * denom_b
    ssim = numer_a * numer_b / denom_all
    slope_mean = (2.0 * mean_y * numer_b - 2.0 * mean_y * numer_a) / denom_all - ssim * (
        2.0 * mean_x / denom_a - 2.0 * mean_x / denom_b
    )
    slope_square = -ssim / denom_b
    slope_cross = 2.0 * numer_a / denom_all
    lane, line = iota((rows, 128), 1), iota((rows, 128), 0) & 31
    low = jnp.where(c == 0, TW, TW - 5)
    high = jnp.where(c == N_COL - 1, 2 * TW, 2 * TW + 5)
    inside = (lane >= low) & (lane < high)
    mine = (lane >= TW) & (lane < 2 * TW) & (line >= r * TH) & (line < r * TH + TH)
    loss = jnp.sum(jnp.where(mine, 1.0 - ssim, 0.0), axis=0, keepdims=True)
    adjoint = jnp.concatenate(
        [jnp.where(inside, slope * (-1.0 / PIX), 0.0) for slope in (slope_mean, slope_square, slope_cross)], axis=0
    )
    wide = high_dot(adjoint, across)
    pulled = [high_dot(down_own, wide[m * rows : (m + 1) * rows]) for m in range(3)]
    x_own = pltpu.roll(x_tile[...].reshape(48, 128), TW, 1)
    y_own = pltpu.roll(y_tile[...].reshape(48, 128), TW, 1)
    lane = iota((48, 128), 1)
    mine = (lane >= TW) & (lane < 2 * TW)
    diff = x_own - y_own
    size = jnp.abs(diff)
    huber = jnp.where(size < HUBER_BETA, 0.5 * diff * diff / HUBER_BETA, size - 0.5 * HUBER_BETA)
    loss = (loss + jnp.sum(jnp.where(mine, huber, 0.0), axis=0, keepdims=True)) / PIX
    grad = jnp.clip(diff / HUBER_BETA, -1.0, 1.0) / PIX + pulled[0] + 2.0 * x_own * pulled[1] + y_own * pulled[2]
    grad = pltpu.roll(jnp.where(mine, grad, 0.0), 128 - TW, 1)
    spread[...] = jnp.zeros(spread.shape, F32)
    for color in range(3):
        for frame in range(FR):
            at = (color * FR + frame) * TH
            spread[pl.ds(frame * 64 + color, TH, stride=8), :] = grad[at : at + TH]
    return loss


def kernel(feat, w1, w2, ws, head, targ, g1, g2, gh, loss_out, *scratch):
    s = types.SimpleNamespace(**dict(zip(SCRATCH_NAMES, scratch)))
    t, r, c = lax.axis_index("tm"), lax.axis_index("row"), lax.axis_index("col")
    place = (t, r, c)

    barrier = pltpu.get_barrier_semaphore()
    around = [
        (dt, dr, dc)
        for dt in (-1, 0, 1)
        for dr in (-1, 0, 1, 2)
        for dc in (-1, 0, 1)
        if (dt, dr, dc) != (0, 0, 0) and (dt == 0 or dr < 2)
    ]
    for dt, dr, dc in around:
        pl.semaphore_signal(
            barrier,
            inc=1,
            device_id=(wrap(t, dt, N_TM), wrap(r, dr, N_ROW), wrap(c, dc, N_COL)),
            device_id_type=MESH,
        )

    def act(rows, step):
        values = silu_forward(feat[rows, :].astype(F32))
        put_tile(s.own0, s.columns, step, values)

    chunks(act)
    s.target[...] = jnp.zeros(s.target.shape, F32)
    s.target[:, :, 0:TW] = targ[...]
    pl.semaphore_wait(barrier, len(around))

    halo0 = Halo(place, 1, s.own0, s.other0, s.rims0, s.edges0, s.lines0, s.send0, s.recv0)
    halo1 = Halo(place, 1, s.own1, s.other1, s.rims1, s.edges1, s.lines1, s.send1, s.recv1)
    halo2 = Halo(place, -1, s.own2, s.other2, s.rims2, s.edges2, s.lines1, s.send2, s.recv2)
    halo0.start(s.columns)
    y_copies = picture_copies(place, s.target, s.y_field, s.send_y, s.recv_y)
    for copy in y_copies:
        copy.start()

    halo0.arrived(0)
    halo0.shift(0, s.shift0, FR)
    convolve(s.shift0, w1, s.pre, FR, 2, FR, 1, NT, False, True)
    halo0.arrived(1)
    halo0.shift(1, s.shift0, 0)
    convolve(s.shift0, w1, s.pre, 0, 0, 1, 0, NT, False, False)

    def act_first(rows, step):
        values = silu_forward(s.pre[rows, :])
        put_tile(s.own1, s.columns, step, values)

    chunks(act_first)
    halo1.start(s.columns)
    halo1.arrived(0)
    halo1.shift(0, s.shift1, FR)
    convolve(s.shift1, w2, s.block, FR, 2, FR, 1, NN, False, True)

    def shortcut(rows, step):
        s.block[rows, :] += lax.dot_general(feat[rows, :], ws[...], NT, preferred_element_type=F32)

    chunks(shortcut)
    halo1.arrived(1)
    halo1.shift(1, s.shift1, 0)
    convolve(s.shift1, w2, s.block, 0, 0, 1, 0, NN, False, False)

    s.headf[...] = jnp.zeros(s.headf.shape, F32)
    s.headf[0:3, :] = head[...].astype(F32)

    def act_block(rows, step):
        s.values1[rows, :] = silu_forward(s.block[rows, :]).astype(BF16).astype(F32)

    chunks(act_block)
    lane = iota((8, 128), 1)
    for part in range(4):
        rows = slice(part * 128, part * 128 + 128)
        color = lax.dot_general(
            s.headf[...].astype(BF16), s.values1[rows, :].astype(BF16), NT, preferred_element_type=F32
        )
        for piece in range(4):
            moved = color if piece == 0 else pltpu.roll(color, 128 - TW * piece, 1)
            at = (4 * part + piece) * 8
            s.spread[at : at + 8, :] = jnp.where(lane < TW, moved, 0.0)
    for color in range(3):
        for frame in range(FR):
            s.image[color * FR + frame] = s.spread[pl.ds(frame * 64 + color, TH, stride=8), :]

    x_copies = picture_copies(place, s.image, s.x_field, s.send_x, s.recv_x)
    for copy in x_copies:
        copy.start()
    for copy in y_copies:
        copy.wait_recv()
    for copy in x_copies:
        copy.wait_recv()
    loss = picture_loss(place, s.image, s.target, s.x_field, s.y_field, s.spread)
    loss_out[...] = jnp.broadcast_to(loss, loss_out.shape)

    grad_head = None
    for part in range(4):
        rows = slice(part * 128, part * 128 + 128)
        color = None
        for piece in range(4):
            at = (4 * part + piece) * 8
            held = s.spread[at : at + 8, :]
            color = held if piece == 0 else color + pltpu.roll(held, TW * piece, 1)
        s.colors[part] = color
        term = high_dot(color, s.values1[rows, :])
        grad_head = term if grad_head is None else grad_head + term
    gh[...] = grad_head

    def back_block(rows, step):
        grad = lax.dot_general(s.colors[step], s.headf[...], TN, precision=HIGH, preferred_element_type=F32)
        values = silu_backward(s.block[rows, :], grad)
        s.values1[rows, :] = values
        put_tile(s.own2, s.columns, step, values)

    chunks(back_block)
    halo2.start(s.columns)
    block_t = s.values1[...].T.astype(BF16)
    s.block_t[...] = block_t
    halo2.arrived(0)
    halo2.shift(0, s.shift2, 0)
    convolve(s.shift2, w2, s.back, 0, 2, 1, 0, NT, True, True)

    def second(step, carry):
        time, row = step // 3, lax.rem(step, 3)
        for col in range(3):
            data = s.shift1[col, pl.ds(time, FR), pl.ds(row, TH)].reshape(VOX, C_MID)
            result = lax.dot_general(s.block_t[...], data, NN, preferred_element_type=F32)
            g2[step * 3 + col] = result.T
        return carry

    lax.fori_loop(0, 9, second, 0)
    g1[27] = lax.dot_general(s.block_t[...], feat[...], NN, preferred_element_type=F32)
    halo2.arrived(1)
    halo2.shift(1, s.shift2, FR)
    convolve(s.shift2, w2, s.back, FR, 0, FR, 1, NT, True, False)

    def back_first(rows, step):
        s.values1[rows, :] = silu_backward(s.pre[rows, :], s.back[rows, :])

    chunks(back_first)
    s.block_t[...] = s.values1[...].T.astype(BF16)

    def first(step, carry):
        time, row = step // 3, lax.rem(step, 3)
        for col in range(3):
            data = s.shift0[col, pl.ds(time, FR), pl.ds(row, TH)].reshape(VOX, C_IN)
            g1[step * 3 + col] = lax.dot_general(s.block_t[...], data, NN, preferred_element_type=F32)
        return carry

    lax.fori_loop(0, 9, first, 0)
    for halo in (halo0, halo1, halo2):
        halo.sent()
    for copy in x_copies + y_copies:
        copy.wait_send()


def halo_scratch(number, chan):
    return [
        (f"own{number}", pltpu.VMEM((FR, TH + 2, TW, chan), BF16)),
        (f"other{number}", pltpu.VMEM((FR, TH + 2, TW, chan), BF16)),
        (f"rims{number}", pltpu.VMEM((2, 2, 3, FR * TH, chan), BF16)),
        (f"edges{number}", pltpu.VMEM((2, FR * TH, chan), BF16)),
        (f"shift{number}", pltpu.VMEM((3, 2 * FR, TH + 2, TW, chan), BF16)),
        (f"send{number}", pltpu.SemaphoreType.DMA((18,))),
        (f"recv{number}", pltpu.SemaphoreType.DMA((18,))),
    ]


SCRATCH = (
    halo_scratch(0, C_IN)
    + halo_scratch(1, C_MID)
    + halo_scratch(2, C_MID)
    + [
        ("lines0", pltpu.VMEM((2, FR, 16, C_IN), F32)),
        ("lines1", pltpu.VMEM((2, FR, 16, C_MID), F32)),
        ("columns", pltpu.VMEM((2, FR * TH, C_IN), F32)),
        ("values1", pltpu.VMEM((VOX, C_MID), F32)),
        ("pre", pltpu.VMEM((VOX, C_MID), F32)),
        ("block", pltpu.VMEM((VOX, C_MID), F32)),
        ("back", pltpu.VMEM((VOX, C_MID), F32)),
        ("block_t", pltpu.VMEM((C_MID, VOX), BF16)),
        ("headf", pltpu.VMEM((8, C_MID), F32)),
        ("spread", pltpu.VMEM((128, 128), F32)),
        ("colors", pltpu.VMEM((4, 8, 128), F32)),
        ("image", pltpu.VMEM((6, TH, 128), F32)),
        ("target", pltpu.VMEM((6, TH, 128), F32)),
        ("x_field", pltpu.VMEM((3, 6, N_ROW * TH, 128), F32)),
        ("y_field", pltpu.VMEM((3, 6, N_ROW * TH, 128), F32)),
        ("send_x", pltpu.SemaphoreType.DMA((11,))),
        ("recv_x", pltpu.SemaphoreType.DMA((11,))),
        ("send_y", pltpu.SemaphoreType.DMA((11,))),
        ("recv_y", pltpu.SemaphoreType.DMA((11,))),
    ]
)
SCRATCH_NAMES = [name for name, _ in SCRATCH]


def body(features, conv_first, conv_second, shortcut_weight, head_weight, target_frames):
    vmem = pl.BlockSpec(memory_space=pltpu.VMEM)
    g1, g2, gh, loss = pl.pallas_call(
        kernel,
        out_shape=[
            jax.ShapeDtypeStruct((28, C_MID, C_IN), F32),
            jax.ShapeDtypeStruct((27, C_MID, C_MID), F32),
            jax.ShapeDtypeStruct((8, C_MID), F32),
            jax.ShapeDtypeStruct((8, 128), F32),
        ],
        in_specs=[vmem] * 6,
        out_specs=[vmem] * 4,
        scratch_shapes=[shape for _, shape in SCRATCH],
        compiler_params=pltpu.CompilerParams(
            collective_id=0, has_side_effects=True, vmem_limit_bytes=60 * 1024 * 1024
        ),
    )(
        features.reshape(VOX, C_IN),
        conv_first.transpose(0, 1, 2, 4, 3).reshape(27, C_MID, C_IN),
        conv_second.reshape(27, C_MID, C_MID),
        shortcut_weight.T,
        head_weight.T,
        target_frames.reshape(6, TH, TW),
    )
    g1, g2, gh, loss = lax.psum((g1, g2, gh[:3], jnp.sum(loss[0])), ("tm", "row", "col"))
    return (
        g1[:27].reshape(3, 3, 3, C_MID, C_IN).transpose(0, 1, 2, 4, 3),
        g2.reshape(3, 3, 3, C_MID, C_MID),
        g1[27].T,
        gh.T,
        loss / (N_TM * N_ROW * N_COL),
    )


def solution(mesh):
    return jax.shard_map(
        body,
        mesh=mesh,
        in_specs=(P("tm", "row", "col", None), P(), P(), P(), P(), P(None, "tm", "row", "col")),
        out_specs=(P(), P(), P(), P(), P()),
        check_vma=False,
    )
```

```python
import functools
import math
import types

import jax
import jax.numpy as jnp
from jax import lax
from jax.experimental import pallas as pl
from jax.experimental.pallas import tpu as pltpu
from jax.sharding import PartitionSpec as P

MESH = pl.DeviceIdType.MESH
F32, BF16 = jnp.float32, jnp.bfloat16
HIGH = lax.Precision.HIGHEST
EPSILON = 1e-06
HUBER_BETA = 0.05
SSIM_CONST_A = 0.0004
SSIM_CONST_B = 0.0036
N_TM, N_ROW, N_COL = 4, 4, 8
FR, TH, TW = 2, 8, 32
VOX = FR * TH * TW
C_IN, C_MID = 384, 192
PIX = 1.0 * 3 * VOX
RAW = [math.exp(-o * o / 4.5) for o in range(6)]
TAPS = [v / (RAW[0] + 2.0 * sum(RAW[1:])) for v in RAW]
NT = (((1,), (1,)), ((), ()))
NN = (((1,), (0,)), ((), ()))
TN = (((0,), (0,)), ((), ()))
PARTS, SPAN = 3, 4096
SIZES = (1024, 256, 64)
AXES = ("yzx", "zxy", "xyz")
SLOTS = 14
LINES = PARTS * SPAN
SECOND_AT = SLOTS * 3 * C_MID
SIDES = [(-1, -1), (0, -1), (1, -1), (-1, 1), (0, 1), (1, 1)]


def band(distance, keep):
    total = jnp.zeros(distance.shape, F32)
    gap = jnp.abs(distance)
    for offset in range(6):
        total = total + jnp.where(gap == offset, TAPS[offset], 0.0)
    return jnp.where(keep, total, 0.0)


def iota(shape, dim):
    return lax.broadcasted_iota(jnp.int32, shape, dim)


def silu_forward(values):
    inverse = lax.rsqrt(jnp.mean(values * values, axis=-1, keepdims=True) + EPSILON)
    unit = values * inverse
    return unit / (1.0 + jnp.exp(-unit))


def silu_backward(values, grad):
    inverse = lax.rsqrt(jnp.mean(values * values, axis=-1, keepdims=True) + EPSILON)
    unit = values * inverse
    gate = 1.0 / (1.0 + jnp.exp(-unit))
    slope = grad * (gate * (1.0 + unit * (1.0 - gate)))
    return inverse * (slope - unit * jnp.mean(slope * unit, axis=-1, keepdims=True))


def wrap(index, step, count):
    return lax.rem(index + (step + count), count)


class Halo:
    def __init__(self, place, ahead, own, other, rims, edges, lines, send, recv):
        self.place, self.ahead = place, ahead
        self.tiles, self.rims, self.edges, self.lines = (own, other), rims, edges, lines
        self.send, self.recv = send, recv

    def copies(self, group):
        t, r, c = self.place
        own, target = self.tiles[0], self.tiles[group]
        there = wrap(t, self.ahead * group, N_TM)
        items = []

        def add(number, src, dst, dr, dc):
            items.append(
                pltpu.make_async_remote_copy(
                    src_ref=src,
                    dst_ref=dst,
                    send_sem=self.send.at[9 * group + number],
                    recv_sem=self.recv.at[9 * group + number],
                    device_id=(there, wrap(r, dr, N_ROW), wrap(c, dc, N_COL)),
                    device_id_type=MESH,
                )
            )

        add(0, own.at[:, 1], target.at[:, 9], -1, 0)
        add(1, own.at[:, 8], target.at[:, 0], 1, 0)
        for number, (dr, dc) in enumerate(SIDES):
            side = 0 if dc == 1 else 1
            add(2 + number, self.edges.at[1 - side], self.rims.at[group, side, 1 - dr], dr, dc)
        if group == 1:
            add(8, own.at[:, pl.ds(1, TH)], target.at[:, pl.ds(1, TH)], 0, 0)
        return items

    def start(self, edges_ref):
        chan = self.edges.shape[-1]
        self.edges[...] = edges_ref[:, :, 0:chan].astype(BF16)
        for group in (0, 1):
            for copy in self.copies(group):
                copy.start()

    def arrived(self, group):
        for copy in self.copies(group):
            copy.wait_recv()

    def sent(self):
        for group in (0, 1):
            for copy in self.copies(group):
                copy.wait_send()

    def shift(self, group, shifted, frame_at):
        t, r, c = self.place
        tile, lines = self.tiles[group], self.lines
        chan = tile.shape[-1]
        for side in (0, 1):
            for frame in range(FR):
                at = slice(frame * TH, frame * TH + TH)
                middle = self.rims[group, side, 1].astype(F32)
                lines[side, frame, 1 : TH + 1] = middle[at]
                lines[side, frame, 0:1] = self.rims[group, side, 0].astype(F32)[frame * TH + TH - 1 : frame * TH + TH]
                lines[side, frame, TH + 1 : TH + 2] = self.rims[group, side, 2].astype(F32)[frame * TH : frame * TH + 1]
        edge_t = jnp.where(self.ahead == 1, t == 0, t == N_TM - 1)
        live = 1.0 if group == 0 else jnp.where(edge_t, 0.0, 1.0)
        top = jnp.where(r == 0, 0.0, 1.0)
        bottom = jnp.where(r == N_ROW - 1, 0.0, 1.0)
        left = jnp.where(c == 0, 0.0, 1.0)
        right = jnp.where(c == N_COL - 1, 0.0, 1.0)
        column = iota((TW, chan), 0)

        def one(step, carry):
            frame, row = step // (TH + 2), lax.rem(step, TH + 2)
            scale = live * jnp.where(row == 0, top, jnp.where(row == TH + 1, bottom, 1.0))
            base = tile[frame, row].astype(F32) * scale
            first = lines[0, frame, pl.ds(row, 1), :] * (scale * left)
            last = lines[1, frame, pl.ds(row, 1), :] * (scale * right)
            shifted[0, frame_at + frame, row] = jnp.where(column == 0, first, pltpu.roll(base, 1, 0)).astype(BF16)
            shifted[1, frame_at + frame, row] = base.astype(BF16)
            shifted[2, frame_at + frame, row] = jnp.where(column == TW - 1, last, pltpu.roll(base, TW - 1, 0)).astype(BF16)
            return carry

        lax.fori_loop(0, FR * (TH + 2), one, 0)


def convolve(shifted, weights, total, full_at, full_tap, half_at, half_out, dims, flip, first):
    half = VOX // FR

    def one(row, carry):
        def tap(time, col):
            if flip:
                return weights[(time * 3 + 2 - row) * 3 + 2 - col]
            return weights[(time * 3 + row) * 3 + col]

        chan = shifted.shape[-1]
        full = None
        part = None
        for col in range(3):
            data = shifted[col, pl.ds(full_at, FR), pl.ds(row, TH)].reshape(VOX, chan)
            term = lax.dot_general(data, tap(full_tap, col), dims, preferred_element_type=F32)
            full = term if full is None else full + term
        total[...] += full
        for col in range(3):
            data = shifted[col, half_at, pl.ds(row, TH)].reshape(half, chan)
            term = lax.dot_general(data, tap(1, col), dims, preferred_element_type=F32)
            part = term if part is None else part + term
        total[pl.ds(half_out * half, half), :] += part
        return carry

    if first:
        total[...] = jnp.zeros(total.shape, F32)
    lax.fori_loop(0, 3, one, 0)


CHUNK = 128


def chunks(body):
    def one(step, carry):
        body(pl.ds(pl.multiple_of(step * CHUNK, CHUNK), CHUNK), step)
        return carry

    lax.fori_loop(0, VOX // CHUNK, one, 0)


def put_tile(tile, edges, step, values):
    rows = CHUNK // TW
    chan = values.shape[-1]
    for at in range(rows):
        edges[0, pl.ds(step * rows + at, 1), 0:chan] = values[at * TW : at * TW + 1]
        edges[1, pl.ds(step * rows + at, 1), 0:chan] = values[at * TW + TW - 1 : at * TW + TW]
    values = values.astype(BF16)
    frame, row = step // (TH // rows), lax.rem(step, TH // rows) * rows
    tile[frame, pl.ds(row + 1, rows)] = values.reshape(rows, TW, values.shape[-1])


def picture_copies(place, tile, field, send, recv):
    t, r, c = place
    items = []
    number = 0
    for dr in range(N_ROW):
        for dc in (-1, 0, 1):
            if dr == 0 and dc == 0:
                continue
            items.append(
                pltpu.make_async_remote_copy(
                    src_ref=tile,
                    dst_ref=field.at[1 - dc, :, pl.ds(pl.multiple_of(r * TH, TH), TH), :],
                    send_sem=send.at[number],
                    recv_sem=recv.at[number],
                    device_id=(t, wrap(r, dr, N_ROW), wrap(c, dc, N_COL)),
                    device_id_type=MESH,
                )
            )
            number += 1
    return items


def canvas(place, tile, field):
    t, r, c = place
    field[1, :, pl.ds(pl.multiple_of(r * TH, TH), TH), :] = tile[...]
    flat = [field[side].reshape(6 * N_ROW * TH, 128) for side in range(3)]
    left = flat[0] * jnp.where(c == 0, 0.0, 1.0)
    right = flat[2] * jnp.where(c == N_COL - 1, 0.0, 1.0)
    return left + pltpu.roll(flat[1], TW, 1) + pltpu.roll(right, 2 * TW, 1)


def high_dot(a, b):
    return jnp.dot(a, b, precision=HIGH, preferred_element_type=F32)


def picture_loss(place, x_tile, y_tile, x_field, y_field, spread):
    t, r, c = place
    rows = 6 * N_ROW * TH
    x, y = canvas(place, x_tile, x_field), canvas(place, y_tile, y_field)
    across = band(iota((128, 128), 0) - iota((128, 128), 1), True)
    row_a, row_b = iota((rows, rows), 0), iota((rows, rows), 1)
    down = band(row_a - row_b, (row_a >> 5) == (row_b >> 5))
    own_a, own_b = iota((48, rows), 0), iota((48, rows), 1)
    down_own = band((own_a & 7) + r * TH - (own_b & 31), (own_a >> 3) == (own_b >> 5))
    wide = high_dot(jnp.concatenate([x, y, x * x, y * y, x * y], axis=0), across)
    mean_x, mean_y, square_x, square_y, cross = [
        high_dot(down, wide[m * rows : (m + 1) * rows]) for m in range(5)
    ]
    var_x = square_x - mean_x * mean_x
    var_y = square_y - mean_y * mean_y
    covar = cross - mean_x * mean_y
    numer_a = 2.0 * mean_x * mean_y + SSIM_CONST_A
    numer_b = 2.0 * covar + SSIM_CONST_B
    denom_a = mean_x * mean_x + mean_y * mean_y + SSIM_CONST_A
    denom_b = var_x + var_y + SSIM_CONST_B
    denom_all = denom_a * denom_b
    ssim = numer_a * numer_b / denom_all
    slope_mean = (2.0 * mean_y * numer_b - 2.0 * mean_y * numer_a) / denom_all - ssim * (
        2.0 * mean_x / denom_a - 2.0 * mean_x / denom_b
    )
    slope_square = -ssim / denom_b
    slope_cross = 2.0 * numer_a / denom_all
    lane, line = iota((rows, 128), 1), iota((rows, 128), 0) & 31
    low = jnp.where(c == 0, TW, TW - 5)
    high = jnp.where(c == N_COL - 1, 2 * TW, 2 * TW + 5)
    inside = (lane >= low) & (lane < high)
    mine = (lane >= TW) & (lane < 2 * TW) & (line >= r * TH) & (line < r * TH + TH)
    loss = jnp.sum(jnp.where(mine, 1.0 - ssim, 0.0), axis=0, keepdims=True)
    adjoint = jnp.concatenate(
        [jnp.where(inside, slope * (-1.0 / PIX), 0.0) for slope in (slope_mean, slope_square, slope_cross)], axis=0
    )
    wide = high_dot(adjoint, across)
    pulled = [high_dot(down_own, wide[m * rows : (m + 1) * rows]) for m in range(3)]
    x_own = pltpu.roll(x_tile[...].reshape(48, 128), TW, 1)
    y_own = pltpu.roll(y_tile[...].reshape(48, 128), TW, 1)
    lane = iota((48, 128), 1)
    mine = (lane >= TW) & (lane < 2 * TW)
    diff = x_own - y_own
    size = jnp.abs(diff)
    huber = jnp.where(size < HUBER_BETA, 0.5 * diff * diff / HUBER_BETA, size - 0.5 * HUBER_BETA)
    loss = (loss + jnp.sum(jnp.where(mine, huber, 0.0), axis=0, keepdims=True)) / PIX
    grad = jnp.clip(diff / HUBER_BETA, -1.0, 1.0) / PIX + pulled[0] + 2.0 * x_own * pulled[1] + y_own * pulled[2]
    grad = pltpu.roll(jnp.where(mine, grad, 0.0), 128 - TW, 1)
    spread[...] = jnp.zeros(spread.shape, F32)
    for color in range(3):
        for frame in range(FR):
            at = (color * FR + frame) * TH
            spread[pl.ds(frame * 64 + color, TH, stride=8), :] = grad[at : at + TH]
    return loss


def axis_line(place, axis):
    t, r, c = place
    if axis == "z":
        return t, lambda step: (wrap(t, step, N_TM), r, c)
    if axis == "y":
        return r, lambda step: (t, wrap(r, step, N_ROW), c)
    return c >> 1, lambda step: (t, r, wrap(c, 2 * step, N_COL))


class Reduce:
    def __init__(self, s, place, part, result):
        self.s, self.part, self.result = s, part, result
        self.core = place[2] & 1
        self.mate = (place[0], place[1], place[2] + 1 - 2 * self.core)
        lines = [axis_line(place, axis) for axis in AXES[part]]
        self.at = [line[0] for line in lines]
        self.there = [line[1] for line in lines]

    def held(self, phase, chunk, half):
        size = SIZES[phase]
        index = lax.rem(self.at[phase] + (chunk + 4), 4)
        base = self.part * SPAN if phase == 0 else 0
        at = pl.multiple_of(base + index * size + half * (size // 2), 32)
        ref = (self.s.flat, self.s.sum1.at[self.part], self.s.sum2.at[self.part])[phase]
        return ref.at[pl.ds(at, size // 2), :]

    def inbox(self, phase):
        return (self.s.inbox0, self.s.inbox1, self.s.inbox2)[phase].at[self.part]

    def stage(self, phase):
        return (self.s.stage0, self.s.stage1, self.s.stage2)[phase].at[self.part]

    def scatter_copy(self, phase, number):
        if phase == 0 or number >= 4:
            src = self.stage(phase).at[number if phase == 0 else number - 4]
        else:
            src = self.held(phase, *((2, 0), (2, 1), (1, 1), (-1, 0))[number])
        sem = (self.part * 3 + phase) * 6 + number
        return pltpu.make_async_remote_copy(
            src_ref=src,
            dst_ref=self.inbox(phase).at[number],
            send_sem=self.s.scatter_send.at[sem],
            recv_sem=self.s.scatter_recv.at[sem],
            device_id=self.there[phase](1 if number % 2 == 0 else -1),
            device_id_type=MESH,
        )

    def scatter_start(self, phase):
        for number, (chunk, half) in enumerate(((2, 0), (2, 1), (1, 1), (-1, 0))):
            if phase == 0:
                self.stage(0)[number] = self.held(0, chunk, half)[...].astype(BF16)
            self.scatter_copy(phase, number).start()

    def scatter_middle(self, phase):
        for number, (chunk, half) in ((4, (1, 0)), (5, (-1, 1))):
            self.scatter_copy(phase, number - 4).wait_recv()
            stage = self.stage(phase).at[number if phase == 0 else number - 4]
            total = self.held(phase, chunk, half)[...] + self.inbox(phase)[number - 4].astype(F32)
            stage[...] = total.astype(stage.dtype)
            self.scatter_copy(phase, number).start()

    def scatter_finish(self, phase):
        for number in (2, 3, 4, 5):
            self.scatter_copy(phase, number).wait_recv()
        half_size = SIZES[phase] // 2
        for half, (first, second) in ((0, (4, 3)), (1, (2, 5))):
            total = self.held(phase, 0, half)[...] + (
                self.inbox(phase)[first].astype(F32) + self.inbox(phase)[second].astype(F32)
            )
            if phase == 0:
                self.s.sum1[self.part, half * half_size : (half + 1) * half_size, :] = total
            elif phase == 1:
                self.s.sum2[self.part, half * half_size : (half + 1) * half_size, :] = total
            else:
                self.region(2, 0, half, self.core)[...] = total.astype(BF16)

    def region(self, phase, chunk, half, core):
        size = SIZES[phase]
        base = self.part * SPAN
        for outer in range(phase):
            base = base + self.at[outer] * SIZES[outer]
        base = base + lax.rem(self.at[phase] + (chunk + 4), 4) * size
        if half is None:
            return self.result.at[core, pl.ds(pl.multiple_of(base, 32), size), :]
        return self.result.at[core, pl.ds(pl.multiple_of(base + half * (size // 2), 32), size // 2), :]

    def gather_copy(self, phase, number, arriving):
        chunk, half = ((0, 0), (0, 1), (0, 1), (0, 0), (-1, 0), (1, 1))[number]
        way = 1 if number % 2 == 0 else -1
        block = self.region(phase, chunk - way if arriving else chunk, half, self.core)
        sem = (self.part * 3 + phase) * 6 + number
        return pltpu.make_async_remote_copy(
            src_ref=block,
            dst_ref=block,
            send_sem=self.s.gather_send.at[sem],
            recv_sem=self.s.gather_recv.at[sem],
            device_id=self.there[phase](way),
            device_id_type=MESH,
        )

    def gather_start(self, phase):
        for number in range(4):
            self.gather_copy(phase, number, False).start()
        if phase == 0:
            self.share(0).start()

    def gather_middle(self, phase):
        for number in (4, 5):
            self.gather_copy(phase, number - 4, True).wait_recv()
            self.gather_copy(phase, number, False).start()

    def gather_finish(self, phase):
        for number in (2, 3):
            self.gather_copy(phase, number, True).wait_recv()
        if phase == 0:
            self.share(1).start()
            self.share(-1).start()
        for number in (4, 5):
            self.gather_copy(phase, number, True).wait_recv()
        if phase == 0:
            self.share(2).start()

    def share(self, chunk, arriving=False):
        block = self.region(0, chunk, None, 1 - self.core if arriving else self.core)
        sem = self.part * 4 + chunk % 4
        return pltpu.make_async_remote_copy(
            src_ref=block,
            dst_ref=block,
            send_sem=self.s.share_send.at[sem],
            recv_sem=self.s.share_recv.at[sem],
            device_id=self.mate,
            device_id_type=MESH,
        )

    def settle(self):
        for chunk in range(4):
            self.share(chunk, True).wait_recv()
        for phase in range(3):
            for number in range(6):
                self.scatter_copy(phase, number).wait_send()
                self.gather_copy(phase, number, False).wait_send()
        for chunk in range(4):
            self.share(chunk).wait_send()


class Small:
    def __init__(self, s, place):
        self.s = s
        core = place[2] & 1
        self.lines = [axis_line(place, axis) for axis in "zyx"]
        self.lines.append((core, lambda step: (place[0], place[1], place[2] + 1 - 2 * core)))

    def copies(self, stage):
        at, there = self.lines[stage]
        mine = self.s.small.at[stage, at]
        return [
            pltpu.make_async_remote_copy(
                src_ref=mine,
                dst_ref=mine,
                send_sem=self.s.small_send.at[stage * 3 + step - 1],
                recv_sem=self.s.small_recv.at[stage * 3 + step - 1],
                device_id=there(step),
                device_id_type=MESH,
            )
            for step in ((1, 2, 3) if stage < 3 else (1,))
        ]

    def start(self, stage, value):
        self.s.small[stage, self.lines[stage][0]] = value
        for copy in self.copies(stage):
            copy.start()

    def finish(self, stage):
        at, there = self.lines[stage]
        count = 4 if stage < 3 else 2
        for step in range(1, count):
            block = self.s.small.at[stage, lax.rem(at + (count - step), count)]
            pltpu.make_async_remote_copy(
                src_ref=block,
                dst_ref=block,
                send_sem=self.s.small_send.at[stage * 3 + step - 1],
                recv_sem=self.s.small_recv.at[stage * 3 + step - 1],
                device_id=there(step),
                device_id_type=MESH,
            ).wait_recv()
        value = self.s.small[stage, 0]
        for index in range(1, count):
            value = value + self.s.small[stage, index]
        return value

    def settle(self):
        for stage in range(4):
            for copy in self.copies(stage):
                copy.wait_send()


def kernel(feat, w1, w2, ws, head, targ, result, small_out, *scratch):
    s = types.SimpleNamespace(**dict(zip(SCRATCH_NAMES, scratch)))
    t, r, c = lax.axis_index("tm"), lax.axis_index("row"), lax.axis_index("col")
    place = (t, r, c)

    barrier = pltpu.get_barrier_semaphore()
    around = [
        (dt, dr, dc)
        for dt in (-1, 0, 1)
        for dr in (-1, 0, 1, 2)
        for dc in (-1, 0, 1)
        if (dt, dr, dc) != (0, 0, 0) and (dt == 0 or dr < 2)
    ] + [(2, 0, 0), (0, 0, -2), (0, 0, 2), (0, 0, 4)]
    for dt, dr, dc in around:
        pl.semaphore_signal(
            barrier,
            inc=1,
            device_id=(wrap(t, dt, N_TM), wrap(r, dr, N_ROW), wrap(c, dc, N_COL)),
            device_id_type=MESH,
        )

    core = c & 1
    mate = (t, r, c + 1 - 2 * core)

    def to_mate(number, src, dst):
        return pltpu.make_async_remote_copy(
            src_ref=src,
            dst_ref=dst,
            send_sem=s.mate_send.at[number],
            recv_sem=s.mate_recv.at[number],
            device_id=mate,
            device_id_type=MESH,
        )

    mates = [
        to_mate(0, feat, s.mate0.at[3, pl.ds(FR, FR), pl.ds(1, TH)]),
        to_mate(1, s.shift0.at[pl.ds(0, 3), pl.ds(FR, FR)], s.mate0.at[pl.ds(0, 3), pl.ds(FR, FR)]),
        to_mate(2, s.shift0.at[pl.ds(0, 3), pl.ds(0, FR)], s.mate0.at[pl.ds(0, 3), pl.ds(0, FR)]),
        to_mate(3, s.shift1.at[:, pl.ds(FR, FR)], s.mate1.at[:, pl.ds(FR, FR)]),
        to_mate(4, s.shift1.at[:, pl.ds(0, FR)], s.mate1.at[:, pl.ds(0, FR)]),
        to_mate(5, s.grads.at[1], s.mate_grads.at[1]),
        to_mate(6, s.grads.at[0], s.mate_grads.at[0]),
    ]

    def tile_rows(step):
        rows = CHUNK // TW
        return step // (TH // rows), lax.rem(step, TH // rows) * rows

    def features(step):
        frame, row = tile_rows(step)
        return feat[frame, pl.ds(row, CHUNK // TW)].reshape(CHUNK, C_IN)

    def act(rows, step):
        raw = features(step)
        frame, row = tile_rows(step)
        s.shift0[3, FR + frame, pl.ds(row + 1, CHUNK // TW)] = raw.reshape(CHUNK // TW, TW, C_IN)
        values = silu_forward(raw.astype(F32))
        put_tile(s.own0, s.columns, step, values)

    chunks(act)
    s.target[...] = jnp.zeros(s.target.shape, F32)
    s.target[:, :, 0:TW] = targ[...]
    pl.semaphore_wait(barrier, len(around))

    halo0 = Halo(place, 1, s.own0, s.other0, s.rims0, s.edges0, s.lines0, s.send0, s.recv0)
    halo1 = Halo(place, 1, s.own1, s.other1, s.rims1, s.edges1, s.lines1, s.send1, s.recv1)
    halo2 = Halo(place, -1, s.own2, s.other2, s.rims2, s.edges2, s.lines1, s.send2, s.recv2)
    halo0.start(s.columns)
    y_copies = picture_copies(place, s.target, s.y_field, s.send_y, s.recv_y)
    for copy in y_copies:
        copy.start()
    mates[0].start()

    halo0.arrived(0)
    halo0.shift(0, s.shift0, FR)
    mates[1].start()
    convolve(s.shift0, w1, s.pre, FR, 2, FR, 1, NT, False, True)
    halo0.arrived(1)
    halo0.shift(1, s.shift0, 0)
    mates[2].start()
    convolve(s.shift0, w1, s.pre, 0, 0, 1, 0, NT, False, False)

    def act_first(rows, step):
        values = silu_forward(s.pre[rows, :])
        put_tile(s.own1, s.columns, step, values)

    chunks(act_first)
    halo1.start(s.columns)
    halo1.arrived(0)
    halo1.shift(0, s.shift1, FR)
    mates[3].start()
    convolve(s.shift1, w2, s.block, FR, 2, FR, 1, NN, False, True)

    def shortcut(rows, step):
        s.block[rows, :] += lax.dot_general(features(step), ws[...], NT, preferred_element_type=F32)

    chunks(shortcut)
    halo1.arrived(1)
    halo1.shift(1, s.shift1, 0)
    mates[4].start()
    convolve(s.shift1, w2, s.block, 0, 0, 1, 0, NN, False, False)

    s.headf[...] = jnp.zeros(s.headf.shape, F32)
    s.headf[0:3, :] = head[...].astype(F32)

    def act_block(rows, step):
        s.values1[rows, :] = silu_forward(s.block[rows, :]).astype(BF16).astype(F32)

    chunks(act_block)
    lane = iota((8, 128), 1)
    for part in range(4):
        rows = slice(part * 128, part * 128 + 128)
        color = lax.dot_general(
            s.headf[...].astype(BF16), s.values1[rows, :].astype(BF16), NT, preferred_element_type=F32
        )
        for piece in range(4):
            moved = color if piece == 0 else pltpu.roll(color, 128 - TW * piece, 1)
            at = (4 * part + piece) * 8
            s.spread[at : at + 8, :] = jnp.where(lane < TW, moved, 0.0)
    for color in range(3):
        for frame in range(FR):
            s.image[color * FR + frame] = s.spread[pl.ds(frame * 64 + color, TH, stride=8), :]

    x_copies = picture_copies(place, s.image, s.x_field, s.send_x, s.recv_x)
    for copy in x_copies:
        copy.start()
    for copy in y_copies:
        copy.wait_recv()
    for copy in x_copies:
        copy.wait_recv()
    loss = picture_loss(place, s.image, s.target, s.x_field, s.y_field, s.spread)

    grad_head = None
    for part in range(4):
        rows = slice(part * 128, part * 128 + 128)
        color = None
        for piece in range(4):
            at = (4 * part + piece) * 8
            held = s.spread[at : at + 8, :]
            color = held if piece == 0 else color + pltpu.roll(held, TW * piece, 1)
        s.colors[part] = color
        term = high_dot(color, s.values1[rows, :])
        grad_head = term if grad_head is None else grad_head + term
    tail = jnp.concatenate([grad_head[:, 128:], jnp.zeros((8, 64), F32)], axis=1)
    small = Small(s, place)
    small.start(
        0,
        jnp.concatenate([grad_head[0:3, 0:128], tail[0:3], jnp.zeros((1, 128), F32), loss], axis=0),
    )

    def back_block(rows, step):
        grad = lax.dot_general(s.colors[step], s.headf[...], TN, precision=HIGH, preferred_element_type=F32)
        values = silu_backward(s.block[rows, :], grad)
        s.values1[rows, :] = values
        put_tile(s.own2, s.columns, step, values)

    chunks(back_block)
    halo2.start(s.columns)
    s.grads[1] = s.values1[...].T.astype(BF16)
    mates[5].start()
    parts = [Reduce(s, place, part, result) for part in range(PARTS)]
    s.flat[LINES - C_MID :, :] = jnp.zeros((C_MID, 128), F32)
    small.start(1, small.finish(0))
    halo2.arrived(0)
    halo2.shift(0, s.shift2, 0)
    convolve(s.shift2, w2, s.back, 0, 2, 1, 0, NT, True, True)
    for number in (3, 4, 5):
        mates[number].wait_recv()

    def second(pair, carry):
        halves = []
        for which in range(2):
            slot = jnp.minimum(core * SLOTS + pair * 2 + which, 26)
            time, row, col = slot // 9, lax.rem(slot // 3, 3), lax.rem(slot, 3)
            data = s.shift1[col, pl.ds(time, FR), pl.ds(row, TH)].reshape(VOX, C_MID)
            term = lax.dot_general(s.grads[1], data, NN, preferred_element_type=F32)
            data = s.mate1[col, pl.ds(time, FR), pl.ds(row, TH)].reshape(VOX, C_MID)
            term = term + lax.dot_general(s.mate_grads[1], data, NN, preferred_element_type=F32)
            halves.append(term.T)
        at = pl.multiple_of(SECOND_AT + pair * (3 * C_MID), C_MID)
        s.flat[pl.ds(at, C_MID), :] = halves[0][:, 0:128]
        s.flat[pl.ds(at + C_MID, C_MID), :] = halves[1][:, 0:128]
        s.flat[pl.ds(at + 2 * C_MID, C_MID), :] = jnp.concatenate([halves[0][:, 128:], halves[1][:, 128:]], axis=1)
        return carry

    lax.fori_loop(0, SLOTS // 2, second, 0)
    parts[2].scatter_start(0)
    halo2.arrived(1)
    halo2.shift(1, s.shift2, FR)
    convolve(s.shift2, w2, s.back, FR, 0, FR, 1, NT, True, False)

    def back_first(rows, step):
        s.values1[rows, :] = silu_backward(s.pre[rows, :], s.back[rows, :])

    chunks(back_first)
    s.grads[0] = s.values1[...].T.astype(BF16)
    mates[6].start()
    parts[2].scatter_middle(0)
    small.start(2, small.finish(1))
    for number in (0, 1, 2, 6):
        mates[number].wait_recv()

    def first(step, carry):
        slot = core * SLOTS + step
        extra = (slot == 27).astype(jnp.int32)
        time, row, col = slot // 9 - extra, lax.rem(slot // 3, 3) + extra, lax.rem(slot, 3) + 3 * extra
        data = s.shift0[col, pl.ds(time, FR), pl.ds(row, TH)].reshape(VOX, C_IN)
        term = lax.dot_general(s.grads[extra], data, NN, preferred_element_type=F32)
        data = s.mate0[col, pl.ds(time, FR), pl.ds(row, TH)].reshape(VOX, C_IN)
        term = term + lax.dot_general(s.mate_grads[extra], data, NN, preferred_element_type=F32)
        at = pl.multiple_of(step * (3 * C_MID), C_MID)
        for block in range(3):
            s.flat[pl.ds(at + block * C_MID, C_MID), :] = term[:, block * 128 : block * 128 + 128]
        return carry

    lax.fori_loop(0, 8, first, 0)
    parts[0].scatter_start(0)
    lax.fori_loop(8, SLOTS, first, 0)
    parts[1].scatter_start(0)
    small.start(3, small.finish(2))
    parts[2].scatter_finish(0)
    parts[2].scatter_start(1)
    for part in (0, 1):
        parts[part].scatter_middle(0)
    parts[2].scatter_middle(1)
    small_out[...] = small.finish(3)
    for part in (0, 1):
        parts[part].scatter_finish(0)
        parts[part].scatter_start(1)
    parts[2].scatter_finish(1)
    parts[2].scatter_start(2)
    for part in (0, 1):
        parts[part].scatter_middle(1)
    parts[2].scatter_middle(2)
    for part in (0, 1):
        parts[part].scatter_finish(1)
        parts[part].scatter_start(2)
    parts[2].scatter_finish(2)
    parts[2].gather_start(2)
    for part in (0, 1):
        parts[part].scatter_middle(2)
    parts[2].gather_middle(2)
    for part in (0, 1):
        parts[part].scatter_finish(2)
        parts[part].gather_start(2)
    parts[2].gather_finish(2)
    parts[2].gather_start(1)
    for part in (0, 1):
        parts[part].gather_middle(2)
    parts[2].gather_middle(1)
    for part in (0, 1):
        parts[part].gather_finish(2)
        parts[part].gather_start(1)
    parts[2].gather_finish(1)
    parts[2].gather_start(0)
    for part in (0, 1):
        parts[part].gather_middle(1)
    parts[2].gather_middle(0)
    for part in (0, 1):
        parts[part].gather_finish(1)
        parts[part].gather_start(0)
    parts[2].gather_finish(0)
    for part in (0, 1):
        parts[part].gather_middle(0)
    for part in (0, 1):
        parts[part].gather_finish(0)
    for part in parts:
        part.settle()
    for halo in (halo0, halo1, halo2):
        halo.sent()
    for copy in x_copies + y_copies + mates:
        copy.wait_send()
    small.settle()


def halo_scratch(number, chan, copies):
    return [
        (f"own{number}", pltpu.VMEM((FR, TH + 2, TW, chan), BF16)),
        (f"other{number}", pltpu.VMEM((FR, TH + 2, TW, chan), BF16)),
        (f"rims{number}", pltpu.VMEM((2, 2, 3, FR * TH, chan), BF16)),
        (f"edges{number}", pltpu.VMEM((2, FR * TH, chan), BF16)),
        (f"shift{number}", pltpu.VMEM((copies, 2 * FR, TH + 2, TW, chan), BF16)),
        (f"send{number}", pltpu.SemaphoreType.DMA((18,))),
        (f"recv{number}", pltpu.SemaphoreType.DMA((18,))),
    ]


SCRATCH = (
    halo_scratch(0, C_IN, 4)
    + halo_scratch(1, C_MID, 3)
    + halo_scratch(2, C_MID, 3)
    + [
        ("lines0", pltpu.VMEM((2, FR, 16, C_IN), F32)),
        ("lines1", pltpu.VMEM((2, FR, 16, C_MID), F32)),
        ("columns", pltpu.VMEM((2, FR * TH, C_IN), F32)),
        ("values1", pltpu.VMEM((VOX, C_MID), F32)),
        ("pre", pltpu.VMEM((VOX, C_MID), F32)),
        ("block", pltpu.VMEM((VOX, C_MID), F32)),
        ("back", pltpu.VMEM((VOX, C_MID), F32)),
        ("grads", pltpu.VMEM((2, C_MID, VOX), BF16)),
        ("mate_grads", pltpu.VMEM((2, C_MID, VOX), BF16)),
        ("mate0", pltpu.VMEM((4, 2 * FR, TH + 2, TW, C_IN), BF16)),
        ("mate1", pltpu.VMEM((3, 2 * FR, TH + 2, TW, C_MID), BF16)),
        ("mate_send", pltpu.SemaphoreType.DMA((7,))),
        ("mate_recv", pltpu.SemaphoreType.DMA((7,))),
        ("flat", pltpu.VMEM((LINES, 128), F32)),
        ("sum1", pltpu.VMEM((PARTS, SIZES[0], 128), F32)),
        ("sum2", pltpu.VMEM((PARTS, SIZES[1], 128), F32)),
        ("stage0", pltpu.VMEM((PARTS, 6, SIZES[0] // 2, 128), BF16)),
        ("stage1", pltpu.VMEM((PARTS, 2, SIZES[1] // 2, 128), F32)),
        ("stage2", pltpu.VMEM((PARTS, 2, SIZES[2] // 2, 128), F32)),
        ("inbox0", pltpu.VMEM((PARTS, 6, SIZES[0] // 2, 128), BF16)),
        ("inbox1", pltpu.VMEM((PARTS, 6, SIZES[1] // 2, 128), F32)),
        ("inbox2", pltpu.VMEM((PARTS, 6, SIZES[2] // 2, 128), F32)),
        ("scatter_send", pltpu.SemaphoreType.DMA((54,))),
        ("scatter_recv", pltpu.SemaphoreType.DMA((54,))),
        ("gather_send", pltpu.SemaphoreType.DMA((54,))),
        ("gather_recv", pltpu.SemaphoreType.DMA((54,))),
        ("share_send", pltpu.SemaphoreType.DMA((12,))),
        ("share_recv", pltpu.SemaphoreType.DMA((12,))),
        ("small", pltpu.VMEM((4, 4, 8, 128), F32)),
        ("small_send", pltpu.SemaphoreType.DMA((12,))),
        ("small_recv", pltpu.SemaphoreType.DMA((12,))),
        ("headf", pltpu.VMEM((8, C_MID), F32)),
        ("spread", pltpu.VMEM((128, 128), F32)),
        ("colors", pltpu.VMEM((4, 8, 128), F32)),
        ("image", pltpu.VMEM((6, TH, 128), F32)),
        ("target", pltpu.VMEM((6, TH, 128), F32)),
        ("x_field", pltpu.VMEM((3, 6, N_ROW * TH, 128), F32)),
        ("y_field", pltpu.VMEM((3, 6, N_ROW * TH, 128), F32)),
        ("send_x", pltpu.SemaphoreType.DMA((11,))),
        ("recv_x", pltpu.SemaphoreType.DMA((11,))),
        ("send_y", pltpu.SemaphoreType.DMA((11,))),
        ("recv_y", pltpu.SemaphoreType.DMA((11,))),
    ]
)
SCRATCH_NAMES = [name for name, _ in SCRATCH]


def widen(first_ref, second_ref, small_ref, g1, gs, g2, gh, loss):
    for which in range(2):
        for block in range(3):
            at = (which * 3 + block) * C_MID
            values = first_ref[0, at : at + C_MID, :].astype(F32)
            g1[which, :, block * 128 : block * 128 + 128] = values
    gs[...] = g1[1]
    g2[0, :, 0:128] = second_ref[0, 0:C_MID, :].astype(F32)
    g2[1, :, 0:128] = second_ref[0, C_MID : 2 * C_MID, :].astype(F32)
    rest = second_ref[0, 2 * C_MID : 3 * C_MID, :].astype(F32)
    g2[0, :, 128:] = rest[:, 0:64]
    g2[1, :, 128:] = rest[:, 64:]
    gh[:, 0:128] = small_ref[0:3, :]
    gh[:, 128:] = small_ref[3:6, 0:64]
    loss[...] = jnp.sum(small_ref[7:8, :], axis=1, keepdims=True) / (N_TM * N_ROW * N_COL)


def body(features, conv_first, conv_second, shortcut_weight, head_weight, target_frames):
    vmem = pl.BlockSpec(memory_space=pltpu.VMEM)
    flat, small = pl.pallas_call(
        kernel,
        out_shape=[
            jax.ShapeDtypeStruct((2, LINES, 128), BF16),
            jax.ShapeDtypeStruct((8, 128), F32),
        ],
        in_specs=[vmem] * 6,
        out_specs=[vmem] * 2,
        scratch_shapes=[shape for _, shape in SCRATCH],
        compiler_params=pltpu.CompilerParams(
            collective_id=0, has_side_effects=True, vmem_limit_bytes=60 * 1024 * 1024
        ),
    )(
        features,
        conv_first.transpose(0, 1, 2, 4, 3).reshape(27, C_MID, C_IN),
        conv_second.reshape(27, C_MID, C_MID),
        shortcut_weight.T,
        head_weight.T,
        target_frames.reshape(6, TH, TW),
    )
    g1, gs, g2, gh, loss = pl.pallas_call(
        widen,
        grid=(SLOTS,),
        out_shape=[
            jax.ShapeDtypeStruct((27, C_MID, C_IN), F32),
            jax.ShapeDtypeStruct((C_MID, C_IN), F32),
            jax.ShapeDtypeStruct((27, C_MID, C_MID), F32),
            jax.ShapeDtypeStruct((3, C_MID), F32),
            jax.ShapeDtypeStruct((1, 1), F32),
        ],
        in_specs=[
            pl.BlockSpec((1, 6 * C_MID, 128), lambda i: (i // 7, lax.rem(i, 7), 0)),
            pl.BlockSpec((1, 3 * C_MID, 128), lambda i: (i // 7, SLOTS + lax.rem(i, 7), 0)),
            pl.BlockSpec((8, 128), lambda i: (0, 0)),
        ],
        out_specs=[
            pl.BlockSpec((2, C_MID, C_IN), lambda i: (i, 0, 0)),
            pl.BlockSpec((C_MID, C_IN), lambda i: (0, 0)),
            pl.BlockSpec((2, C_MID, C_MID), lambda i: (i, 0, 0)),
            pl.BlockSpec((3, C_MID), lambda i: (0, 0)),
            pl.BlockSpec((1, 1), lambda i: (0, 0)),
        ],
    )(flat, flat, small)
    return (
        g1.reshape(3, 3, 3, C_MID, C_IN).transpose(0, 1, 2, 4, 3),
        g2.reshape(3, 3, 3, C_MID, C_MID),
        gs.T,
        gh.T,
        loss.reshape(()),
    )


def solution(mesh):
    return jax.shard_map(
        body,
        mesh=mesh,
        in_specs=(P("tm", "row", "col", None), P(), P(), P(), P(), P(None, "tm", "row", "col")),
        out_specs=(P(), P(), P(), P(), P()),
        check_vma=False,
    )
```

```python
import functools
import math
import types

import jax
import jax.numpy as jnp
from jax import lax
from jax.experimental import pallas as pl
from jax.experimental.pallas import tpu as pltpu
from jax.sharding import PartitionSpec as P

MESH = pl.DeviceIdType.MESH
F32, BF16 = jnp.float32, jnp.bfloat16
HIGH = lax.Precision.HIGHEST
EPSILON = 1e-06
HUBER_BETA = 0.05
SSIM_CONST_A = 0.0004
SSIM_CONST_B = 0.0036
N_TM, N_ROW, N_COL = 4, 4, 8
FR, TH, TW = 2, 8, 32
VOX = FR * TH * TW
C_IN, C_MID = 384, 192
PIX = 1.0 * 3 * VOX
RAW = [math.exp(-o * o / 4.5) for o in range(6)]
TAPS = [v / (RAW[0] + 2.0 * sum(RAW[1:])) for v in RAW]
NT = (((1,), (1,)), ((), ()))
NN = (((1,), (0,)), ((), ()))
TN = (((0,), (0,)), ((), ()))
SMALL = 96
LARGE = 4 * SMALL
SPAN = 4 * LARGE
PARTS, GROUPS = 3, 3
AXES = ("yzx", "zxy", "xyz")
SLOTS = 14
GROUP = PARTS * SPAN
LINES = GROUPS * GROUP
FILLED = SLOTS // 2 * 3 * C_MID
SIDES = [(-1, -1), (0, -1), (1, -1), (-1, 1), (0, 1), (1, 1)]


def band(distance, keep):
    total = jnp.zeros(distance.shape, F32)
    gap = jnp.abs(distance)
    for offset in range(6):
        total = total + jnp.where(gap == offset, TAPS[offset], 0.0)
    return jnp.where(keep, total, 0.0)


def iota(shape, dim):
    return lax.broadcasted_iota(jnp.int32, shape, dim)


def silu_forward(values):
    inverse = lax.rsqrt(jnp.mean(values * values, axis=-1, keepdims=True) + EPSILON)
    unit = values * inverse
    return unit / (1.0 + jnp.exp(-unit))


def silu_backward(values, grad):
    inverse = lax.rsqrt(jnp.mean(values * values, axis=-1, keepdims=True) + EPSILON)
    unit = values * inverse
    gate = 1.0 / (1.0 + jnp.exp(-unit))
    slope = grad * (gate * (1.0 + unit * (1.0 - gate)))
    return inverse * (slope - unit * jnp.mean(slope * unit, axis=-1, keepdims=True))


def wrap(index, step, count):
    return lax.rem(index + (step + count), count)


class Halo:
    def __init__(self, place, ahead, own, other, rims, edges, lines, send, recv):
        self.place, self.ahead = place, ahead
        self.tiles, self.rims, self.edges, self.lines = (own, other), rims, edges, lines
        self.send, self.recv = send, recv

    def copies(self, group):
        t, r, c = self.place
        own, target = self.tiles[0], self.tiles[group]
        there = wrap(t, self.ahead * group, N_TM)
        items = []

        def add(number, src, dst, dr, dc):
            items.append(
                pltpu.make_async_remote_copy(
                    src_ref=src,
                    dst_ref=dst,
                    send_sem=self.send.at[9 * group + number],
                    recv_sem=self.recv.at[9 * group + number],
                    device_id=(there, wrap(r, dr, N_ROW), wrap(c, dc, N_COL)),
                    device_id_type=MESH,
                )
            )

        add(0, own.at[:, 1], target.at[:, 9], -1, 0)
        add(1, own.at[:, 8], target.at[:, 0], 1, 0)
        for number, (dr, dc) in enumerate(SIDES):
            side = 0 if dc == 1 else 1
            add(2 + number, self.edges.at[1 - side], self.rims.at[group, side, 1 - dr], dr, dc)
        if group == 1:
            add(8, own.at[:, pl.ds(1, TH)], target.at[:, pl.ds(1, TH)], 0, 0)
        return items

    def start(self, edges_ref):
        chan = self.edges.shape[-1]
        self.edges[...] = edges_ref[:, :, 0:chan].astype(BF16)
        near, far = self.copies(0), self.copies(1)
        for copy in far[8:] + near + far[:8]:
            copy.start()

    def arrived(self, group):
        for copy in self.copies(group):
            copy.wait_recv()

    def sent(self):
        for group in (0, 1):
            for copy in self.copies(group):
                copy.wait_send()

    def shift(self, group, shifted, frame_at):
        t, r, c = self.place
        tile, lines = self.tiles[group], self.lines
        chan = tile.shape[-1]
        for side in (0, 1):
            for frame in range(FR):
                at = slice(frame * TH, frame * TH + TH)
                middle = self.rims[group, side, 1].astype(F32)
                lines[side, frame, 1 : TH + 1] = middle[at]
                lines[side, frame, 0:1] = self.rims[group, side, 0].astype(F32)[frame * TH + TH - 1 : frame * TH + TH]
                lines[side, frame, TH + 1 : TH + 2] = self.rims[group, side, 2].astype(F32)[frame * TH : frame * TH + 1]
        edge_t = jnp.where(self.ahead == 1, t == 0, t == N_TM - 1)
        live = 1.0 if group == 0 else jnp.where(edge_t, 0.0, 1.0)
        top = jnp.where(r == 0, 0.0, 1.0)
        bottom = jnp.where(r == N_ROW - 1, 0.0, 1.0)
        left = jnp.where(c == 0, 0.0, 1.0)
        right = jnp.where(c == N_COL - 1, 0.0, 1.0)
        column = iota((TW, chan), 0)

        def one(step, carry):
            frame, row = step // (TH + 2), lax.rem(step, TH + 2)
            scale = live * jnp.where(row == 0, top, jnp.where(row == TH + 1, bottom, 1.0))
            base = tile[frame, row].astype(F32) * scale
            first = lines[0, frame, pl.ds(row, 1), :] * (scale * left)
            last = lines[1, frame, pl.ds(row, 1), :] * (scale * right)
            shifted[0, frame_at + frame, row] = jnp.where(column == 0, first, pltpu.roll(base, 1, 0)).astype(BF16)
            shifted[1, frame_at + frame, row] = base.astype(BF16)
            shifted[2, frame_at + frame, row] = jnp.where(column == TW - 1, last, pltpu.roll(base, TW - 1, 0)).astype(BF16)
            return carry

        lax.fori_loop(0, FR * (TH + 2), one, 0)


def convolve(shifted, weights, total, full_at, full_tap, half_at, half_out, dims, flip, first):
    half = VOX // FR

    def one(row, carry):
        def tap(time, col):
            if flip:
                return weights[(time * 3 + 2 - row) * 3 + 2 - col]
            return weights[(time * 3 + row) * 3 + col]

        chan = shifted.shape[-1]
        full = None
        part = None
        for col in range(3):
            data = shifted[col, pl.ds(full_at, FR), pl.ds(row, TH)].reshape(VOX, chan)
            term = lax.dot_general(data, tap(full_tap, col), dims, preferred_element_type=F32)
            full = term if full is None else full + term
        total[...] += full
        for col in range(3):
            data = shifted[col, half_at, pl.ds(row, TH)].reshape(half, chan)
            term = lax.dot_general(data, tap(1, col), dims, preferred_element_type=F32)
            part = term if part is None else part + term
        total[pl.ds(half_out * half, half), :] += part
        return carry

    if first:
        total[...] = jnp.zeros(total.shape, F32)
    lax.fori_loop(0, 3, one, 0)


CHUNK = 128


def chunks(body):
    def one(step, carry):
        body(pl.ds(pl.multiple_of(step * CHUNK, CHUNK), CHUNK), step)
        return carry

    lax.fori_loop(0, VOX // CHUNK, one, 0)


def put_tile(tile, edges, step, values):
    rows = CHUNK // TW
    chan = values.shape[-1]
    for at in range(rows):
        edges[0, pl.ds(step * rows + at, 1), 0:chan] = values[at * TW : at * TW + 1]
        edges[1, pl.ds(step * rows + at, 1), 0:chan] = values[at * TW + TW - 1 : at * TW + TW]
    values = values.astype(BF16)
    frame, row = step // (TH // rows), lax.rem(step, TH // rows) * rows
    tile[frame, pl.ds(row + 1, rows)] = values.reshape(rows, TW, values.shape[-1])


def picture_copies(place, tile, field, send, recv):
    t, r, c = place
    items = []
    number = 0
    for dr in range(N_ROW):
        for dc in (-1, 0, 1):
            if dr == 0 and dc == 0:
                continue
            items.append(
                pltpu.make_async_remote_copy(
                    src_ref=tile,
                    dst_ref=field.at[1 - dc, :, pl.ds(pl.multiple_of(r * TH, TH), TH), :],
                    send_sem=send.at[number],
                    recv_sem=recv.at[number],
                    device_id=(t, wrap(r, dr, N_ROW), wrap(c, dc, N_COL)),
                    device_id_type=MESH,
                )
            )
            number += 1
    return items


def canvas(place, tile, field):
    t, r, c = place
    field[1, :, pl.ds(pl.multiple_of(r * TH, TH), TH), :] = tile[...]
    flat = [field[side].reshape(6 * N_ROW * TH, 128) for side in range(3)]
    left = flat[0] * jnp.where(c == 0, 0.0, 1.0)
    right = flat[2] * jnp.where(c == N_COL - 1, 0.0, 1.0)
    return left + pltpu.roll(flat[1], TW, 1) + pltpu.roll(right, 2 * TW, 1)


def high_dot(a, b):
    return jnp.dot(a, b, precision=HIGH, preferred_element_type=F32)


def picture_loss(place, x_tile, y_tile, x_field, y_field, spread):
    t, r, c = place
    rows = 6 * N_ROW * TH
    x, y = canvas(place, x_tile, x_field), canvas(place, y_tile, y_field)
    across = band(iota((128, 128), 0) - iota((128, 128), 1), True)
    row_a, row_b = iota((rows, rows), 0), iota((rows, rows), 1)
    down = band(row_a - row_b, (row_a >> 5) == (row_b >> 5))
    own_a, own_b = iota((48, rows), 0), iota((48, rows), 1)
    down_own = band((own_a & 7) + r * TH - (own_b & 31), (own_a >> 3) == (own_b >> 5))
    wide = high_dot(jnp.concatenate([x, y, x * x, y * y, x * y], axis=0), across)
    mean_x, mean_y, square_x, square_y, cross = [
        high_dot(down, wide[m * rows : (m + 1) * rows]) for m in range(5)
    ]
    var_x = square_x - mean_x * mean_x
    var_y = square_y - mean_y * mean_y
    covar = cross - mean_x * mean_y
    numer_a = 2.0 * mean_x * mean_y + SSIM_CONST_A
    numer_b = 2.0 * covar + SSIM_CONST_B
    denom_a = mean_x * mean_x + mean_y * mean_y + SSIM_CONST_A
    denom_b = var_x + var_y + SSIM_CONST_B
    denom_all = denom_a * denom_b
    ssim = numer_a * numer_b / denom_all
    slope_mean = (2.0 * mean_y * numer_b - 2.0 * mean_y * numer_a) / denom_all - ssim * (
        2.0 * mean_x / denom_a - 2.0 * mean_x / denom_b
    )
    slope_square = -ssim / denom_b
    slope_cross = 2.0 * numer_a / denom_all
    lane, line = iota((rows, 128), 1), iota((rows, 128), 0) & 31
    low = jnp.where(c == 0, TW, TW - 5)
    high = jnp.where(c == N_COL - 1, 2 * TW, 2 * TW + 5)
    inside = (lane >= low) & (lane < high)
    mine = (lane >= TW) & (lane < 2 * TW) & (line >= r * TH) & (line < r * TH + TH)
    loss = jnp.sum(jnp.where(mine, 1.0 - ssim, 0.0), axis=0, keepdims=True)
    adjoint = jnp.concatenate(
        [jnp.where(inside, slope * (-1.0 / PIX), 0.0) for slope in (slope_mean, slope_square, slope_cross)], axis=0
    )
    wide = high_dot(adjoint, across)
    pulled = [high_dot(down_own, wide[m * rows : (m + 1) * rows]) for m in range(3)]
    x_own = pltpu.roll(x_tile[...].reshape(48, 128), TW, 1)
    y_own = pltpu.roll(y_tile[...].reshape(48, 128), TW, 1)
    lane = iota((48, 128), 1)
    mine = (lane >= TW) & (lane < 2 * TW)
    diff = x_own - y_own
    size = jnp.abs(diff)
    huber = jnp.where(size < HUBER_BETA, 0.5 * diff * diff / HUBER_BETA, size - 0.5 * HUBER_BETA)
    loss = (loss + jnp.sum(jnp.where(mine, huber, 0.0), axis=0, keepdims=True)) / PIX
    grad = jnp.clip(diff / HUBER_BETA, -1.0, 1.0) / PIX + pulled[0] + 2.0 * x_own * pulled[1] + y_own * pulled[2]
    grad = pltpu.roll(jnp.where(mine, grad, 0.0), 128 - TW, 1)
    spread[...] = jnp.zeros(spread.shape, F32)
    for color in range(3):
        for frame in range(FR):
            at = (color * FR + frame) * TH
            spread[pl.ds(frame * 64 + color, TH, stride=8), :] = grad[at : at + TH]
    return loss


def axis_line(place, axis):
    t, r, c = place
    if axis == "z":
        return t, lambda step: (wrap(t, step, N_TM), r, c)
    if axis == "y":
        return r, lambda step: (t, wrap(r, step, N_ROW), c)
    return c >> 1, lambda step: (t, r, wrap(c, 2 * step, N_COL))


class Reduce:
    def __init__(self, s, place, group, result):
        self.s, self.group, self.result = s, group, result
        self.core = place[2] & 1
        self.mate = (place[0], place[1], place[2] + 1 - 2 * self.core)
        self.lines = [[axis_line(place, axis) for axis in AXES[part]] for part in range(PARTS)]

    def at(self, part, phase, step=0):
        return lax.rem(self.lines[part][phase][0] + (step + 4), 4)

    def copy(self, part, phase, stage, step, src, dst):
        sem = ((self.group * PARTS + part) * 5 + stage) * 3 + step - 1
        return pltpu.make_async_remote_copy(
            src_ref=src,
            dst_ref=dst,
            send_sem=self.s.ring_send.at[sem],
            recv_sem=self.s.ring_recv.at[sem],
            device_id=self.lines[part][phase][1](step),
            device_id_type=MESH,
        )

    def base(self, part):
        return (self.group * PARTS + part) * SPAN

    def lines_of(self, part, step):
        return pl.ds(pl.multiple_of(self.base(part) + self.at(part, 0, step) * LARGE, 32), LARGE)

    def region(self, part, large, small=None, core=None):
        core = self.core if core is None else core
        base = self.base(part) + self.at(part, 0, large) * LARGE
        if small is None:
            return self.result.at[core, pl.ds(pl.multiple_of(base, 32), LARGE), :]
        base = base + self.at(part, 1, small) * SMALL
        return self.result.at[core, pl.ds(pl.multiple_of(base, 32), SMALL), :]

    def send(self, part, stage, step):
        s, group = self.s, self.group
        if stage == 0:
            where = (group, part, step - 1)
            return self.copy(part, 0, 0, step, s.stage0.at[where], s.inbox0.at[where])
        if stage == 1:
            src = s.sum1.at[group, part, pl.ds(pl.multiple_of(self.at(part, 1, step) * SMALL, 32), SMALL), :]
            return self.copy(part, 1, 1, step, src, s.inbox1.at[group, part, step - 1])
        if stage == 2:
            block = s.last.at[group, part, self.at(part, 2)]
            return self.copy(part, 2, 2, step, block, block)
        block = self.region(part, 0, 0) if stage == 3 else self.region(part, 0)
        return self.copy(part, 1 if stage == 3 else 0, stage, step, block, block)

    def arrival(self, part, stage, step):
        if stage < 2:
            return self.send(part, stage, step)
        if stage == 2:
            block = self.s.last.at[self.group, part, self.at(part, 2, -step)]
            return self.copy(part, 2, 2, step, block, block)
        block = self.region(part, 0, -step) if stage == 3 else self.region(part, -step)
        return self.copy(part, 1 if stage == 3 else 0, stage, step, block, block)

    def share(self, part, large, arriving=False):
        block = self.region(part, large, core=1 - self.core if arriving else None)
        sem = (self.group * PARTS + part) * 4 + (large + 4) % 4
        return pltpu.make_async_remote_copy(
            src_ref=block,
            dst_ref=block,
            send_sem=self.s.share_send.at[sem],
            recv_sem=self.s.share_recv.at[sem],
            device_id=self.mate,
            device_id_type=MESH,
        )

    def run(self, stage):
        s, group = self.s, self.group
        for part in range(PARTS):
            if stage > 0:
                for step in (1, 3, 2):
                    self.arrival(part, stage - 1, step).wait_recv()
                    if stage == 5:
                        self.share(part, -step).start()
            if stage == 0:
                for step in (2, 1, 3):
                    s.stage0[group, part, step - 1] = s.flat[self.lines_of(part, step), :].astype(BF16)
            elif stage == 1:
                total = s.inbox0[group, part, 0].astype(F32) + s.inbox0[group, part, 1].astype(F32)
                total = total + s.inbox0[group, part, 2].astype(F32)
                s.sum1[group, part] = s.flat[self.lines_of(part, 0), :] + total
            elif stage == 2:
                own = s.sum1[group, part, pl.ds(pl.multiple_of(self.at(part, 1) * SMALL, 32), SMALL), :]
                total = s.inbox1[group, part, 0] + s.inbox1[group, part, 1] + s.inbox1[group, part, 2]
                s.last[group, part, self.at(part, 2)] = own + total
            elif stage == 3:
                total = s.last[group, part, 0] + s.last[group, part, 1]
                total = total + s.last[group, part, 2] + s.last[group, part, 3]
                self.region(part, 0, 0)[...] = total.astype(BF16)
            if stage < 5:
                for step in (2, 1, 3):
                    self.send(part, stage, step).start()
            if stage == 4:
                self.share(part, 0).start()

    def settle(self):
        for part in range(PARTS):
            for large in range(4):
                self.share(part, large, True).wait_recv()
            for stage in range(5):
                for step in (1, 2, 3):
                    self.send(part, stage, step).wait_send()
            for large in range(4):
                self.share(part, large).wait_send()


class Small:
    def __init__(self, s, place):
        self.s = s
        core = place[2] & 1
        self.lines = [axis_line(place, axis) for axis in "zyx"]
        self.lines.append((core, lambda step: (place[0], place[1], place[2] + 1 - 2 * core)))

    def copies(self, stage):
        at, there = self.lines[stage]
        mine = self.s.small.at[stage, at]
        return [
            pltpu.make_async_remote_copy(
                src_ref=mine,
                dst_ref=mine,
                send_sem=self.s.small_send.at[stage * 3 + step - 1],
                recv_sem=self.s.small_recv.at[stage * 3 + step - 1],
                device_id=there(step),
                device_id_type=MESH,
            )
            for step in ((1, 2, 3) if stage < 3 else (1,))
        ]

    def start(self, stage, value):
        self.s.small[stage, self.lines[stage][0]] = value
        for copy in self.copies(stage):
            copy.start()

    def finish(self, stage):
        at, there = self.lines[stage]
        count = 4 if stage < 3 else 2
        for step in range(1, count):
            block = self.s.small.at[stage, lax.rem(at + (count - step), count)]
            pltpu.make_async_remote_copy(
                src_ref=block,
                dst_ref=block,
                send_sem=self.s.small_send.at[stage * 3 + step - 1],
                recv_sem=self.s.small_recv.at[stage * 3 + step - 1],
                device_id=there(step),
                device_id_type=MESH,
            ).wait_recv()
        value = self.s.small[stage, 0]
        for index in range(1, count):
            value = value + self.s.small[stage, index]
        return value

    def settle(self):
        for stage in range(4):
            for copy in self.copies(stage):
                copy.wait_send()


def kernel(feat, w1_hbm, w2_hbm, ws, head, targ, result, small_out, *scratch):
    s = types.SimpleNamespace(**dict(zip(SCRATCH_NAMES, scratch)))
    t, r, c = lax.axis_index("tm"), lax.axis_index("row"), lax.axis_index("col")
    place = (t, r, c)

    w1, w2 = s.w1, s.w2
    loads = [
        pltpu.make_async_copy(w1_hbm, w1, s.load.at[0]),
        pltpu.make_async_copy(w2_hbm, w2, s.load.at[1]),
    ]
    barrier = pltpu.get_barrier_semaphore()
    around = [
        (dt, dr, dc)
        for dt in (-1, 0, 1)
        for dr in (-1, 0, 1, 2)
        for dc in (-1, 0, 1)
        if (dt, dr, dc) != (0, 0, 0) and (dt == 0 or dr < 2)
    ] + [(2, 0, 0), (0, 0, -2), (0, 0, 2), (0, 0, 4)]
    for dt, dr, dc in around:
        pl.semaphore_signal(
            barrier,
            inc=1,
            device_id=(wrap(t, dt, N_TM), wrap(r, dr, N_ROW), wrap(c, dc, N_COL)),
            device_id_type=MESH,
        )

    core = c & 1
    mate = (t, r, c + 1 - 2 * core)

    def to_mate(number, src, dst):
        return pltpu.make_async_remote_copy(
            src_ref=src,
            dst_ref=dst,
            send_sem=s.mate_send.at[number],
            recv_sem=s.mate_recv.at[number],
            device_id=mate,
            device_id_type=MESH,
        )

    mates = [
        to_mate(0, feat, s.mate0.at[3, pl.ds(FR, FR), pl.ds(1, TH)]),
        to_mate(1, s.shift0.at[pl.ds(0, 3), pl.ds(FR, FR)], s.mate0.at[pl.ds(0, 3), pl.ds(FR, FR)]),
        to_mate(2, s.shift0.at[pl.ds(0, 3), pl.ds(0, FR)], s.mate0.at[pl.ds(0, 3), pl.ds(0, FR)]),
        to_mate(3, s.shift1.at[:, pl.ds(FR, FR)], s.mate1.at[:, pl.ds(FR, FR)]),
        to_mate(4, s.shift1.at[:, pl.ds(0, FR)], s.mate1.at[:, pl.ds(0, FR)]),
        to_mate(5, s.grads.at[1], s.mate_grads.at[1]),
        to_mate(6, s.grads.at[0], s.mate_grads.at[0]),
    ]

    def tile_rows(step):
        rows = CHUNK // TW
        return step // (TH // rows), lax.rem(step, TH // rows) * rows

    def features(step):
        frame, row = tile_rows(step)
        return feat[frame, pl.ds(row, CHUNK // TW)].reshape(CHUNK, C_IN)

    for load in loads:
        load.start()

    def act(rows, step):
        raw = features(step)
        frame, row = tile_rows(step)
        s.shift0[3, FR + frame, pl.ds(row + 1, CHUNK // TW)] = raw.reshape(CHUNK // TW, TW, C_IN)
        values = silu_forward(raw.astype(F32))
        put_tile(s.own0, s.columns, step, values)

    chunks(act)
    s.target[...] = jnp.zeros(s.target.shape, F32)
    s.target[:, :, 0:TW] = targ[...]
    pl.semaphore_wait(barrier, len(around))

    halo0 = Halo(place, 1, s.own0, s.other0, s.rims0, s.edges0, s.lines0, s.send0, s.recv0)
    halo1 = Halo(place, 1, s.own1, s.other1, s.rims1, s.edges1, s.lines1, s.send1, s.recv1)
    halo2 = Halo(place, -1, s.own2, s.other2, s.rims2, s.edges2, s.lines1, s.send2, s.recv2)
    halo0.start(s.columns)
    y_copies = picture_copies(place, s.target, s.y_field, s.send_y, s.recv_y)
    for copy in y_copies:
        copy.start()
    mates[0].start()

    halo0.arrived(0)
    halo0.shift(0, s.shift0, FR)
    mates[1].start()
    loads[0].wait()
    convolve(s.shift0, w1, s.pre, FR, 2, FR, 1, NT, False, True)
    halo0.arrived(1)
    halo0.shift(1, s.shift0, 0)
    mates[2].start()
    convolve(s.shift0, w1, s.pre, 0, 0, 1, 0, NT, False, False)

    def act_first(rows, step):
        values = silu_forward(s.pre[rows, :])
        put_tile(s.own1, s.columns, step, values)

    chunks(act_first)
    halo1.start(s.columns)
    halo1.arrived(0)
    halo1.shift(0, s.shift1, FR)
    mates[3].start()
    loads[1].wait()
    convolve(s.shift1, w2, s.block, FR, 2, FR, 1, NN, False, True)

    def shortcut(rows, step):
        s.block[rows, :] += lax.dot_general(features(step), ws[...], NT, preferred_element_type=F32)

    chunks(shortcut)
    halo1.arrived(1)
    halo1.shift(1, s.shift1, 0)
    mates[4].start()
    convolve(s.shift1, w2, s.block, 0, 0, 1, 0, NN, False, False)

    s.headf[...] = jnp.zeros(s.headf.shape, F32)
    s.headf[0:3, :] = head[...].astype(F32)

    def act_block(rows, step):
        s.values1[rows, :] = silu_forward(s.block[rows, :]).astype(BF16).astype(F32)

    chunks(act_block)
    lane = iota((8, 128), 1)
    for part in range(4):
        rows = slice(part * 128, part * 128 + 128)
        color = lax.dot_general(
            s.headf[...].astype(BF16), s.values1[rows, :].astype(BF16), NT, preferred_element_type=F32
        )
        for piece in range(4):
            moved = color if piece == 0 else pltpu.roll(color, 128 - TW * piece, 1)
            at = (4 * part + piece) * 8
            s.spread[at : at + 8, :] = jnp.where(lane < TW, moved, 0.0)
    for color in range(3):
        for frame in range(FR):
            s.image[color * FR + frame] = s.spread[pl.ds(frame * 64 + color, TH, stride=8), :]

    x_copies = picture_copies(place, s.image, s.x_field, s.send_x, s.recv_x)
    for copy in x_copies:
        copy.start()
    for copy in y_copies:
        copy.wait_recv()
    for copy in x_copies:
        copy.wait_recv()
    loss = picture_loss(place, s.image, s.target, s.x_field, s.y_field, s.spread)

    grad_head = None
    for part in range(4):
        rows = slice(part * 128, part * 128 + 128)
        color = None
        for piece in range(4):
            at = (4 * part + piece) * 8
            held = s.spread[at : at + 8, :]
            color = held if piece == 0 else color + pltpu.roll(held, TW * piece, 1)
        s.colors[part] = color
        term = high_dot(color, s.values1[rows, :])
        grad_head = term if grad_head is None else grad_head + term
    tail = jnp.concatenate([grad_head[:, 128:], jnp.zeros((8, 64), F32)], axis=1)
    small = Small(s, place)
    small.start(
        0,
        jnp.concatenate([grad_head[0:3, 0:128], tail[0:3], jnp.zeros((1, 128), F32), loss], axis=0),
    )

    def back_block(rows, step):
        grad = lax.dot_general(s.colors[step], s.headf[...], TN, precision=HIGH, preferred_element_type=F32)
        values = silu_backward(s.block[rows, :], grad)
        s.values1[rows, :] = values
        put_tile(s.own2, s.columns, step, values)

    chunks(back_block)
    halo2.start(s.columns)
    s.grads[1] = s.values1[...].T.astype(BF16)
    mates[5].start()
    groups = [Reduce(s, place, group, result) for group in range(GROUPS)]
    for group in range(GROUPS):
        s.flat[group * GROUP + FILLED : (group + 1) * GROUP, :] = jnp.zeros((GROUP - FILLED, 128), F32)
    small.start(1, small.finish(0))
    halo2.arrived(0)
    halo2.shift(0, s.shift2, 0)
    convolve(s.shift2, w2, s.back, 0, 2, 1, 0, NT, True, True)
    for number in (3, 4, 5):
        mates[number].wait_recv()

    def second(pair, carry):
        halves = []
        for which in range(2):
            slot = jnp.minimum(core * SLOTS + pair * 2 + which, 26)
            time, row, col = slot // 9, lax.rem(slot // 3, 3), lax.rem(slot, 3)
            data = s.shift1[col, pl.ds(time, FR), pl.ds(row, TH)].reshape(VOX, C_MID)
            term = lax.dot_general(s.grads[1], data, NN, preferred_element_type=F32)
            data = s.mate1[col, pl.ds(time, FR), pl.ds(row, TH)].reshape(VOX, C_MID)
            term = term + lax.dot_general(s.mate_grads[1], data, NN, preferred_element_type=F32)
            halves.append(term.T)
        at = pl.multiple_of(2 * GROUP + pair * (3 * C_MID), C_MID)
        s.flat[pl.ds(at, C_MID), :] = halves[0][:, 0:128]
        s.flat[pl.ds(at + C_MID, C_MID), :] = halves[1][:, 0:128]
        s.flat[pl.ds(at + 2 * C_MID, C_MID), :] = jnp.concatenate([halves[0][:, 128:], halves[1][:, 128:]], axis=1)
        return carry

    lax.fori_loop(0, SLOTS // 2, second, 0)
    groups[2].run(0)
    halo2.arrived(1)
    halo2.shift(1, s.shift2, FR)
    convolve(s.shift2, w2, s.back, FR, 0, FR, 1, NT, True, False)

    def back_first(rows, step):
        s.values1[rows, :] = silu_backward(s.pre[rows, :], s.back[rows, :])

    chunks(back_first)
    s.grads[0] = s.values1[...].T.astype(BF16)
    mates[6].start()
    groups[2].run(1)
    small.start(2, small.finish(1))
    for number in (0, 1, 2, 6):
        mates[number].wait_recv()

    def first(step, carry):
        slot = core * SLOTS + step
        extra = (slot == 27).astype(jnp.int32)
        time, row, col = slot // 9 - extra, lax.rem(slot // 3, 3) + extra, lax.rem(slot, 3) + 3 * extra
        data = s.shift0[col, pl.ds(time, FR), pl.ds(row, TH)].reshape(VOX, C_IN)
        term = lax.dot_general(s.grads[extra], data, NN, preferred_element_type=F32)
        data = s.mate0[col, pl.ds(time, FR), pl.ds(row, TH)].reshape(VOX, C_IN)
        term = term + lax.dot_general(s.mate_grads[extra], data, NN, preferred_element_type=F32)
        late = (step >= SLOTS // 2).astype(jnp.int32)
        at = pl.multiple_of(late * GROUP + (step - late * (SLOTS // 2)) * (3 * C_MID), C_MID)
        for block in range(3):
            s.flat[pl.ds(at + block * C_MID, C_MID), :] = term[:, block * 128 : block * 128 + 128]
        return carry

    lax.fori_loop(0, SLOTS // 2, first, 0)
    groups[0].run(0)
    groups[2].run(2)
    lax.fori_loop(SLOTS // 2, SLOTS, first, 0)
    groups[1].run(0)
    groups[2].run(3)
    small.start(3, small.finish(2))
    groups[0].run(1)
    groups[2].run(4)
    groups[1].run(1)
    groups[0].run(2)
    groups[2].run(5)
    groups[1].run(2)
    small_out[...] = small.finish(3)
    for stage in (3, 4, 5):
        groups[0].run(stage)
        groups[1].run(stage)
    for group in groups:
        group.settle()
    for halo in (halo0, halo1, halo2):
        halo.sent()
    for copy in x_copies + y_copies + mates:
        copy.wait_send()
    small.settle()


def halo_scratch(number, chan, copies):
    return [
        (f"own{number}", pltpu.VMEM((FR, TH + 2, TW, chan), BF16)),
        (f"other{number}", pltpu.VMEM((FR, TH + 2, TW, chan), BF16)),
        (f"rims{number}", pltpu.VMEM((2, 2, 3, FR * TH, chan), BF16)),
        (f"edges{number}", pltpu.VMEM((2, FR * TH, chan), BF16)),
        (f"shift{number}", pltpu.VMEM((copies, 2 * FR, TH + 2, TW, chan), BF16)),
        (f"send{number}", pltpu.SemaphoreType.DMA((18,))),
        (f"recv{number}", pltpu.SemaphoreType.DMA((18,))),
    ]


SCRATCH = (
    halo_scratch(0, C_IN, 4)
    + halo_scratch(1, C_MID, 3)
    + halo_scratch(2, C_MID, 3)
    + [
        ("w1", pltpu.VMEM((27, C_MID, C_IN), BF16)),
        ("w2", pltpu.VMEM((27, C_MID, C_MID), BF16)),
        ("load", pltpu.SemaphoreType.DMA((2,))),
        ("lines0", pltpu.VMEM((2, FR, 16, C_IN), F32)),
        ("lines1", pltpu.VMEM((2, FR, 16, C_MID), F32)),
        ("columns", pltpu.VMEM((2, FR * TH, C_IN), F32)),
        ("values1", pltpu.VMEM((VOX, C_MID), F32)),
        ("pre", pltpu.VMEM((VOX, C_MID), F32)),
        ("block", pltpu.VMEM((VOX, C_MID), F32)),
        ("back", pltpu.VMEM((VOX, C_MID), F32)),
        ("grads", pltpu.VMEM((2, C_MID, VOX), BF16)),
        ("mate_grads", pltpu.VMEM((2, C_MID, VOX), BF16)),
        ("mate0", pltpu.VMEM((4, 2 * FR, TH + 2, TW, C_IN), BF16)),
        ("mate1", pltpu.VMEM((3, 2 * FR, TH + 2, TW, C_MID), BF16)),
        ("mate_send", pltpu.SemaphoreType.DMA((7,))),
        ("mate_recv", pltpu.SemaphoreType.DMA((7,))),
        ("flat", pltpu.VMEM((LINES, 128), F32)),
        ("stage0", pltpu.VMEM((GROUPS, PARTS, 3, LARGE, 128), BF16)),
        ("inbox0", pltpu.VMEM((GROUPS, PARTS, 3, LARGE, 128), BF16)),
        ("sum1", pltpu.VMEM((GROUPS, PARTS, LARGE, 128), F32)),
        ("inbox1", pltpu.VMEM((GROUPS, PARTS, 3, SMALL, 128), F32)),
        ("last", pltpu.VMEM((GROUPS, PARTS, 4, SMALL, 128), F32)),
        ("ring_send", pltpu.SemaphoreType.DMA((GROUPS * PARTS * 15,))),
        ("ring_recv", pltpu.SemaphoreType.DMA((GROUPS * PARTS * 15,))),
        ("share_send", pltpu.SemaphoreType.DMA((GROUPS * PARTS * 4,))),
        ("share_recv", pltpu.SemaphoreType.DMA((GROUPS * PARTS * 4,))),
        ("small", pltpu.VMEM((4, 4, 8, 128), F32)),
        ("small_send", pltpu.SemaphoreType.DMA((12,))),
        ("small_recv", pltpu.SemaphoreType.DMA((12,))),
        ("headf", pltpu.VMEM((8, C_MID), F32)),
        ("spread", pltpu.VMEM((128, 128), F32)),
        ("colors", pltpu.VMEM((4, 8, 128), F32)),
        ("image", pltpu.VMEM((6, TH, 128), F32)),
        ("target", pltpu.VMEM((6, TH, 128), F32)),
        ("x_field", pltpu.VMEM((3, 6, N_ROW * TH, 128), F32)),
        ("y_field", pltpu.VMEM((3, 6, N_ROW * TH, 128), F32)),
        ("send_x", pltpu.SemaphoreType.DMA((11,))),
        ("recv_x", pltpu.SemaphoreType.DMA((11,))),
        ("send_y", pltpu.SemaphoreType.DMA((11,))),
        ("recv_y", pltpu.SemaphoreType.DMA((11,))),
    ]
)
SCRATCH_NAMES = [name for name, _ in SCRATCH]


def widen(flat, small_ref, g1, gs, g2, gh, loss, wide1, wide2, sems):
    copies = []

    def one1(slot, carry):
        core, step = slot // SLOTS, lax.rem(slot, SLOTS)
        late = step // (SLOTS // 2)
        at = pl.multiple_of(late * GROUP + (step - late * (SLOTS // 2)) * (3 * C_MID), C_MID)
        for block in range(3):
            rows = flat[core, pl.ds(at + block * C_MID, C_MID), :]
            wide1[slot, :, block * 128 : block * 128 + 128] = rows.astype(F32)
        return carry

    def one2(pair, carry):
        core, step = pair // (SLOTS // 2), lax.rem(pair, SLOTS // 2)
        at = pl.multiple_of(2 * GROUP + step * (3 * C_MID), C_MID)
        wide2[2 * pair, :, 0:128] = flat[core, pl.ds(at, C_MID), :].astype(F32)
        wide2[2 * pair + 1, :, 0:128] = flat[core, pl.ds(at + C_MID, C_MID), :].astype(F32)
        rest = flat[core, pl.ds(at + 2 * C_MID, C_MID), :].astype(F32)
        wide2[2 * pair, :, 128:] = rest[:, 0:64]
        wide2[2 * pair + 1, :, 128:] = rest[:, 64:]
        return carry

    for piece in range(7):
        lax.fori_loop(4 * piece, 4 * piece + 4, one1, 0)
        last = min(4 * piece + 4, 27)
        rows = pl.ds(4 * piece, last - 4 * piece)
        copies.append(pltpu.make_async_copy(wide1.at[rows], g1.at[rows], sems.at[len(copies)]))
        copies[-1].start()
        lax.fori_loop(2 * piece, 2 * piece + 2, one2, 0)
        copies.append(pltpu.make_async_copy(wide2.at[rows], g2.at[rows], sems.at[len(copies)]))
        copies[-1].start()
    copies.append(pltpu.make_async_copy(wide1.at[27], gs, sems.at[len(copies)]))
    copies[-1].start()
    gh[:, 0:128] = small_ref[0:3, :]
    gh[:, 128:] = small_ref[3:6, 0:64]
    loss[...] = jnp.sum(small_ref[7:8, :], axis=1, keepdims=True) / (N_TM * N_ROW * N_COL)
    for copy in copies:
        copy.wait()


def body(features, conv_first, conv_second, shortcut_weight, head_weight, target_frames):
    vmem, hbm = pl.BlockSpec(memory_space=pltpu.VMEM), pl.BlockSpec(memory_space=pl.ANY)
    flat, small = pl.pallas_call(
        kernel,
        out_shape=[pltpu.VMEM((2, LINES, 128), BF16), pltpu.VMEM((8, 128), F32)],
        in_specs=[vmem, hbm, hbm, vmem, vmem, vmem],
        out_specs=[vmem] * 2,
        scratch_shapes=[shape for _, shape in SCRATCH],
        compiler_params=pltpu.CompilerParams(
            collective_id=0, has_side_effects=True, vmem_limit_bytes=52 * 1024 * 1024
        ),
    )(
        features,
        conv_first.transpose(0, 1, 2, 4, 3).reshape(27, C_MID, C_IN),
        conv_second.reshape(27, C_MID, C_MID),
        shortcut_weight.T,
        head_weight.T,
        target_frames.reshape(6, TH, TW),
    )
    g1, gs, g2, gh, loss = pl.pallas_call(
        widen,
        out_shape=[
            jax.ShapeDtypeStruct((27, C_MID, C_IN), F32),
            jax.ShapeDtypeStruct((C_MID, C_IN), F32),
            jax.ShapeDtypeStruct((27, C_MID, C_MID), F32),
            jax.ShapeDtypeStruct((3, C_MID), F32),
            jax.ShapeDtypeStruct((1, 1), F32),
        ],
        in_specs=[vmem] * 2,
        out_specs=[hbm] * 3 + [vmem] * 2,
        scratch_shapes=[
            pltpu.VMEM((28, C_MID, C_IN), F32),
            pltpu.VMEM((28, C_MID, C_MID), F32),
            pltpu.SemaphoreType.DMA((15,)),
        ],
        compiler_params=pltpu.CompilerParams(vmem_limit_bytes=40 * 1024 * 1024),
    )(flat, small)
    return (
        g1.reshape(3, 3, 3, C_MID, C_IN).transpose(0, 1, 2, 4, 3),
        g2.reshape(3, 3, 3, C_MID, C_MID),
        gs.T,
        gh.T,
        loss.reshape(()),
    )


def solution(mesh):
    return jax.shard_map(
        body,
        mesh=mesh,
        in_specs=(P("tm", "row", "col", None), P(), P(), P(), P(), P(None, "tm", "row", "col")),
        out_specs=(P(), P(), P(), P(), P()),
        check_vma=False,
    )
```

```python
import functools
import math
import types

import jax
import jax.numpy as jnp
from jax import lax
from jax.experimental import pallas as pl
from jax.experimental.pallas import tpu as pltpu
from jax.sharding import PartitionSpec as P

MESH = pl.DeviceIdType.MESH
F32, BF16 = jnp.float32, jnp.bfloat16
HIGH = lax.Precision.HIGHEST
EPSILON = 1e-06
HUBER_BETA = 0.05
SSIM_CONST_A = 0.0004
SSIM_CONST_B = 0.0036
N_TM, N_ROW, N_COL = 4, 4, 8
FR, TH, TW = 2, 8, 32
VOX = FR * TH * TW
C_IN, C_MID = 384, 192
PIX = 1.0 * 3 * VOX
RAW = [math.exp(-o * o / 4.5) for o in range(6)]
TAPS = [v / (RAW[0] + 2.0 * sum(RAW[1:])) for v in RAW]
NT = (((1,), (1,)), ((), ()))
NN = (((1,), (0,)), ((), ()))
TN = (((0,), (0,)), ((), ()))
PARTS, GROUPS = 3, 3
SMALL = (96, 80, 96)
LARGE = tuple(4 * size for size in SMALL)
SPAN = tuple(4 * size for size in LARGE)
AXES = ("yzx", "zxy", "xyz")
SLOTS = 14
START = (0, PARTS * SPAN[0], PARTS * (SPAN[0] + SPAN[1]))
LINES = PARTS * sum(SPAN)
FIRST_FILLED, SECOND_FILLED = SLOTS * 3 * C_MID, START[2] + SLOTS // 2 * 3 * C_MID
EARLY = 8
SIDES = [(-1, -1), (0, -1), (1, -1), (-1, 1), (0, 1), (1, 1)]


def band(distance, keep):
    total = jnp.zeros(distance.shape, F32)
    gap = jnp.abs(distance)
    for offset in range(6):
        total = total + jnp.where(gap == offset, TAPS[offset], 0.0)
    return jnp.where(keep, total, 0.0)


def iota(shape, dim):
    return lax.broadcasted_iota(jnp.int32, shape, dim)


def silu_forward(values):
    inverse = lax.rsqrt(jnp.mean(values * values, axis=-1, keepdims=True) + EPSILON)
    unit = values * inverse
    return unit / (1.0 + jnp.exp(-unit))


def silu_backward(values, grad):
    inverse = lax.rsqrt(jnp.mean(values * values, axis=-1, keepdims=True) + EPSILON)
    unit = values * inverse
    gate = 1.0 / (1.0 + jnp.exp(-unit))
    slope = grad * (gate * (1.0 + unit * (1.0 - gate)))
    return inverse * (slope - unit * jnp.mean(slope * unit, axis=-1, keepdims=True))


def wrap(index, step, count):
    return lax.rem(index + (step + count), count)


class Halo:
    def __init__(self, place, ahead, chan, own, other, rims, edges, lines, send, recv):
        self.place, self.ahead, self.chan = place, ahead, chan
        self.packed = chan % 128 != 0
        self.tiles, self.rims, self.edges, self.lines = (own, other), rims, edges, lines
        self.send, self.recv = send, recv

    def copy(self, number, src, dst, dt, dr, dc):
        t, r, c = self.place
        return pltpu.make_async_remote_copy(
            src_ref=src,
            dst_ref=dst,
            send_sem=self.send.at[number],
            recv_sem=self.recv.at[number],
            device_id=(wrap(t, dt, N_TM), wrap(r, dr, N_ROW), wrap(c, dc, N_COL)),
            device_id_type=MESH,
        )

    def rows(self, group, at):
        tile = self.tiles[group]
        return tile.at[at] if self.packed else tile.at[:, at]

    def near(self):
        items = [
            self.copy(0, self.rows(0, 1), self.rows(0, TH + 1), 0, -1, 0),
            self.copy(1, self.rows(0, TH), self.rows(0, 0), 0, 1, 0),
        ]
        for number, (dr, dc) in enumerate(SIDES):
            side = 0 if dc == 1 else 1
            items.append(self.copy(2 + number, self.edges.at[1 - side], self.rims.at[0, side, 1 - dr], 0, dr, dc))
        return items

    def far_tile(self):
        middle = pl.ds(1, TH)
        return self.copy(8, self.rows(0, middle), self.rows(1, middle), self.ahead, 0, 0)

    def far_rim(self):
        return [
            self.copy(9, self.rims.at[0], self.rims.at[1], self.ahead, 0, 0),
            self.copy(10, self.rows(0, 0), self.rows(1, 0), self.ahead, 0, 0),
            self.copy(11, self.rows(0, TH + 1), self.rows(1, TH + 1), self.ahead, 0, 0),
        ]

    def start(self, edges_ref):
        self.far_tile().start()
        self.edges[...] = edges_ref[:, :, 0 : self.chan].astype(BF16)
        for copy in self.near():
            copy.start()

    def arrived(self, group):
        for copy in self.near() if group == 0 else [self.far_tile()] + self.far_rim():
            copy.wait_recv()
        if group == 0:
            for copy in self.far_rim():
                copy.start()

    def sent(self):
        for copy in self.near() + [self.far_tile()] + self.far_rim():
            copy.wait_send()

    def shift(self, group, shifted, frame_at):
        t, r, c = self.place
        tile, lines, chan = self.tiles[group], self.lines, self.chan
        for side in (0, 1):
            for frame in range(FR):
                at = slice(frame * TH, frame * TH + TH)
                middle = self.rims[group, side, 1].astype(F32)
                lines[side, frame, 1 : TH + 1] = middle[at]
                lines[side, frame, 0:1] = self.rims[group, side, 0].astype(F32)[frame * TH + TH - 1 : frame * TH + TH]
                lines[side, frame, TH + 1 : TH + 2] = self.rims[group, side, 2].astype(F32)[frame * TH : frame * TH + 1]
        edge_t = jnp.where(self.ahead == 1, t == 0, t == N_TM - 1)
        live = 1.0 if group == 0 else jnp.where(edge_t, 0.0, 1.0)
        top = jnp.where(r == 0, 0.0, 1.0)
        bottom = jnp.where(r == N_ROW - 1, 0.0, 1.0)
        left = jnp.where(c == 0, 0.0, 1.0)
        right = jnp.where(c == N_COL - 1, 0.0, 1.0)
        column = iota((TW, chan), 0)
        for frame in range(FR):

            def one(row, carry, frame=frame):
                scale = live * jnp.where(row == 0, top, jnp.where(row == TH + 1, bottom, 1.0))
                if self.packed:
                    base = tile[row].astype(F32)[:, frame * chan : (frame + 1) * chan] * scale
                else:
                    base = tile[frame, row].astype(F32) * scale
                first = lines[0, frame, pl.ds(row, 1), :] * (scale * left)
                last = lines[1, frame, pl.ds(row, 1), :] * (scale * right)
                before, after = pltpu.roll(base, 1, 0), pltpu.roll(base, TW - 1, 0)
                shifted[0, frame_at + frame, row] = jnp.where(column == 0, first, before).astype(BF16)
                shifted[1, frame_at + frame, row] = base.astype(BF16)
                shifted[2, frame_at + frame, row] = jnp.where(column == TW - 1, last, after).astype(BF16)
                return carry

            lax.fori_loop(0, TH + 2, one, 0)


def convolve(shifted, weights, total, full_at, full_tap, half_at, half_out, dims, flip, first):
    half, chan = VOX // FR, shifted.shape[-1]
    joined = chan % 128 == 0

    def one(row, carry):
        def tap(time, col):
            if flip:
                return weights[(time * 3 + 2 - row) * 3 + 2 - col]
            return weights[(time * 3 + row) * 3 + col]

        def data(frame, col):
            return shifted[col, frame, pl.ds(row, TH)].reshape(half, chan)

        for out in range(FR):
            terms = [(full_at + out, full_tap, col) for col in range(3)]
            if out == half_out:
                terms += [(half_at, 1, col) for col in range(3)]
            if joined:
                values = jnp.concatenate([data(frame, col) for frame, _, col in terms], axis=1)
                taps = jnp.concatenate([tap(time, col) for _, time, col in terms], axis=dims[0][1][0])
                result = lax.dot_general(values, taps, dims, preferred_element_type=F32)
            else:
                result = None
                for frame, time, col in terms:
                    term = lax.dot_general(data(frame, col), tap(time, col), dims, preferred_element_type=F32)
                    result = term if result is None else result + term
            total[out * half : (out + 1) * half, :] += result
        return carry

    if first:
        total[...] = jnp.zeros(total.shape, F32)
    lax.fori_loop(0, 3, one, 0)


CHUNK = 128


def chunks(body):
    for step in range(VOX // CHUNK):
        body(slice(step * CHUNK, (step + 1) * CHUNK), step)


def put_tile(tile, edges, step, values):
    rows = CHUNK // TW
    chan = values.shape[-1]
    for at in range(rows):
        line = step * rows + at
        edges[0, line : line + 1, 0:chan] = values[at * TW : at * TW + 1]
        edges[1, line : line + 1, 0:chan] = values[at * TW + TW - 1 : at * TW + TW]
    frame, row = divmod(step * rows, TH)
    values = values.astype(BF16).reshape(rows, TW, chan)
    if len(tile.shape) == 3:
        tile[row + 1 : row + 1 + rows, :, frame * chan : (frame + 1) * chan] = values
    else:
        tile[frame, row + 1 : row + 1 + rows] = values


def picture_copies(place, tile, field, send, recv):
    t, r, c = place
    items = []
    number = 0
    for dr in range(N_ROW):
        for dc in (-1, 0, 1):
            if dr == 0 and dc == 0:
                continue
            items.append(
                pltpu.make_async_remote_copy(
                    src_ref=tile,
                    dst_ref=field.at[1 - dc, :, pl.ds(pl.multiple_of(r * TH, TH), TH), :],
                    send_sem=send.at[number],
                    recv_sem=recv.at[number],
                    device_id=(t, wrap(r, dr, N_ROW), wrap(c, dc, N_COL)),
                    device_id_type=MESH,
                )
            )
            number += 1
    return items


def canvas(place, tile, field):
    t, r, c = place
    field[1, :, pl.ds(pl.multiple_of(r * TH, TH), TH), :] = tile[...]
    flat = [field[side].reshape(6 * N_ROW * TH, 128) for side in range(3)]
    left = flat[0] * jnp.where(c == 0, 0.0, 1.0)
    right = flat[2] * jnp.where(c == N_COL - 1, 0.0, 1.0)
    return left + pltpu.roll(flat[1], TW, 1) + pltpu.roll(right, 2 * TW, 1)


def high_dot(a, b):
    return jnp.dot(a, b, precision=HIGH, preferred_element_type=F32)


def thirds(values):
    high = values.astype(BF16).astype(F32)
    rest = values - high
    middle = rest.astype(BF16).astype(F32)
    return jnp.concatenate([high, middle, rest - middle], axis=0)


WINDOW = TH + 16


def picture_bands(place, across, down, down_own):
    across[...] = band(iota((128, 128), 0) - iota((128, 128), 1), True)
    out, source = iota(down.shape, 0), iota(down.shape, 1)
    picture = sum((out >= WINDOW * at).astype(jnp.int32) for at in range(1, 6))
    line = out - WINDOW * picture + (place[1] * TH - 8)
    down[...] = band(line - (source & 31), (picture == (source >> 5)) & (line >= 0) & (line < N_ROW * TH))
    out, source = iota(down_own.shape, 0), iota(down_own.shape, 1)
    picture = sum((source >= WINDOW * at).astype(jnp.int32) for at in range(1, 6))
    down_own[...] = band((out & 7) + 8 - (source - WINDOW * picture), (out >> 3) == picture)


def blurred(maps, across, down):
    rows = maps[0].shape[0]
    wide = high_dot(jnp.concatenate(maps, axis=0), across[...])
    wide = jnp.concatenate([wide[m * rows : (m + 1) * rows] for m in range(len(maps))], axis=1)
    result = high_dot(down[...], wide)
    return [result[:, m * 128 : (m + 1) * 128] for m in range(len(maps))]


def picture_loss(place, x_tile, y_tile, x_field, y, mean_y, square_y, bands, spread):
    t, r, c = place
    across, down, down_own = bands
    x = canvas(place, x_tile, x_field)
    mean_x, square_x, cross = blurred([x, x * x, x * y], across, down)
    rows = 6 * WINDOW
    var_x = square_x - mean_x * mean_x
    var_y = square_y - mean_y * mean_y
    covar = cross - mean_x * mean_y
    numer_a = 2.0 * mean_x * mean_y + SSIM_CONST_A
    numer_b = 2.0 * covar + SSIM_CONST_B
    denom_a = mean_x * mean_x + mean_y * mean_y + SSIM_CONST_A
    denom_b = var_x + var_y + SSIM_CONST_B
    denom_all = denom_a * denom_b
    ssim = numer_a * numer_b / denom_all
    slope_mean = (2.0 * mean_y * numer_b - 2.0 * mean_y * numer_a) / denom_all - ssim * (
        2.0 * mean_x / denom_a - 2.0 * mean_x / denom_b
    )
    slope_square = -ssim / denom_b
    slope_cross = 2.0 * numer_a / denom_all
    lane, line = iota((rows, 128), 1), iota((rows, 128), 0)
    line = line - WINDOW * sum((line >= WINDOW * at).astype(jnp.int32) for at in range(1, 6)) + (r * TH - 8)
    low = jnp.where(c == 0, TW, TW - 5)
    high = jnp.where(c == N_COL - 1, 2 * TW, 2 * TW + 5)
    inside = (lane >= low) & (lane < high) & (line >= 0) & (line < N_ROW * TH)
    mine = (lane >= TW) & (lane < 2 * TW) & (line >= r * TH) & (line < r * TH + TH)
    loss = jnp.sum(jnp.where(mine, 1.0 - ssim, 0.0), axis=0, keepdims=True)
    adjoint = [jnp.where(inside, slope * (-1.0 / PIX), 0.0) for slope in (slope_mean, slope_square, slope_cross)]
    pulled = blurred(adjoint, across, down_own)
    x_own = pltpu.roll(x_tile[...].reshape(48, 128), TW, 1)
    y_own = pltpu.roll(y_tile[...].reshape(48, 128), TW, 1)
    lane = iota((48, 128), 1)
    mine = (lane >= TW) & (lane < 2 * TW)
    diff = x_own - y_own
    size = jnp.abs(diff)
    huber = jnp.where(size < HUBER_BETA, 0.5 * diff * diff / HUBER_BETA, size - 0.5 * HUBER_BETA)
    loss = (loss + jnp.sum(jnp.where(mine, huber, 0.0), axis=0, keepdims=True)) / PIX
    grad = jnp.clip(diff / HUBER_BETA, -1.0, 1.0) / PIX + pulled[0] + 2.0 * x_own * pulled[1] + y_own * pulled[2]
    grad = pltpu.roll(jnp.where(mine, grad, 0.0), 128 - TW, 1)
    spread[...] = jnp.zeros(spread.shape, F32)
    for color in range(3):
        for frame in range(FR):
            at = (color * FR + frame) * TH
            spread[pl.ds(frame * 64 + color, TH, stride=8), :] = grad[at : at + TH]
    return loss


def axis_line(place, axis):
    t, r, c = place
    if axis == "z":
        return t, lambda step: (wrap(t, step, N_TM), r, c)
    if axis == "y":
        return r, lambda step: (t, wrap(r, step, N_ROW), c)
    return c >> 1, lambda step: (t, r, wrap(c, 2 * step, N_COL))


class Reduce:
    def __init__(self, s, place, group, result):
        self.s, self.group, self.result = s, group, result
        self.small, self.large = SMALL[group], LARGE[group]
        self.core = place[2] & 1
        self.mate = (place[0], place[1], place[2] + 1 - 2 * self.core)
        self.lines = [[axis_line(place, axis) for axis in AXES[part]] for part in range(PARTS)]

    def at(self, part, phase, step=0):
        return lax.rem(self.lines[part][phase][0] + (step + 4), 4)

    def copy(self, part, phase, stage, step, src, dst):
        sem = ((self.group * PARTS + part) * 5 + stage) * 3 + step - 1
        return pltpu.make_async_remote_copy(
            src_ref=src,
            dst_ref=dst,
            send_sem=self.s.ring_send.at[sem],
            recv_sem=self.s.ring_recv.at[sem],
            device_id=self.lines[part][phase][1](step),
            device_id_type=MESH,
        )

    def base(self, part):
        return START[self.group] + part * SPAN[self.group]

    def lines_of(self, part, step):
        return pl.ds(pl.multiple_of(self.base(part) + self.at(part, 0, step) * self.large, 16), self.large)

    def region(self, part, large, small=None, core=None):
        core = self.core if core is None else core
        base = self.base(part) + self.at(part, 0, large) * self.large
        if small is None:
            return self.result.at[core, pl.ds(pl.multiple_of(base, 16), self.large), :]
        base = base + self.at(part, 1, small) * self.small
        return self.result.at[core, pl.ds(pl.multiple_of(base, 16), self.small), :]

    def send(self, part, stage, step):
        s, group = self.s, self.group
        if stage == 0:
            where = (group, part, step - 1, pl.ds(0, self.large))
            return self.copy(part, 0, 0, step, s.stage0.at[where], s.inbox0.at[where])
        if stage == 1:
            src = s.sum1.at[group, part, pl.ds(pl.multiple_of(self.at(part, 1, step) * self.small, 16), self.small), :]
            return self.copy(part, 1, 1, step, src, s.inbox1.at[group, part, step - 1, pl.ds(0, self.small)])
        if stage == 2:
            block = s.last.at[group, part, self.at(part, 2), pl.ds(0, self.small)]
            return self.copy(part, 2, 2, step, block, block)
        block = self.region(part, 0, 0) if stage == 3 else self.region(part, 0)
        return self.copy(part, 1 if stage == 3 else 0, stage, step, block, block)

    def arrival(self, part, stage, step):
        if stage < 2:
            return self.send(part, stage, step)
        if stage == 2:
            block = self.s.last.at[self.group, part, self.at(part, 2, -step), pl.ds(0, self.small)]
            return self.copy(part, 2, 2, step, block, block)
        block = self.region(part, 0, -step) if stage == 3 else self.region(part, -step)
        return self.copy(part, 1 if stage == 3 else 0, stage, step, block, block)

    def share(self, part, large, arriving=False):
        block = self.region(part, large, core=1 - self.core if arriving else None)
        sem = (self.group * PARTS + part) * 4 + (large + 4) % 4
        return pltpu.make_async_remote_copy(
            src_ref=block,
            dst_ref=block,
            send_sem=self.s.share_send.at[sem],
            recv_sem=self.s.share_recv.at[sem],
            device_id=self.mate,
            device_id_type=MESH,
        )

    def run(self, stage):
        s, group = self.s, self.group
        for part in range(PARTS):
            if stage > 0:
                for step in (1, 3, 2):
                    self.arrival(part, stage - 1, step).wait_recv()
                    if stage == 5:
                        self.share(part, -step).start()
            large, small = pl.ds(0, self.large), pl.ds(0, self.small)
            if stage == 0:
                for step in (2, 1, 3):
                    s.stage0[group, part, step - 1, large, :] = s.flat[self.lines_of(part, step), :].astype(BF16)
                    self.send(part, 0, step).start()
            elif stage == 1:
                total = [s.inbox0[group, part, index, large, :].astype(F32) for index in range(3)]
                s.sum1[group, part, large, :] = s.flat[self.lines_of(part, 0), :] + (total[0] + total[1] + total[2])
            elif stage == 2:
                own = s.sum1[group, part, pl.ds(pl.multiple_of(self.at(part, 1) * self.small, 16), self.small), :]
                total = [s.inbox1[group, part, index, small, :] for index in range(3)]
                s.last[group, part, self.at(part, 2), small, :] = own + (total[0] + total[1] + total[2])
            elif stage == 3:
                total = [s.last[group, part, index, small, :] for index in range(4)]
                self.region(part, 0, 0)[...] = ((total[0] + total[1]) + (total[2] + total[3])).astype(BF16)
            if 0 < stage < 5:
                for step in (2, 1, 3):
                    self.send(part, stage, step).start()
            if stage == 4:
                self.share(part, 0).start()

    def settle(self):
        for part in range(PARTS):
            for large in range(4):
                self.share(part, large, True).wait_recv()
            for stage in range(5):
                for step in (1, 2, 3):
                    self.send(part, stage, step).wait_send()
            for large in range(4):
                self.share(part, large).wait_send()


class Small:
    def __init__(self, s, place):
        self.s = s
        core = place[2] & 1
        self.lines = [axis_line(place, axis) for axis in "zyx"]
        self.lines.append((core, lambda step: (place[0], place[1], place[2] + 1 - 2 * core)))

    def copies(self, stage):
        at, there = self.lines[stage]
        mine = self.s.small.at[stage, at]
        return [
            pltpu.make_async_remote_copy(
                src_ref=mine,
                dst_ref=mine,
                send_sem=self.s.small_send.at[stage * 3 + step - 1],
                recv_sem=self.s.small_recv.at[stage * 3 + step - 1],
                device_id=there(step),
                device_id_type=MESH,
            )
            for step in ((1, 2, 3) if stage < 3 else (1,))
        ]

    def start(self, stage, value):
        self.s.small[stage, self.lines[stage][0]] = value
        for copy in self.copies(stage):
            copy.start()

    def finish(self, stage):
        at, there = self.lines[stage]
        count = 4 if stage < 3 else 2
        for step in range(1, count):
            block = self.s.small.at[stage, lax.rem(at + (count - step), count)]
            pltpu.make_async_remote_copy(
                src_ref=block,
                dst_ref=block,
                send_sem=self.s.small_send.at[stage * 3 + step - 1],
                recv_sem=self.s.small_recv.at[stage * 3 + step - 1],
                device_id=there(step),
                device_id_type=MESH,
            ).wait_recv()
        value = self.s.small[stage, 0]
        for index in range(1, count):
            value = value + self.s.small[stage, index]
        return value

    def settle(self):
        for stage in range(4):
            for copy in self.copies(stage):
                copy.wait_send()


def kernel(feat, w1_hbm, w2_hbm, ws, head, targ, result, small_out, *scratch):
    s = types.SimpleNamespace(**dict(zip(SCRATCH_NAMES, scratch)))
    t, r, c = lax.axis_index("tm"), lax.axis_index("row"), lax.axis_index("col")
    place = (t, r, c)

    w1, w2 = s.w1, s.w2
    loads = [
        pltpu.make_async_copy(w1_hbm, w1, s.load.at[0]),
        pltpu.make_async_copy(w2_hbm, w2, s.load.at[1]),
    ]
    barrier = pltpu.get_barrier_semaphore()
    around = [(0, dr, dc) for dr in (-1, 0, 1, 2) for dc in (-1, 0, 1) if (dr, dc) != (0, 0)]
    around += [(-1, 0, 0), (1, 0, 0), (2, 0, 0), (0, 0, -2), (0, 0, 2), (0, 0, 4)]
    for dt, dr, dc in around:
        pl.semaphore_signal(
            barrier,
            inc=1,
            device_id=(wrap(t, dt, N_TM), wrap(r, dr, N_ROW), wrap(c, dc, N_COL)),
            device_id_type=MESH,
        )

    core = c & 1
    mate = (t, r, c + 1 - 2 * core)

    def to_mate(number, src, dst):
        return pltpu.make_async_remote_copy(
            src_ref=src,
            dst_ref=dst,
            send_sem=s.mate_send.at[number],
            recv_sem=s.mate_recv.at[number],
            device_id=mate,
            device_id_type=MESH,
        )

    mates = [
        to_mate(0, feat, s.mate0.at[3, pl.ds(FR, FR), pl.ds(1, TH)]),
        to_mate(1, s.shift0.at[pl.ds(0, 3), pl.ds(FR, FR)], s.mate0.at[pl.ds(0, 3), pl.ds(FR, FR)]),
        to_mate(2, s.shift0.at[pl.ds(0, 3), pl.ds(0, FR)], s.mate0.at[pl.ds(0, 3), pl.ds(0, FR)]),
        to_mate(3, s.shift1.at[:, pl.ds(FR, FR)], s.mate1.at[:, pl.ds(FR, FR)]),
        to_mate(4, s.shift1.at[:, pl.ds(0, FR)], s.mate1.at[:, pl.ds(0, FR)]),
        to_mate(5, s.grads.at[1, :, pl.ds(0, VOX)], s.grads.at[1, :, pl.ds(VOX, VOX)]),
        to_mate(6, s.grads.at[0, :, pl.ds(0, VOX)], s.grads.at[0, :, pl.ds(VOX, VOX)]),
    ]

    def tile_rows(step):
        return divmod(step * (CHUNK // TW), TH)

    def features(step):
        frame, row = tile_rows(step)
        return feat[frame, pl.ds(row, CHUNK // TW)].reshape(CHUNK, C_IN)

    for load in loads:
        load.start()

    def act(rows, step):
        raw = features(step)
        frame, row = tile_rows(step)
        s.shift0[3, FR + frame, pl.ds(row + 1, CHUNK // TW)] = raw.reshape(CHUNK // TW, TW, C_IN)
        values = silu_forward(raw.astype(F32))
        put_tile(s.own0, s.columns, step, values)

    chunks(act)
    s.target[...] = jnp.zeros(s.target.shape, F32)
    s.target[:, :, 0:TW] = targ[...]
    pl.semaphore_wait(barrier, len(around))

    halo0 = Halo(place, 1, C_IN, s.own0, s.other0, s.rims0, s.edges0, s.lines0, s.send0, s.recv0)
    halo1 = Halo(place, 1, C_MID, s.own1, s.other1, s.rims1, s.edges1, s.lines1, s.send1, s.recv1)
    halo2 = Halo(place, -1, C_MID, s.own2, s.other2, s.rims2, s.edges2, s.lines1, s.send2, s.recv2)
    halo0.start(s.columns)
    y_copies = picture_copies(place, s.target, s.y_field, s.send_y, s.recv_y)
    for copy in y_copies:
        copy.start()
    mates[0].start()
    bands = (s.across, s.down, s.down_own)
    picture_bands(place, *bands)

    halo0.arrived(0)
    halo0.shift(0, s.shift0, FR)
    mates[1].start()
    loads[0].wait()
    convolve(s.shift0, w1, s.pre, FR, 2, FR, 1, NT, False, True)
    halo0.arrived(1)
    halo0.shift(1, s.shift0, 0)
    mates[2].start()
    convolve(s.shift0, w1, s.pre, 0, 0, 1, 0, NT, False, False)

    def act_first(rows, step):
        values = silu_forward(s.pre[rows, :])
        put_tile(s.own1, s.columns, step, values)

    chunks(act_first)
    halo1.start(s.columns)
    for copy in y_copies:
        copy.wait_recv()
    s.y_full[...] = canvas(place, s.target, s.y_field)
    s.y_blur[0], s.y_blur[1] = blurred([s.y_full[...], s.y_full[...] * s.y_full[...]], s.across, s.down)
    halo1.arrived(0)
    halo1.shift(0, s.shift1, FR)
    mates[3].start()
    loads[1].wait()
    convolve(s.shift1, w2, s.block, FR, 2, FR, 1, NN, False, True)

    def shortcut(rows, step):
        s.block[rows, :] += lax.dot_general(features(step), ws[...], NT, preferred_element_type=F32)

    chunks(shortcut)
    halo1.arrived(1)
    halo1.shift(1, s.shift1, 0)
    mates[4].start()
    convolve(s.shift1, w2, s.block, 0, 0, 1, 0, NN, False, False)

    s.headf[...] = jnp.zeros(s.headf.shape, F32)
    s.headf[0:3, :] = head[...].astype(F32)

    def act_block(rows, step):
        s.values1[rows, :] = silu_forward(s.block[rows, :]).astype(BF16).astype(F32)

    chunks(act_block)
    lane = iota((8, 128), 1)
    for part in range(4):
        rows = slice(part * 128, part * 128 + 128)
        color = lax.dot_general(
            s.headf[...].astype(BF16), s.values1[rows, :].astype(BF16), NT, preferred_element_type=F32
        )
        for piece in range(4):
            moved = color if piece == 0 else pltpu.roll(color, 128 - TW * piece, 1)
            at = (4 * part + piece) * 8
            s.spread[at : at + 8, :] = jnp.where(lane < TW, moved, 0.0)
    for color in range(3):
        for frame in range(FR):
            s.image[color * FR + frame] = s.spread[pl.ds(frame * 64 + color, TH, stride=8), :]

    x_copies = picture_copies(place, s.image, s.x_field, s.send_x, s.recv_x)
    for copy in x_copies:
        copy.start()
    for copy in x_copies:
        copy.wait_recv()
    loss = picture_loss(
        place, s.image, s.target, s.x_field, s.y_full[...], s.y_blur[0], s.y_blur[1], bands, s.spread
    )

    grad_head = None
    for part in range(4):
        rows = slice(part * 128, part * 128 + 128)
        color = None
        for piece in range(4):
            at = (4 * part + piece) * 8
            held = s.spread[at : at + 8, :]
            color = held if piece == 0 else color + pltpu.roll(held, TW * piece, 1)
        split = thirds(color)
        s.colors[part] = jnp.concatenate([split, jnp.zeros((128 - 24, 128), F32)], axis=0).T[:, 0:24].astype(BF16)
        term = jnp.dot(split.astype(BF16), s.values1[rows, :].astype(BF16), preferred_element_type=F32)
        grad_head = term if grad_head is None else grad_head + term
    grad_head = grad_head[0:8] + (grad_head[8:16] + grad_head[16:24])
    heads = jnp.concatenate([s.headf[...]] * 3, axis=0).astype(BF16)
    tail = jnp.concatenate([grad_head[:, 128:], jnp.zeros((8, 64), F32)], axis=1)
    small = Small(s, place)
    small.start(
        0,
        jnp.concatenate([grad_head[0:3, 0:128], tail[0:3], jnp.zeros((1, 128), F32), loss], axis=0),
    )

    def back_block(rows, step):
        grad = jnp.dot(s.colors[step], heads, preferred_element_type=F32)
        values = silu_backward(s.block[rows, :], grad)
        s.values1[rows, :] = values
        put_tile(s.own2, s.columns, step, values)

    chunks(back_block)
    halo2.start(s.columns)
    s.grads[1, :, 0:VOX] = s.values1[...].T.astype(BF16)
    mates[5].start()
    groups = [Reduce(s, place, group, result) for group in range(GROUPS)]
    s.flat[FIRST_FILLED : START[2], :] = jnp.zeros((START[2] - FIRST_FILLED, 128), F32)
    s.flat[SECOND_FILLED:LINES, :] = jnp.zeros((LINES - SECOND_FILLED, 128), F32)
    small.start(1, small.finish(0))
    halo2.arrived(0)
    halo2.shift(0, s.shift2, 0)
    convolve(s.shift2, w2, s.back, 0, 2, 1, 0, NT, True, True)
    for number in (3, 4, 5):
        mates[number].wait_recv()

    def patches(mine, theirs, slot):
        extra = (slot == 27).astype(jnp.int32)
        time, row, col = slot // 9 - extra, lax.rem(slot // 3, 3) + extra, lax.rem(slot, 3) + 3 * extra
        where = (col, pl.ds(time, FR), pl.ds(row, TH))
        chan = mine.shape[-1]
        return jnp.concatenate([mine[where].reshape(VOX, chan), theirs[where].reshape(VOX, chan)], axis=0)

    def second(pair, carry):
        halves = []
        for which in range(2):
            slot = jnp.minimum(core * SLOTS + pair * 2 + which, 26)
            data = patches(s.shift1, s.mate1, slot)
            halves.append(lax.dot_general(s.grads[1], data, NN, preferred_element_type=F32).T)
        at = pl.multiple_of(START[2] + pair * (3 * C_MID), 16)
        s.flat[pl.ds(at, C_MID), :] = halves[0][:, 0:128]
        s.flat[pl.ds(at + C_MID, C_MID), :] = halves[1][:, 0:128]
        s.flat[pl.ds(at + 2 * C_MID, C_MID), :] = jnp.concatenate([halves[0][:, 128:], halves[1][:, 128:]], axis=1)
        return carry

    lax.fori_loop(0, SLOTS // 2, second, 0)
    groups[2].run(0)
    halo2.arrived(1)
    halo2.shift(1, s.shift2, FR)
    convolve(s.shift2, w2, s.back, FR, 0, FR, 1, NT, True, False)

    def back_first(rows, step):
        s.values1[rows, :] = silu_backward(s.pre[rows, :], s.back[rows, :])

    chunks(back_first)
    s.grads[0, :, 0:VOX] = s.values1[...].T.astype(BF16)
    mates[6].start()
    groups[2].run(1)
    small.start(2, small.finish(1))
    for number in (0, 1, 2, 6):
        mates[number].wait_recv()

    def put_slot(step, values):
        at = pl.multiple_of(step * (3 * C_MID), C_MID)
        for block in range(3):
            s.flat[pl.ds(at + block * C_MID, C_MID), :] = values[:, block * 128 : block * 128 + 128]

    def first(pair, carry):
        data = [patches(s.shift0, s.mate0, core * SLOTS + 2 * pair + which) for which in range(2)]
        data = jnp.concatenate(data, axis=1)
        both = lax.dot_general(s.grads[0], data, NN, preferred_element_type=F32)
        put_slot(2 * pair, both[:, 0:C_IN])
        put_slot(2 * pair + 1, both[:, C_IN:])
        return carry

    def first_alone(step):
        slot = core * SLOTS + step
        data = patches(s.shift0, s.mate0, slot)
        grads = s.grads[(slot == 27).astype(jnp.int32)]
        put_slot(step, lax.dot_general(grads, data, NN, preferred_element_type=F32))

    lax.fori_loop(0, EARLY // 2, first, 0)
    groups[0].run(0)
    groups[2].run(2)
    lax.fori_loop(EARLY // 2, SLOTS // 2 - 1, first, 0)
    first_alone(SLOTS - 2)
    first_alone(SLOTS - 1)
    groups[1].run(0)
    groups[2].run(3)
    small.start(3, small.finish(2))
    groups[0].run(1)
    groups[2].run(4)
    groups[1].run(1)
    groups[0].run(2)
    groups[1].run(2)
    small_out[...] = small.finish(3)
    groups[0].run(3)
    groups[1].run(3)
    groups[0].run(4)
    groups[2].run(5)
    groups[1].run(4)
    groups[0].run(5)
    groups[1].run(5)
    for group in groups:
        group.settle()
    for halo in (halo0, halo1, halo2):
        halo.sent()
    for copy in x_copies + y_copies + mates:
        copy.wait_send()
    small.settle()


def halo_scratch(number, chan, copies):
    tile = (FR, TH + 2, TW, chan) if chan % 128 == 0 else (TH + 2, TW, FR * chan)
    return [
        (f"own{number}", pltpu.VMEM(tile, BF16)),
        (f"other{number}", pltpu.VMEM(tile, BF16)),
        (f"rims{number}", pltpu.VMEM((2, 2, 3, FR * TH, chan), BF16)),
        (f"edges{number}", pltpu.VMEM((2, FR * TH, chan), BF16)),
        (f"shift{number}", pltpu.VMEM((copies, 2 * FR, TH + 2, TW, chan), BF16)),
        (f"send{number}", pltpu.SemaphoreType.DMA((12,))),
        (f"recv{number}", pltpu.SemaphoreType.DMA((12,))),
    ]


SCRATCH = (
    halo_scratch(0, C_IN, 4)
    + halo_scratch(1, C_MID, 3)
    + halo_scratch(2, C_MID, 3)
    + [
        ("w1", pltpu.VMEM((27, C_MID, C_IN), BF16)),
        ("w2", pltpu.VMEM((27, C_MID, C_MID), BF16)),
        ("load", pltpu.SemaphoreType.DMA((2,))),
        ("lines0", pltpu.VMEM((2, FR, 16, C_IN), F32)),
        ("lines1", pltpu.VMEM((2, FR, 16, C_MID), F32)),
        ("columns", pltpu.VMEM((2, FR * TH, C_IN), F32)),
        ("values1", pltpu.VMEM((VOX, C_MID), F32)),
        ("pre", pltpu.VMEM((VOX, C_MID), F32)),
        ("block", pltpu.VMEM((VOX, C_MID), F32)),
        ("back", pltpu.VMEM((VOX, C_MID), F32)),
        ("grads", pltpu.VMEM((2, C_MID, 2 * VOX), BF16)),
        ("mate0", pltpu.VMEM((4, 2 * FR, TH + 2, TW, C_IN), BF16)),
        ("mate1", pltpu.VMEM((3, 2 * FR, TH + 2, TW, C_MID), BF16)),
        ("mate_send", pltpu.SemaphoreType.DMA((7,))),
        ("mate_recv", pltpu.SemaphoreType.DMA((7,))),
        ("flat", pltpu.VMEM((LINES, 128), F32)),
        ("stage0", pltpu.VMEM((GROUPS, PARTS, 3, max(LARGE), 128), BF16)),
        ("inbox0", pltpu.VMEM((GROUPS, PARTS, 3, max(LARGE), 128), BF16)),
        ("sum1", pltpu.VMEM((GROUPS, PARTS, max(LARGE), 128), F32)),
        ("inbox1", pltpu.VMEM((GROUPS, PARTS, 3, max(SMALL), 128), F32)),
        ("last", pltpu.VMEM((GROUPS, PARTS, 4, max(SMALL), 128), F32)),
        ("ring_send", pltpu.SemaphoreType.DMA((GROUPS * PARTS * 15,))),
        ("ring_recv", pltpu.SemaphoreType.DMA((GROUPS * PARTS * 15,))),
        ("share_send", pltpu.SemaphoreType.DMA((GROUPS * PARTS * 4,))),
        ("share_recv", pltpu.SemaphoreType.DMA((GROUPS * PARTS * 4,))),
        ("small", pltpu.VMEM((4, 4, 8, 128), F32)),
        ("small_send", pltpu.SemaphoreType.DMA((12,))),
        ("small_recv", pltpu.SemaphoreType.DMA((12,))),
        ("headf", pltpu.VMEM((8, C_MID), F32)),
        ("spread", pltpu.VMEM((128, 128), F32)),
        ("colors", pltpu.VMEM((4, 128, 24), BF16)),
        ("image", pltpu.VMEM((6, TH, 128), F32)),
        ("target", pltpu.VMEM((6, TH, 128), F32)),
        ("x_field", pltpu.VMEM((3, 6, N_ROW * TH, 128), F32)),
        ("y_field", pltpu.VMEM((3, 6, N_ROW * TH, 128), F32)),
        ("across", pltpu.VMEM((128, 128), F32)),
        ("down", pltpu.VMEM((6 * WINDOW, 6 * N_ROW * TH), F32)),
        ("down_own", pltpu.VMEM((6 * TH, 6 * WINDOW), F32)),
        ("y_full", pltpu.VMEM((6 * N_ROW * TH, 128), F32)),
        ("y_blur", pltpu.VMEM((2, 6 * WINDOW, 128), F32)),
        ("send_x", pltpu.SemaphoreType.DMA((11,))),
        ("recv_x", pltpu.SemaphoreType.DMA((11,))),
        ("send_y", pltpu.SemaphoreType.DMA((11,))),
        ("recv_y", pltpu.SemaphoreType.DMA((11,))),
    ]
)
SCRATCH_NAMES = [name for name, _ in SCRATCH]


def widen(flat, small_ref, g1, gs, g2, gh, loss, wide1, wide2, sems):
    copies = []

    def one1(slot, carry):
        core, step = slot // SLOTS, lax.rem(slot, SLOTS)
        at = pl.multiple_of(step * (3 * C_MID), C_MID)
        for block in range(3):
            rows = flat[core, pl.ds(at + block * C_MID, C_MID), :]
            wide1[slot, :, block * 128 : block * 128 + 128] = rows.astype(F32)
        return carry

    def one2(pair, carry):
        core, step = pair // (SLOTS // 2), lax.rem(pair, SLOTS // 2)
        at = pl.multiple_of(START[2] + step * (3 * C_MID), 16)
        wide2[2 * pair, :, 0:128] = flat[core, pl.ds(at, C_MID), :].astype(F32)
        wide2[2 * pair + 1, :, 0:128] = flat[core, pl.ds(at + C_MID, C_MID), :].astype(F32)
        rest = flat[core, pl.ds(at + 2 * C_MID, C_MID), :].astype(F32)
        wide2[2 * pair, :, 128:] = rest[:, 0:64]
        wide2[2 * pair + 1, :, 128:] = rest[:, 64:]
        return carry

    for piece in range(7):
        lax.fori_loop(4 * piece, 4 * piece + 4, one1, 0)
        last = min(4 * piece + 4, 27)
        rows = pl.ds(4 * piece, last - 4 * piece)
        copies.append(pltpu.make_async_copy(wide1.at[rows], g1.at[rows], sems.at[len(copies)]))
        copies[-1].start()
        lax.fori_loop(2 * piece, 2 * piece + 2, one2, 0)
        copies.append(pltpu.make_async_copy(wide2.at[rows], g2.at[rows], sems.at[len(copies)]))
        copies[-1].start()
    copies.append(pltpu.make_async_copy(wide1.at[27], gs, sems.at[len(copies)]))
    copies[-1].start()
    gh[:, 0:128] = small_ref[0:3, :]
    gh[:, 128:] = small_ref[3:6, 0:64]
    loss[...] = jnp.sum(small_ref[7:8, :], axis=1, keepdims=True) / (N_TM * N_ROW * N_COL)
    for copy in copies:
        copy.wait()


def body(features, conv_first, conv_second, shortcut_weight, head_weight, target_frames):
    vmem, hbm = pl.BlockSpec(memory_space=pltpu.VMEM), pl.BlockSpec(memory_space=pl.ANY)
    flat, small = pl.pallas_call(
        kernel,
        out_shape=[pltpu.VMEM((2, LINES, 128), BF16), pltpu.VMEM((8, 128), F32)],
        in_specs=[vmem, hbm, hbm, vmem, vmem, vmem],
        out_specs=[vmem] * 2,
        scratch_shapes=[shape for _, shape in SCRATCH],
        compiler_params=pltpu.CompilerParams(
            collective_id=0, has_side_effects=True, vmem_limit_bytes=52 * 1024 * 1024
        ),
    )(
        features,
        conv_first.transpose(0, 1, 2, 4, 3).reshape(27, C_MID, C_IN),
        conv_second.reshape(27, C_MID, C_MID),
        shortcut_weight.T,
        head_weight.T,
        target_frames.reshape(6, TH, TW),
    )
    g1, gs, g2, gh, loss = pl.pallas_call(
        widen,
        out_shape=[
            jax.ShapeDtypeStruct((27, C_MID, C_IN), F32),
            jax.ShapeDtypeStruct((C_MID, C_IN), F32),
            jax.ShapeDtypeStruct((27, C_MID, C_MID), F32),
            jax.ShapeDtypeStruct((3, C_MID), F32),
            jax.ShapeDtypeStruct((1, 1), F32),
        ],
        in_specs=[vmem] * 2,
        out_specs=[hbm] * 3 + [vmem] * 2,
        scratch_shapes=[
            pltpu.VMEM((28, C_MID, C_IN), F32),
            pltpu.VMEM((28, C_MID, C_MID), F32),
            pltpu.SemaphoreType.DMA((15,)),
        ],
        compiler_params=pltpu.CompilerParams(vmem_limit_bytes=40 * 1024 * 1024),
    )(flat, small)
    return (
        g1.reshape(3, 3, 3, C_MID, C_IN).transpose(0, 1, 2, 4, 3),
        g2.reshape(3, 3, 3, C_MID, C_MID),
        gs.T,
        gh.T,
        loss.reshape(()),
    )


def solution(mesh):
    return jax.shard_map(
        body,
        mesh=mesh,
        in_specs=(P("tm", "row", "col", None), P(), P(), P(), P(), P(None, "tm", "row", "col")),
        out_specs=(P(), P(), P(), P(), P()),
        check_vma=False,
    )
```

```python
import functools
import math
import types

import jax
import jax.numpy as jnp
from jax import lax
from jax.experimental import pallas as pl
from jax.experimental.pallas import tpu as pltpu
from jax.sharding import PartitionSpec as P

MESH = pl.DeviceIdType.MESH
F32, BF16 = jnp.float32, jnp.bfloat16
HIGH = lax.Precision.HIGHEST
EPSILON = 1e-06
HUBER_BETA = 0.05
SSIM_CONST_A = 0.0004
SSIM_CONST_B = 0.0036
N_TM, N_ROW, N_COL = 4, 4, 8
FR, TH, TW = 2, 8, 32
VOX = FR * TH * TW
C_IN, C_MID = 384, 192
PIX = 1.0 * 3 * VOX
RAW = [math.exp(-o * o / 4.5) for o in range(6)]
TAPS = [v / (RAW[0] + 2.0 * sum(RAW[1:])) for v in RAW]
NT = (((1,), (1,)), ((), ()))
NN = (((1,), (0,)), ((), ()))
TN = (((0,), (0,)), ((), ()))
PARTS, GROUPS = 3, 3
SMALL = (96, 80, 80)
LARGE = tuple(4 * size for size in SMALL)
SPAN = tuple(4 * size for size in LARGE)
AXES = ("yzx", "zxy", "xyz")
SLOTS = 14
START = (0, PARTS * SPAN[0], PARTS * (SPAN[0] + SPAN[1]))
LINES = PARTS * sum(SPAN)
FIRST_FILLED = SLOTS * 3 * C_MID
EARLY = 8
SIDES = [(-1, -1), (0, -1), (1, -1), (-1, 1), (0, 1), (1, 1)]


def band(distance, keep):
    total = jnp.zeros(distance.shape, F32)
    gap = jnp.abs(distance)
    for offset in range(6):
        total = total + jnp.where(gap == offset, TAPS[offset], 0.0)
    return jnp.where(keep, total, 0.0)


def iota(shape, dim):
    return lax.broadcasted_iota(jnp.int32, shape, dim)


def silu_forward(values):
    inverse = lax.rsqrt(jnp.mean(values * values, axis=-1, keepdims=True) + EPSILON)
    unit = values * inverse
    return unit / (1.0 + jnp.exp(-unit))


def silu_backward(values, grad):
    inverse = lax.rsqrt(jnp.mean(values * values, axis=-1, keepdims=True) + EPSILON)
    unit = values * inverse
    gate = 1.0 / (1.0 + jnp.exp(-unit))
    slope = grad * (gate * (1.0 + unit * (1.0 - gate)))
    return inverse * (slope - unit * jnp.mean(slope * unit, axis=-1, keepdims=True))


def rest_at(pair):
    last = SLOTS // 2 - 1
    at = jnp.where(pair == last, FIRST_FILLED, START[2] + pair * (3 * C_MID) + 2 * C_MID)
    return pl.multiple_of(at, 16)


def wrap(index, step, count):
    return lax.rem(index + (step + count), count)


class Halo:
    def __init__(self, place, ahead, chan, own, other, rims, edges, lines, send, recv):
        self.place, self.ahead, self.chan = place, ahead, chan
        self.packed = chan % 128 != 0
        self.tiles, self.rims, self.edges, self.lines = (own, other), rims, edges, lines
        self.send, self.recv = send, recv

    def copy(self, number, src, dst, dt, dr, dc):
        t, r, c = self.place
        return pltpu.make_async_remote_copy(
            src_ref=src,
            dst_ref=dst,
            send_sem=self.send.at[number],
            recv_sem=self.recv.at[number],
            device_id=(wrap(t, dt, N_TM), wrap(r, dr, N_ROW), wrap(c, dc, N_COL)),
            device_id_type=MESH,
        )

    def rows(self, group, at):
        tile = self.tiles[group]
        return tile.at[at] if self.packed else tile.at[:, at]

    def near(self):
        items = [
            self.copy(0, self.rows(0, 1), self.rows(0, TH + 1), 0, -1, 0),
            self.copy(1, self.rows(0, TH), self.rows(0, 0), 0, 1, 0),
        ]
        for number, (dr, dc) in enumerate(SIDES):
            side = 0 if dc == 1 else 1
            items.append(self.copy(2 + number, self.edges.at[1 - side], self.rims.at[0, side, 1 - dr], 0, dr, dc))
        return items

    def far_rows(self, number, at):
        return self.copy(number, self.rows(0, at), self.rows(1, at), self.ahead, 0, 0)

    def far_tile(self):
        return self.far_rows(8, pl.ds(1, TH))

    def far_rim(self):
        rims = self.copy(9, self.rims.at[0], self.rims.at[1], self.ahead, 0, 0)
        return [rims, self.far_rows(10, 0), self.far_rows(11, TH + 1)]

    def start(self, edges_ref):
        self.far_tile().start()
        self.edges[...] = edges_ref[:, :, 0 : self.chan].astype(BF16)
        for copy in self.near():
            copy.start()

    def arrived(self, group):
        for copy in self.near() if group == 0 else [self.far_tile()] + self.far_rim():
            copy.wait_recv()
        if group == 0:
            for copy in self.far_rim():
                copy.start()

    def sent(self):
        for copy in self.near() + [self.far_tile()] + self.far_rim():
            copy.wait_send()

    def shift(self, group, shifted, frame_at):
        t, r, c = self.place
        tile, lines, chan = self.tiles[group], self.lines, self.chan
        for side in (0, 1):
            for frame in range(FR):
                at = slice(frame * TH, frame * TH + TH)
                middle = self.rims[group, side, 1].astype(F32)
                lines[side, frame, 1 : TH + 1] = middle[at]
                lines[side, frame, 0:1] = self.rims[group, side, 0].astype(F32)[frame * TH + TH - 1 : frame * TH + TH]
                lines[side, frame, TH + 1 : TH + 2] = self.rims[group, side, 2].astype(F32)[frame * TH : frame * TH + 1]
        edge_t = jnp.where(self.ahead == 1, t == 0, t == N_TM - 1)
        live = 1.0 if group == 0 else jnp.where(edge_t, 0.0, 1.0)
        top = jnp.where(r == 0, 0.0, 1.0)
        bottom = jnp.where(r == N_ROW - 1, 0.0, 1.0)
        left = jnp.where(c == 0, 0.0, 1.0)
        right = jnp.where(c == N_COL - 1, 0.0, 1.0)
        column = iota((TW, chan), 0)
        for frame in range(FR):

            def one(row, carry, frame=frame):
                scale = live * jnp.where(row == 0, top, jnp.where(row == TH + 1, bottom, 1.0))
                if self.packed:
                    base = tile[row].astype(F32)[:, frame * chan : (frame + 1) * chan] * scale
                else:
                    base = tile[frame, row].astype(F32) * scale
                first = lines[0, frame, pl.ds(row, 1), :] * (scale * left)
                last = lines[1, frame, pl.ds(row, 1), :] * (scale * right)
                before, after = pltpu.roll(base, 1, 0), pltpu.roll(base, TW - 1, 0)
                shifted[0, frame_at + frame, row] = jnp.where(column == 0, first, before).astype(BF16)
                shifted[1, frame_at + frame, row] = base.astype(BF16)
                shifted[2, frame_at + frame, row] = jnp.where(column == TW - 1, last, after).astype(BF16)
                return carry

            lax.fori_loop(0, TH + 2, one, 0)


def convolve(shifted, weights, total, sources, dims, flip, first):
    half, chan = VOX // FR, shifted.shape[-1]
    joined = chan % 128 == 0

    def one(row, carry):
        def tap(time, col):
            if flip:
                return weights[(time * 3 + 2 - row) * 3 + 2 - col]
            return weights[(time * 3 + row) * 3 + col]

        def data(frame, col):
            return shifted[col, frame, pl.ds(row, TH)].reshape(half, chan)

        for out in range(FR):
            terms = [(frame, time, col) for frame, time in sources[out] for col in range(3)]
            if not terms:
                continue
            if joined:
                values = jnp.concatenate([data(frame, col) for frame, _, col in terms], axis=1)
                taps = jnp.concatenate([tap(time, col) for _, time, col in terms], axis=dims[0][1][0])
                result = lax.dot_general(values, taps, dims, preferred_element_type=F32)
            else:
                result = None
                for frame, time, col in terms:
                    term = lax.dot_general(data(frame, col), tap(time, col), dims, preferred_element_type=F32)
                    result = term if result is None else result + term
            total[out * half : (out + 1) * half, :] += result
        return carry

    if first:
        total[...] = jnp.zeros(total.shape, F32)
    lax.fori_loop(0, 3, one, 0)


CHUNK = 128


def chunks(body):
    for step in range(VOX // CHUNK):
        body(slice(step * CHUNK, (step + 1) * CHUNK), step)


def put_tile(tile, edges, step, values):
    rows = CHUNK // TW
    chan = values.shape[-1]
    for at in range(rows):
        line = step * rows + at
        edges[0, line : line + 1, 0:chan] = values[at * TW : at * TW + 1]
        edges[1, line : line + 1, 0:chan] = values[at * TW + TW - 1 : at * TW + TW]
    frame, row = divmod(step * rows, TH)
    values = values.astype(BF16).reshape(rows, TW, chan)
    if len(tile.shape) == 3:
        tile[row + 1 : row + 1 + rows, :, frame * chan : (frame + 1) * chan] = values
    else:
        tile[frame, row + 1 : row + 1 + rows] = values


def picture_copies(place, tile, field, send, recv):
    t, r, c = place
    items = []
    number = 0
    for dr in range(N_ROW):
        for dc in (-1, 0, 1):
            if dr == 0 and dc == 0:
                continue
            items.append(
                pltpu.make_async_remote_copy(
                    src_ref=tile,
                    dst_ref=field.at[1 - dc, :, pl.ds(pl.multiple_of(r * TH, TH), TH), :],
                    send_sem=send.at[number],
                    recv_sem=recv.at[number],
                    device_id=(t, wrap(r, dr, N_ROW), wrap(c, dc, N_COL)),
                    device_id_type=MESH,
                )
            )
            number += 1
    return items


def pack_pictures(tile, packed):
    for group in range(2):
        total = tile[4 * group]
        for number in range(4 * group + 1, min(4 * group + 4, 6)):
            total = total + pltpu.roll(tile[number], TW * (number % 4), 1)
        packed[group] = total


def canvas(place, packed, field):
    t, r, c = place
    field[1, :, pl.ds(pl.multiple_of(r * TH, TH), TH), :] = packed[...]
    lane = iota((N_ROW * TH, 128), 1)
    low = jnp.where(c == 0, TW, 0)
    high = jnp.where(c == N_COL - 1, 2 * TW, 3 * TW)
    pictures = []
    for number in range(6):
        group, place_in = divmod(number, 4)
        total = jnp.zeros((N_ROW * TH, 128), F32)
        for side in range(3):
            turn = (TW * (side - place_in)) % 128
            moved = pltpu.roll(field[side, group], turn, 1) if turn else field[side, group]
            total = jnp.where((lane >= TW * side) & (lane < TW * side + TW), moved, total)
        pictures.append(jnp.where((lane >= low) & (lane < high), total, 0.0))
    return jnp.concatenate(pictures, axis=0)


def high_dot(a, b):
    return jnp.dot(a, b, precision=HIGH, preferred_element_type=F32)


def thirds(values):
    high = values.astype(BF16).astype(F32)
    rest = values - high
    middle = rest.astype(BF16).astype(F32)
    return jnp.concatenate([high, middle, rest - middle], axis=0)


WINDOW = TH + 16


def picture_bands(place, across, down, down_own):
    across[...] = band(iota((128, 128), 0) - iota((128, 128), 1), True)
    out, source = iota(down.shape, 0), iota(down.shape, 1)
    picture = sum((out >= WINDOW * at).astype(jnp.int32) for at in range(1, 6))
    line = out - WINDOW * picture + (place[1] * TH - 8)
    down[...] = band(line - (source & 31), (picture == (source >> 5)) & (line >= 0) & (line < N_ROW * TH))
    out, source = iota(down_own.shape, 0), iota(down_own.shape, 1)
    picture = sum((source >= WINDOW * at).astype(jnp.int32) for at in range(1, 6))
    down_own[...] = band((out & 7) + 8 - (source - WINDOW * picture), (out >> 3) == picture)


def blurred(maps, across, down):
    rows = maps[0].shape[0]
    wide = high_dot(jnp.concatenate(maps, axis=0), across[...])
    wide = jnp.concatenate([wide[m * rows : (m + 1) * rows] for m in range(len(maps))], axis=1)
    result = high_dot(down[...], wide)
    return [result[:, m * 128 : (m + 1) * 128] for m in range(len(maps))]


def picture_loss(place, x_tile, y_tile, x_packed, x_field, y, mean_y, square_y, bands, spread):
    t, r, c = place
    across, down, down_own = bands
    x = canvas(place, x_packed, x_field)
    mean_x, square_x, cross = blurred([x, x * x, x * y], across, down)
    rows = 6 * WINDOW
    var_x = square_x - mean_x * mean_x
    var_y = square_y - mean_y * mean_y
    covar = cross - mean_x * mean_y
    numer_a = 2.0 * mean_x * mean_y + SSIM_CONST_A
    numer_b = 2.0 * covar + SSIM_CONST_B
    denom_a = mean_x * mean_x + mean_y * mean_y + SSIM_CONST_A
    denom_b = var_x + var_y + SSIM_CONST_B
    denom_all = denom_a * denom_b
    ssim = numer_a * numer_b / denom_all
    slope_mean = (2.0 * mean_y * numer_b - 2.0 * mean_y * numer_a) / denom_all - ssim * (
        2.0 * mean_x / denom_a - 2.0 * mean_x / denom_b
    )
    slope_square = -ssim / denom_b
    slope_cross = 2.0 * numer_a / denom_all
    lane, line = iota((rows, 128), 1), iota((rows, 128), 0)
    line = line - WINDOW * sum((line >= WINDOW * at).astype(jnp.int32) for at in range(1, 6)) + (r * TH - 8)
    low = jnp.where(c == 0, TW, TW - 5)
    high = jnp.where(c == N_COL - 1, 2 * TW, 2 * TW + 5)
    inside = (lane >= low) & (lane < high) & (line >= 0) & (line < N_ROW * TH)
    mine = (lane >= TW) & (lane < 2 * TW) & (line >= r * TH) & (line < r * TH + TH)
    loss = jnp.sum(jnp.where(mine, 1.0 - ssim, 0.0), axis=0, keepdims=True)
    adjoint = [jnp.where(inside, slope * (-1.0 / PIX), 0.0) for slope in (slope_mean, slope_square, slope_cross)]
    pulled = blurred(adjoint, across, down_own)
    x_own = pltpu.roll(x_tile[...].reshape(48, 128), TW, 1)
    y_own = pltpu.roll(y_tile[...].reshape(48, 128), TW, 1)
    lane = iota((48, 128), 1)
    mine = (lane >= TW) & (lane < 2 * TW)
    diff = x_own - y_own
    size = jnp.abs(diff)
    huber = jnp.where(size < HUBER_BETA, 0.5 * diff * diff / HUBER_BETA, size - 0.5 * HUBER_BETA)
    loss = (loss + jnp.sum(jnp.where(mine, huber, 0.0), axis=0, keepdims=True)) / PIX
    grad = jnp.clip(diff / HUBER_BETA, -1.0, 1.0) / PIX + pulled[0] + 2.0 * x_own * pulled[1] + y_own * pulled[2]
    grad = pltpu.roll(jnp.where(mine, grad, 0.0), 128 - TW, 1)
    spread[...] = jnp.zeros(spread.shape, F32)
    for color in range(3):
        for frame in range(FR):
            at = (color * FR + frame) * TH
            spread[pl.ds(frame * 64 + color, TH, stride=8), :] = grad[at : at + TH]
    return loss


def axis_line(place, axis):
    t, r, c = place
    if axis == "z":
        return t, lambda step: (wrap(t, step, N_TM), r, c)
    if axis == "y":
        return r, lambda step: (t, wrap(r, step, N_ROW), c)
    return c >> 1, lambda step: (t, r, wrap(c, 2 * step, N_COL))


class Reduce:
    def __init__(self, s, place, group, result):
        self.s, self.group, self.result = s, group, result
        self.small, self.large = SMALL[group], LARGE[group]
        self.core = place[2] & 1
        self.mate = (place[0], place[1], place[2] + 1 - 2 * self.core)
        self.lines = [[axis_line(place, axis) for axis in AXES[part]] for part in range(PARTS)]

    def at(self, part, phase, step=0):
        return lax.rem(self.lines[part][phase][0] + (step + 4), 4)

    def copy(self, part, phase, stage, step, src, dst):
        sem = ((self.group * PARTS + part) * 5 + stage) * 3 + step - 1
        return pltpu.make_async_remote_copy(
            src_ref=src,
            dst_ref=dst,
            send_sem=self.s.ring_send.at[sem],
            recv_sem=self.s.ring_recv.at[sem],
            device_id=self.lines[part][phase][1](step),
            device_id_type=MESH,
        )

    def base(self, part):
        return START[self.group] + part * SPAN[self.group]

    def lines_of(self, part, step):
        return pl.ds(pl.multiple_of(self.base(part) + self.at(part, 0, step) * self.large, 16), self.large)

    def region(self, part, large, small=None, core=None):
        core = self.core if core is None else core
        base = self.base(part) + self.at(part, 0, large) * self.large
        if small is None:
            return self.result.at[core, pl.ds(pl.multiple_of(base, 16), self.large), :]
        base = base + self.at(part, 1, small) * self.small
        return self.result.at[core, pl.ds(pl.multiple_of(base, 16), self.small), :]

    def send(self, part, stage, step):
        s, group = self.s, self.group
        if stage == 0:
            where = (group, part, step - 1, pl.ds(0, self.large))
            return self.copy(part, 0, 0, step, s.stage0.at[where], s.inbox0.at[where])
        if stage == 1:
            src = s.sum1.at[group, part, pl.ds(pl.multiple_of(self.at(part, 1, step) * self.small, 16), self.small), :]
            return self.copy(part, 1, 1, step, src, s.inbox1.at[group, part, step - 1, pl.ds(0, self.small)])
        if stage == 2:
            block = s.last.at[group, part, self.at(part, 2), pl.ds(0, self.small)]
            return self.copy(part, 2, 2, step, block, block)
        block = self.region(part, 0, 0) if stage == 3 else self.region(part, 0)
        return self.copy(part, 1 if stage == 3 else 0, stage, step, block, block)

    def arrival(self, part, stage, step):
        if stage < 2:
            return self.send(part, stage, step)
        if stage == 2:
            block = self.s.last.at[self.group, part, self.at(part, 2, -step), pl.ds(0, self.small)]
            return self.copy(part, 2, 2, step, block, block)
        block = self.region(part, 0, -step) if stage == 3 else self.region(part, -step)
        return self.copy(part, 1 if stage == 3 else 0, stage, step, block, block)

    def share(self, part, large, arriving=False):
        block = self.region(part, large, core=1 - self.core if arriving else None)
        sem = (self.group * PARTS + part) * 4 + (large + 4) % 4
        return pltpu.make_async_remote_copy(
            src_ref=block,
            dst_ref=block,
            send_sem=self.s.share_send.at[sem],
            recv_sem=self.s.share_recv.at[sem],
            device_id=self.mate,
            device_id_type=MESH,
        )

    def run(self, stage):
        s, group = self.s, self.group
        if stage == 5:
            for earlier in range(4):
                self.left(earlier)
        for part in range(PARTS):
            if stage > 0:
                for step in (1, 3, 2):
                    self.arrival(part, stage - 1, step).wait_recv()
                    if stage == 5:
                        self.share(part, -step).start()
            large, small = pl.ds(0, self.large), pl.ds(0, self.small)
            if stage == 0:
                for step in (2, 1, 3):
                    s.stage0[group, part, step - 1, large, :] = s.flat[self.lines_of(part, step), :].astype(BF16)
                    self.send(part, 0, step).start()
            elif stage == 1:
                total = [s.inbox0[group, part, index, large, :].astype(F32) for index in range(3)]
                s.sum1[group, part, large, :] = s.flat[self.lines_of(part, 0), :] + (total[0] + total[1] + total[2])
            elif stage == 2:
                own = s.sum1[group, part, pl.ds(pl.multiple_of(self.at(part, 1) * self.small, 16), self.small), :]
                total = [s.inbox1[group, part, index, small, :] for index in range(3)]
                s.last[group, part, self.at(part, 2), small, :] = own + (total[0] + total[1] + total[2])
            elif stage == 3:
                total = [s.last[group, part, index, small, :] for index in range(4)]
                self.region(part, 0, 0)[...] = ((total[0] + total[1]) + (total[2] + total[3])).astype(BF16)
            if 0 < stage < 5:
                for step in (2, 1, 3):
                    self.send(part, stage, step).start()
            if stage == 4:
                self.share(part, 0).start()

    def left(self, stage):
        for part in range(PARTS):
            for step in (1, 2, 3):
                self.send(part, stage, step).wait_send()

    def settle(self):
        self.left(4)
        for part in range(PARTS):
            for large in range(4):
                self.share(part, large, True).wait_recv()
            for large in range(4):
                self.share(part, large).wait_send()


class Small:
    def __init__(self, s, place):
        self.s = s
        core = place[2] & 1
        self.lines = [axis_line(place, axis) for axis in "zyx"]
        self.lines.append((core, lambda step: (place[0], place[1], place[2] + 1 - 2 * core)))

    def copies(self, stage):
        at, there = self.lines[stage]
        mine = self.s.small.at[stage, at]
        return [
            pltpu.make_async_remote_copy(
                src_ref=mine,
                dst_ref=mine,
                send_sem=self.s.small_send.at[stage * 3 + step - 1],
                recv_sem=self.s.small_recv.at[stage * 3 + step - 1],
                device_id=there(step),
                device_id_type=MESH,
            )
            for step in ((1, 2, 3) if stage < 3 else (1,))
        ]

    def start(self, stage, value):
        self.s.small[stage, self.lines[stage][0]] = value
        for copy in self.copies(stage):
            copy.start()

    def finish(self, stage):
        at, there = self.lines[stage]
        count = 4 if stage < 3 else 2
        for step in range(1, count):
            block = self.s.small.at[stage, lax.rem(at + (count - step), count)]
            pltpu.make_async_remote_copy(
                src_ref=block,
                dst_ref=block,
                send_sem=self.s.small_send.at[stage * 3 + step - 1],
                recv_sem=self.s.small_recv.at[stage * 3 + step - 1],
                device_id=there(step),
                device_id_type=MESH,
            ).wait_recv()
        value = self.s.small[stage, 0]
        for index in range(1, count):
            value = value + self.s.small[stage, index]
        return value

    def settle(self):
        for stage in range(4):
            for copy in self.copies(stage):
                copy.wait_send()


def kernel(feat, w1_hbm, w2_hbm, ws, head, targ, result, small_out, *scratch):
    s = types.SimpleNamespace(**dict(zip(SCRATCH_NAMES, scratch)))
    t, r, c = lax.axis_index("tm"), lax.axis_index("row"), lax.axis_index("col")
    place = (t, r, c)

    w1, w2 = s.w1, s.w2
    loads = [
        pltpu.make_async_copy(w1_hbm, w1, s.load.at[0]),
        pltpu.make_async_copy(w2_hbm, w2, s.load.at[1]),
    ]
    barrier = pltpu.get_barrier_semaphore()
    around = [(0, dr, dc) for dr in (-1, 0, 1, 2) for dc in (-1, 0, 1) if (dr, dc) != (0, 0)]
    around += [(-1, 0, 0), (1, 0, 0), (2, 0, 0), (0, 0, -2), (0, 0, 2), (0, 0, 4)]
    for dt, dr, dc in around:
        pl.semaphore_signal(
            barrier,
            inc=1,
            device_id=(wrap(t, dt, N_TM), wrap(r, dr, N_ROW), wrap(c, dc, N_COL)),
            device_id_type=MESH,
        )

    core = c & 1
    mate = (t, r, c + 1 - 2 * core)

    def to_mate(number, src, dst):
        return pltpu.make_async_remote_copy(
            src_ref=src,
            dst_ref=dst,
            send_sem=s.mate_send.at[number],
            recv_sem=s.mate_recv.at[number],
            device_id=mate,
            device_id_type=MESH,
        )

    mates = [
        to_mate(0, feat, s.mate0.at[3, pl.ds(FR, FR), pl.ds(1, TH)]),
        to_mate(1, s.shift0.at[pl.ds(0, 3), pl.ds(FR, FR)], s.mate0.at[pl.ds(0, 3), pl.ds(FR, FR)]),
        to_mate(2, s.shift0.at[pl.ds(0, 3), pl.ds(0, FR)], s.mate0.at[pl.ds(0, 3), pl.ds(0, FR)]),
        to_mate(3, s.shift1.at[:, pl.ds(FR, FR)], s.mate1.at[:, pl.ds(FR, FR)]),
        to_mate(4, s.shift1.at[:, pl.ds(0, FR)], s.mate1.at[:, pl.ds(0, FR)]),
        to_mate(5, s.grads.at[1, :, pl.ds(0, VOX)], s.grads.at[1, :, pl.ds(VOX, VOX)]),
        to_mate(6, s.grads.at[0, :, pl.ds(0, VOX)], s.grads.at[0, :, pl.ds(VOX, VOX)]),
    ]

    def tile_rows(step):
        return divmod(step * (CHUNK // TW), TH)

    def features(step):
        frame, row = tile_rows(step)
        return feat[frame, pl.ds(row, CHUNK // TW)].reshape(CHUNK, C_IN)

    for load in loads:
        load.start()

    def act(rows, step):
        raw = features(step)
        frame, row = tile_rows(step)
        s.shift0[3, FR + frame, pl.ds(row + 1, CHUNK // TW)] = raw.reshape(CHUNK // TW, TW, C_IN)
        values = silu_forward(raw.astype(F32))
        put_tile(s.own0, s.columns, step, values)

    chunks(act)
    s.target[...] = jnp.zeros(s.target.shape, F32)
    s.target[:, :, 0:TW] = targ[...]
    pack_pictures(s.target, s.y_packed)
    pl.semaphore_wait(barrier, len(around))

    halo0 = Halo(place, 1, C_IN, s.own0, s.other0, s.rims0, s.edges0, s.lines0, s.send0, s.recv0)
    halo1 = Halo(place, 1, C_MID, s.own1, s.other1, s.rims1, s.edges1, s.lines1, s.send1, s.recv1)
    halo2 = Halo(place, -1, C_MID, s.own2, s.other2, s.rims2, s.edges2, s.lines1, s.send2, s.recv2)
    halo0.start(s.columns)
    y_copies = picture_copies(place, s.y_packed, s.y_field, s.send_y, s.recv_y)
    for copy in y_copies:
        copy.start()
    bands = (s.across, s.down, s.down_own)
    picture_bands(place, *bands)

    halo0.arrived(0)
    halo0.shift(0, s.shift0, FR)
    loads[0].wait()
    convolve(s.shift0, w1, s.pre, ([(2, 2)], [(3, 2), (2, 1)]), NT, False, True)
    halo0.arrived(1)
    halo0.shift(1, s.shift0, 0)
    convolve(s.shift0, w1, s.pre, ([(0, 0), (1, 1)], [(1, 0)]), NT, False, False)

    def act_first(rows, step):
        values = silu_forward(s.pre[rows, :])
        put_tile(s.own1, s.columns, step, values)

    chunks(act_first)
    halo1.start(s.columns)
    for number in (0, 1, 2):
        mates[number].start()
    for copy in y_copies:
        copy.wait_recv()
    s.y_full[...] = canvas(place, s.y_packed, s.y_field)
    s.y_blur[0], s.y_blur[1] = blurred([s.y_full[...], s.y_full[...] * s.y_full[...]], s.across, s.down)
    halo1.arrived(0)
    halo1.shift(0, s.shift1, FR)
    loads[1].wait()
    convolve(s.shift1, w2, s.block, ([(2, 2)], [(3, 2), (2, 1)]), NN, False, True)

    def shortcut(rows, step):
        s.block[rows, :] += lax.dot_general(features(step), ws[...], NT, preferred_element_type=F32)

    chunks(shortcut)
    halo1.arrived(1)
    halo1.shift(1, s.shift1, 0)
    convolve(s.shift1, w2, s.block, ([(0, 0), (1, 1)], [(1, 0)]), NN, False, False)

    s.headf[...] = jnp.zeros(s.headf.shape, F32)
    s.headf[0:3, :] = head[...].astype(F32)

    def act_block(rows, step):
        s.values1[rows, :] = silu_forward(s.block[rows, :]).astype(BF16).astype(F32)

    chunks(act_block)
    lane = iota((8, 128), 1)
    for part in range(4):
        rows = slice(part * 128, part * 128 + 128)
        color = lax.dot_general(
            s.headf[...].astype(BF16), s.values1[rows, :].astype(BF16), NT, preferred_element_type=F32
        )
        for piece in range(4):
            moved = color if piece == 0 else pltpu.roll(color, 128 - TW * piece, 1)
            at = (4 * part + piece) * 8
            s.spread[at : at + 8, :] = jnp.where(lane < TW, moved, 0.0)
    for color in range(3):
        for frame in range(FR):
            s.image[color * FR + frame] = s.spread[pl.ds(frame * 64 + color, TH, stride=8), :]

    pack_pictures(s.image, s.x_packed)
    x_copies = picture_copies(place, s.x_packed, s.x_field, s.send_x, s.recv_x)
    for copy in x_copies:
        copy.start()
    for number in (3, 4):
        mates[number].start()
    for copy in x_copies:
        copy.wait_recv()
    loss = picture_loss(
        place, s.image, s.target, s.x_packed, s.x_field, s.y_full[...], s.y_blur[0], s.y_blur[1], bands, s.spread
    )

    grad_head = None
    for part in range(4):
        rows = slice(part * 128, part * 128 + 128)
        color = None
        for piece in range(4):
            at = (4 * part + piece) * 8
            held = s.spread[at : at + 8, :]
            color = held if piece == 0 else color + pltpu.roll(held, TW * piece, 1)
        split = thirds(color)
        s.colors[part] = jnp.concatenate([split, jnp.zeros((128 - 24, 128), F32)], axis=0).T[:, 0:24].astype(BF16)
        term = jnp.dot(split.astype(BF16), s.values1[rows, :].astype(BF16), preferred_element_type=F32)
        grad_head = term if grad_head is None else grad_head + term
    grad_head = grad_head[0:8] + (grad_head[8:16] + grad_head[16:24])
    heads = jnp.concatenate([s.headf[...]] * 3, axis=0).astype(BF16)
    tail = jnp.concatenate([grad_head[:, 128:], jnp.zeros((8, 64), F32)], axis=1)
    small = Small(s, place)
    small.start(
        0,
        jnp.concatenate([grad_head[0:3, 0:128], tail[0:3], jnp.zeros((1, 128), F32), loss], axis=0),
    )

    def back_block(rows, step):
        grad = jnp.dot(s.colors[step], heads, preferred_element_type=F32)
        values = silu_backward(s.block[rows, :], grad)
        s.values1[rows, :] = values
        put_tile(s.own2, s.columns, step, values)

    chunks(back_block)
    halo2.start(s.columns)
    s.grads[1, :, 0:VOX] = s.values1[...].T.astype(BF16)
    mates[5].start()
    groups = [Reduce(s, place, group, result) for group in range(GROUPS)]
    s.flat[FIRST_FILLED + C_MID : START[2], :] = jnp.zeros((START[2] - FIRST_FILLED - C_MID, 128), F32)
    small.start(1, small.finish(0))
    for number in (3, 4, 5):
        mates[number].wait_recv()

    def patches(mine, theirs, slot):
        extra = (slot == 27).astype(jnp.int32)
        time, row, col = slot // 9 - extra, lax.rem(slot // 3, 3) + extra, lax.rem(slot, 3) + 3 * extra
        where = (col, pl.ds(time, FR), pl.ds(row, TH))
        chan = mine.shape[-1]
        return jnp.concatenate([mine[where].reshape(VOX, chan), theirs[where].reshape(VOX, chan)], axis=0)

    def second(pair, carry):
        halves = []
        for which in range(2):
            slot = jnp.minimum(core * SLOTS + pair * 2 + which, 26)
            data = patches(s.shift1, s.mate1, slot)
            halves.append(lax.dot_general(s.grads[1], data, NN, preferred_element_type=F32).T)
        at = pl.multiple_of(START[2] + pair * (3 * C_MID), 16)
        s.flat[pl.ds(at, C_MID), :] = halves[0][:, 0:128]
        s.flat[pl.ds(at + C_MID, C_MID), :] = halves[1][:, 0:128]
        s.flat[pl.ds(rest_at(pair), C_MID), :] = jnp.concatenate([halves[0][:, 128:], halves[1][:, 128:]], axis=1)
        return carry

    lax.fori_loop(0, 3, second, 0)
    halo2.arrived(0)
    lax.fori_loop(3, SLOTS // 2, second, 0)
    groups[2].run(0)
    halo2.shift(0, s.shift2, 0)
    convolve(s.shift2, w2, s.back, ([(0, 2), (1, 1)], [(1, 2)]), NT, True, True)
    halo2.arrived(1)
    halo2.shift(1, s.shift2, FR)
    convolve(s.shift2, w2, s.back, ([(2, 0)], [(3, 0), (2, 1)]), NT, True, False)

    def back_first(rows, step):
        s.values1[rows, :] = silu_backward(s.pre[rows, :], s.back[rows, :])

    chunks(back_first)
    s.grads[0, :, 0:VOX] = s.values1[...].T.astype(BF16)
    mates[6].start()
    groups[2].run(1)
    small.start(2, small.finish(1))
    for number in (0, 1, 2, 6):
        mates[number].wait_recv()

    def put_slot(step, values):
        at = pl.multiple_of(step * (3 * C_MID), C_MID)
        for block in range(3):
            s.flat[pl.ds(at + block * C_MID, C_MID), :] = values[:, block * 128 : block * 128 + 128]

    def first(pair, carry):
        data = [patches(s.shift0, s.mate0, core * SLOTS + 2 * pair + which) for which in range(2)]
        data = jnp.concatenate(data, axis=1)
        both = lax.dot_general(s.grads[0], data, NN, preferred_element_type=F32)
        put_slot(2 * pair, both[:, 0:C_IN])
        put_slot(2 * pair + 1, both[:, C_IN:])
        return carry

    def first_alone(step):
        slot = core * SLOTS + step
        data = patches(s.shift0, s.mate0, slot)
        grads = s.grads[(slot == 27).astype(jnp.int32)]
        put_slot(step, lax.dot_general(grads, data, NN, preferred_element_type=F32))

    lax.fori_loop(0, EARLY // 2, first, 0)
    groups[0].run(0)
    lax.fori_loop(EARLY // 2, SLOTS // 2 - 1, first, 0)
    first_alone(SLOTS - 2)
    first_alone(SLOTS - 1)
    groups[1].run(0)
    groups[0].run(1)
    groups[2].run(2)
    groups[1].run(1)
    small.start(3, small.finish(2))
    groups[0].run(2)
    groups[2].run(3)
    groups[1].run(2)
    groups[0].run(3)
    small_out[...] = small.finish(3)
    groups[2].run(4)
    groups[1].run(3)
    groups[0].run(4)
    groups[1].run(4)
    for halo in (halo0, halo1, halo2):
        halo.sent()
    for copy in x_copies + y_copies + mates:
        copy.wait_send()
    small.settle()
    groups[0].run(5)
    groups[2].run(5)
    groups[0].settle()
    groups[2].settle()
    groups[1].run(5)
    groups[1].settle()


def halo_scratch(number, chan, copies):
    tile = (FR, TH + 2, TW, chan) if chan % 128 == 0 else (TH + 2, TW, FR * chan)
    return [
        (f"own{number}", pltpu.VMEM(tile, BF16)),
        (f"other{number}", pltpu.VMEM(tile, BF16)),
        (f"rims{number}", pltpu.VMEM((2, 2, 3, FR * TH, chan), BF16)),
        (f"edges{number}", pltpu.VMEM((2, FR * TH, chan), BF16)),
        (f"shift{number}", pltpu.VMEM((copies, 2 * FR, TH + 2, TW, chan), BF16)),
        (f"send{number}", pltpu.SemaphoreType.DMA((12,))),
        (f"recv{number}", pltpu.SemaphoreType.DMA((12,))),
    ]


SCRATCH = (
    halo_scratch(0, C_IN, 4)
    + halo_scratch(1, C_MID, 3)
    + halo_scratch(2, C_MID, 3)
    + [
        ("w1", pltpu.VMEM((27, C_MID, C_IN), BF16)),
        ("w2", pltpu.VMEM((27, C_MID, C_MID), BF16)),
        ("load", pltpu.SemaphoreType.DMA((2,))),
        ("lines0", pltpu.VMEM((2, FR, 16, C_IN), F32)),
        ("lines1", pltpu.VMEM((2, FR, 16, C_MID), F32)),
        ("columns", pltpu.VMEM((2, FR * TH, C_IN), F32)),
        ("values1", pltpu.VMEM((VOX, C_MID), F32)),
        ("pre", pltpu.VMEM((VOX, C_MID), F32)),
        ("block", pltpu.VMEM((VOX, C_MID), F32)),
        ("back", pltpu.VMEM((VOX, C_MID), F32)),
        ("grads", pltpu.VMEM((2, C_MID, 2 * VOX), BF16)),
        ("mate0", pltpu.VMEM((4, 2 * FR, TH + 2, TW, C_IN), BF16)),
        ("mate1", pltpu.VMEM((3, 2 * FR, TH + 2, TW, C_MID), BF16)),
        ("mate_send", pltpu.SemaphoreType.DMA((7,))),
        ("mate_recv", pltpu.SemaphoreType.DMA((7,))),
        ("flat", pltpu.VMEM((LINES, 128), F32)),
        ("stage0", pltpu.VMEM((GROUPS, PARTS, 3, max(LARGE), 128), BF16)),
        ("inbox0", pltpu.VMEM((GROUPS, PARTS, 3, max(LARGE), 128), BF16)),
        ("sum1", pltpu.VMEM((GROUPS, PARTS, max(LARGE), 128), F32)),
        ("inbox1", pltpu.VMEM((GROUPS, PARTS, 3, max(SMALL), 128), F32)),
        ("last", pltpu.VMEM((GROUPS, PARTS, 4, max(SMALL), 128), F32)),
        ("ring_send", pltpu.SemaphoreType.DMA((GROUPS * PARTS * 15,))),
        ("ring_recv", pltpu.SemaphoreType.DMA((GROUPS * PARTS * 15,))),
        ("share_send", pltpu.SemaphoreType.DMA((GROUPS * PARTS * 4,))),
        ("share_recv", pltpu.SemaphoreType.DMA((GROUPS * PARTS * 4,))),
        ("small", pltpu.VMEM((4, 4, 8, 128), F32)),
        ("small_send", pltpu.SemaphoreType.DMA((12,))),
        ("small_recv", pltpu.SemaphoreType.DMA((12,))),
        ("headf", pltpu.VMEM((8, C_MID), F32)),
        ("spread", pltpu.VMEM((128, 128), F32)),
        ("colors", pltpu.VMEM((4, 128, 24), BF16)),
        ("image", pltpu.VMEM((6, TH, 128), F32)),
        ("target", pltpu.VMEM((6, TH, 128), F32)),
        ("x_packed", pltpu.VMEM((2, TH, 128), F32)),
        ("y_packed", pltpu.VMEM((2, TH, 128), F32)),
        ("x_field", pltpu.VMEM((3, 2, N_ROW * TH, 128), F32)),
        ("y_field", pltpu.VMEM((3, 2, N_ROW * TH, 128), F32)),
        ("across", pltpu.VMEM((128, 128), F32)),
        ("down", pltpu.VMEM((6 * WINDOW, 6 * N_ROW * TH), F32)),
        ("down_own", pltpu.VMEM((6 * TH, 6 * WINDOW), F32)),
        ("y_full", pltpu.VMEM((6 * N_ROW * TH, 128), F32)),
        ("y_blur", pltpu.VMEM((2, 6 * WINDOW, 128), F32)),
        ("send_x", pltpu.SemaphoreType.DMA((11,))),
        ("recv_x", pltpu.SemaphoreType.DMA((11,))),
        ("send_y", pltpu.SemaphoreType.DMA((11,))),
        ("recv_y", pltpu.SemaphoreType.DMA((11,))),
    ]
)
SCRATCH_NAMES = [name for name, _ in SCRATCH]


def widen(flat, small_ref, g1, gs, g2, gh, loss, wide1, wide2, sems):
    copies = []

    def one1(slot, carry):
        core, step = slot // SLOTS, lax.rem(slot, SLOTS)
        at = pl.multiple_of(step * (3 * C_MID), C_MID)
        for block in range(3):
            rows = flat[core, pl.ds(at + block * C_MID, C_MID), :]
            wide1[slot, :, block * 128 : block * 128 + 128] = rows.astype(F32)
        return carry

    def one2(pair, carry):
        core, step = pair // (SLOTS // 2), lax.rem(pair, SLOTS // 2)
        at = pl.multiple_of(START[2] + step * (3 * C_MID), 16)
        wide2[2 * pair, :, 0:128] = flat[core, pl.ds(at, C_MID), :].astype(F32)
        wide2[2 * pair + 1, :, 0:128] = flat[core, pl.ds(at + C_MID, C_MID), :].astype(F32)
        rest = flat[core, pl.ds(rest_at(step), C_MID), :].astype(F32)
        wide2[2 * pair, :, 128:] = rest[:, 0:64]
        wide2[2 * pair + 1, :, 128:] = rest[:, 64:]
        return carry

    for piece in range(7):
        lax.fori_loop(4 * piece, 4 * piece + 4, one1, 0)
        last = min(4 * piece + 4, 27)
        rows = pl.ds(4 * piece, last - 4 * piece)
        copies.append(pltpu.make_async_copy(wide1.at[rows], g1.at[rows], sems.at[len(copies)]))
        copies[-1].start()
        lax.fori_loop(2 * piece, 2 * piece + 2, one2, 0)
        copies.append(pltpu.make_async_copy(wide2.at[rows], g2.at[rows], sems.at[len(copies)]))
        copies[-1].start()
    copies.append(pltpu.make_async_copy(wide1.at[27], gs, sems.at[len(copies)]))
    copies[-1].start()
    gh[:, 0:128] = small_ref[0:3, :]
    gh[:, 128:] = small_ref[3:6, 0:64]
    loss[...] = jnp.sum(small_ref[7:8, :], axis=1, keepdims=True) / (N_TM * N_ROW * N_COL)
    for copy in copies:
        copy.wait()


def body(features, conv_first, conv_second, shortcut_weight, head_weight, target_frames):
    vmem, hbm = pl.BlockSpec(memory_space=pltpu.VMEM), pl.BlockSpec(memory_space=pl.ANY)
    flat, small = pl.pallas_call(
        kernel,
        out_shape=[pltpu.VMEM((2, LINES, 128), BF16), pltpu.VMEM((8, 128), F32)],
        in_specs=[vmem, hbm, hbm, vmem, vmem, vmem],
        out_specs=[vmem] * 2,
        scratch_shapes=[shape for _, shape in SCRATCH],
        compiler_params=pltpu.CompilerParams(
            collective_id=0, has_side_effects=True, vmem_limit_bytes=52 * 1024 * 1024
        ),
    )(
        features,
        conv_first.transpose(0, 1, 2, 4, 3).reshape(27, C_MID, C_IN),
        conv_second.reshape(27, C_MID, C_MID),
        shortcut_weight.T,
        head_weight.T,
        target_frames.reshape(6, TH, TW),
    )
    g1, gs, g2, gh, loss = pl.pallas_call(
        widen,
        out_shape=[
            jax.ShapeDtypeStruct((27, C_MID, C_IN), F32),
            jax.ShapeDtypeStruct((C_MID, C_IN), F32),
            jax.ShapeDtypeStruct((27, C_MID, C_MID), F32),
            jax.ShapeDtypeStruct((3, C_MID), F32),
            jax.ShapeDtypeStruct((1, 1), F32),
        ],
        in_specs=[vmem] * 2,
        out_specs=[hbm] * 3 + [vmem] * 2,
        scratch_shapes=[
            pltpu.VMEM((28, C_MID, C_IN), F32),
            pltpu.VMEM((28, C_MID, C_MID), F32),
            pltpu.SemaphoreType.DMA((15,)),
        ],
        compiler_params=pltpu.CompilerParams(vmem_limit_bytes=40 * 1024 * 1024),
    )(flat, small)
    return (
        g1.reshape(3, 3, 3, C_MID, C_IN).transpose(0, 1, 2, 4, 3),
        g2.reshape(3, 3, 3, C_MID, C_MID),
        gs.T,
        gh.T,
        loss.reshape(()),
    )


def solution(mesh):
    return jax.shard_map(
        body,
        mesh=mesh,
        in_specs=(P("tm", "row", "col", None), P(), P(), P(), P(), P(None, "tm", "row", "col")),
        out_specs=(P(), P(), P(), P(), P()),
        check_vma=False,
    )
```

```python
import functools
import math
import types

import jax
import jax.numpy as jnp
from jax import lax
from jax.experimental import pallas as pl
from jax.experimental.pallas import tpu as pltpu
from jax.sharding import PartitionSpec as P

MESH = pl.DeviceIdType.MESH
F32, BF16 = jnp.float32, jnp.bfloat16
HIGH = lax.Precision.HIGHEST
LAST = BF16
EPSILON = 1e-06
HUBER_BETA = 0.05
SSIM_CONST_A = 0.0004
SSIM_CONST_B = 0.0036
N_TM, N_ROW, N_COL = 4, 4, 8
FR, TH, TW = 2, 8, 32
VOX = FR * TH * TW
C_IN, C_MID = 384, 192
PIX = 1.0 * 3 * VOX
RAW = [math.exp(-o * o / 4.5) for o in range(6)]
TAPS = [v / (RAW[0] + 2.0 * sum(RAW[1:])) for v in RAW]
NT = (((1,), (1,)), ((), ()))
NN = (((1,), (0,)), ((), ()))
TN = (((0,), (0,)), ((), ()))
PARTS, GROUPS = 3, 3
SMALL = (96, 80, 80)
LARGE = tuple(4 * size for size in SMALL)
SPAN = tuple(4 * size for size in LARGE)
AXES = ("yzx", "zxy", "xyz")
SLOTS = 14
START = (0, PARTS * SPAN[0], PARTS * (SPAN[0] + SPAN[1]))
LINES = PARTS * sum(SPAN)
FIRST_FILLED = SLOTS * 3 * C_MID
EARLY = 8
SIDES = [(-1, -1), (0, -1), (1, -1), (-1, 1), (0, 1), (1, 1)]


def band(distance, keep):
    total = jnp.zeros(distance.shape, F32)
    gap = jnp.abs(distance)
    for offset in range(6):
        total = total + jnp.where(gap == offset, TAPS[offset], 0.0)
    return jnp.where(keep, total, 0.0)


def iota(shape, dim):
    return lax.broadcasted_iota(jnp.int32, shape, dim)


def silu_forward(values):
    inverse = lax.rsqrt(jnp.mean(values * values, axis=-1, keepdims=True) + EPSILON)
    unit = values * inverse
    return unit / (1.0 + jnp.exp(-unit))


def silu_backward(values, grad):
    inverse = lax.rsqrt(jnp.mean(values * values, axis=-1, keepdims=True) + EPSILON)
    unit = values * inverse
    gate = 1.0 / (1.0 + jnp.exp(-unit))
    slope = grad * (gate * (1.0 + unit * (1.0 - gate)))
    return inverse * (slope - unit * jnp.mean(slope * unit, axis=-1, keepdims=True))


def rest_at(pair):
    last = SLOTS // 2 - 1
    at = jnp.where(pair == last, FIRST_FILLED, START[2] + pair * (3 * C_MID) + 2 * C_MID)
    return pl.multiple_of(at, 16)


def wrap(index, step, count):
    return lax.rem(index + (step + count), count)


class Halo:
    def __init__(self, place, ahead, chan, own, other, rims, edges, lines, send, recv):
        self.place, self.ahead, self.chan = place, ahead, chan
        self.packed = chan % 128 != 0
        self.tiles, self.rims, self.edges, self.lines = (own, other), rims, edges, lines
        self.send, self.recv = send, recv

    def copy(self, number, src, dst, dt, dr, dc):
        t, r, c = self.place
        return pltpu.make_async_remote_copy(
            src_ref=src,
            dst_ref=dst,
            send_sem=self.send.at[number],
            recv_sem=self.recv.at[number],
            device_id=(wrap(t, dt, N_TM), wrap(r, dr, N_ROW), wrap(c, dc, N_COL)),
            device_id_type=MESH,
        )

    def rows(self, group, at):
        tile = self.tiles[group]
        return tile.at[at] if self.packed else tile.at[:, at]

    def near(self):
        items = [
            self.copy(0, self.rows(0, 1), self.rows(0, TH + 1), 0, -1, 0),
            self.copy(1, self.rows(0, TH), self.rows(0, 0), 0, 1, 0),
        ]
        for number, (dr, dc) in enumerate(SIDES):
            side = 0 if dc == 1 else 1
            items.append(self.copy(2 + number, self.edges.at[1 - side], self.rims.at[0, side, 1 - dr], 0, dr, dc))
        return items

    def far_rows(self, number, at):
        return self.copy(number, self.rows(0, at), self.rows(1, at), self.ahead, 0, 0)

    def far_tile(self):
        return self.far_rows(8, pl.ds(1, TH))

    def far_rim(self):
        rims = self.copy(9, self.rims.at[0], self.rims.at[1], self.ahead, 0, 0)
        return [rims, self.far_rows(10, 0), self.far_rows(11, TH + 1)]

    def start(self, edges_ref):
        self.far_tile().start()
        self.edges[...] = edges_ref[:, :, 0 : self.chan].astype(BF16)
        for copy in self.near():
            copy.start()

    def arrived(self, group):
        for copy in self.near() if group == 0 else [self.far_tile()] + self.far_rim():
            copy.wait_recv()
        if group == 0:
            for copy in self.far_rim():
                copy.start()

    def sent(self):
        for copy in self.near() + [self.far_tile()] + self.far_rim():
            copy.wait_send()

    def shift(self, group, shifted, frame_at):
        t, r, c = self.place
        tile, lines, chan = self.tiles[group], self.lines, self.chan
        for side in (0, 1):
            for frame in range(FR):
                at = slice(frame * TH, frame * TH + TH)
                middle = self.rims[group, side, 1].astype(F32)
                lines[side, frame, 1 : TH + 1] = middle[at]
                lines[side, frame, 0:1] = self.rims[group, side, 0].astype(F32)[frame * TH + TH - 1 : frame * TH + TH]
                lines[side, frame, TH + 1 : TH + 2] = self.rims[group, side, 2].astype(F32)[frame * TH : frame * TH + 1]
        edge_t = jnp.where(self.ahead == 1, t == 0, t == N_TM - 1)
        live = 1.0 if group == 0 else jnp.where(edge_t, 0.0, 1.0)
        top = jnp.where(r == 0, 0.0, 1.0)
        bottom = jnp.where(r == N_ROW - 1, 0.0, 1.0)
        left = jnp.where(c == 0, 0.0, 1.0)
        right = jnp.where(c == N_COL - 1, 0.0, 1.0)
        column = iota((TW, chan), 0)
        for frame in range(FR):

            def one(row, carry, frame=frame):
                scale = live * jnp.where(row == 0, top, jnp.where(row == TH + 1, bottom, 1.0))
                if self.packed:
                    base = tile[row].astype(F32)[:, frame * chan : (frame + 1) * chan] * scale
                else:
                    base = tile[frame, row].astype(F32) * scale
                first = lines[0, frame, pl.ds(row, 1), :] * (scale * left)
                last = lines[1, frame, pl.ds(row, 1), :] * (scale * right)
                before, after = pltpu.roll(base, 1, 0), pltpu.roll(base, TW - 1, 0)
                shifted[0, frame_at + frame, row] = jnp.where(column == 0, first, before).astype(BF16)
                shifted[1, frame_at + frame, row] = base.astype(BF16)
                shifted[2, frame_at + frame, row] = jnp.where(column == TW - 1, last, after).astype(BF16)
                return carry

            lax.fori_loop(0, TH + 2, one, 0)


def convolve(shifted, weights, total, sources, dims, flip, first):
    half, chan = VOX // FR, shifted.shape[-1]
    joined = chan % 128 == 0

    def one(row, carry):
        def tap(time, col):
            if flip:
                return weights[(time * 3 + 2 - row) * 3 + 2 - col]
            return weights[(time * 3 + row) * 3 + col]

        def data(frame, col):
            return shifted[col, frame, pl.ds(row, TH)].reshape(half, chan)

        for out in range(FR):
            terms = [(frame, time, col) for frame, time in sources[out] for col in range(3)]
            if not terms:
                continue
            if joined:
                values = jnp.concatenate([data(frame, col) for frame, _, col in terms], axis=1)
                taps = jnp.concatenate([tap(time, col) for _, time, col in terms], axis=dims[0][1][0])
                result = lax.dot_general(values, taps, dims, preferred_element_type=F32)
            else:
                result = None
                for frame, time, col in terms:
                    term = lax.dot_general(data(frame, col), tap(time, col), dims, preferred_element_type=F32)
                    result = term if result is None else result + term
            total[out * half : (out + 1) * half, :] += result
        return carry

    if first:
        total[...] = jnp.zeros(total.shape, F32)
    lax.fori_loop(0, 3, one, 0)


CHUNK = 128


def chunks(body):
    for step in range(VOX // CHUNK):
        body(slice(step * CHUNK, (step + 1) * CHUNK), step)


def put_tile(tile, edges, step, values):
    rows = CHUNK // TW
    chan = values.shape[-1]
    for at in range(rows):
        line = step * rows + at
        edges[0, line : line + 1, 0:chan] = values[at * TW : at * TW + 1]
        edges[1, line : line + 1, 0:chan] = values[at * TW + TW - 1 : at * TW + TW]
    frame, row = divmod(step * rows, TH)
    values = values.astype(BF16).reshape(rows, TW, chan)
    if len(tile.shape) == 3:
        tile[row + 1 : row + 1 + rows, :, frame * chan : (frame + 1) * chan] = values
    else:
        tile[frame, row + 1 : row + 1 + rows] = values


def picture_copies(place, tile, field, send, recv):
    t, r, c = place
    items = []
    number = 0
    for dr in range(N_ROW):
        for dc in (-1, 0, 1):
            if dr == 0 and dc == 0:
                continue
            items.append(
                pltpu.make_async_remote_copy(
                    src_ref=tile,
                    dst_ref=field.at[1 - dc, :, pl.ds(pl.multiple_of(r * TH, TH), TH), :],
                    send_sem=send.at[number],
                    recv_sem=recv.at[number],
                    device_id=(t, wrap(r, dr, N_ROW), wrap(c, dc, N_COL)),
                    device_id_type=MESH,
                )
            )
            number += 1
    return items


def pack_pictures(tile, packed):
    for group in range(2):
        total = tile[4 * group]
        for number in range(4 * group + 1, min(4 * group + 4, 6)):
            total = total + pltpu.roll(tile[number], TW * (number % 4), 1)
        packed[group] = total


def canvas(place, packed, field):
    t, r, c = place
    field[1, :, pl.ds(pl.multiple_of(r * TH, TH), TH), :] = packed[...]
    lane = iota((N_ROW * TH, 128), 1)
    low = jnp.where(c == 0, TW, 0)
    high = jnp.where(c == N_COL - 1, 2 * TW, 3 * TW)
    pictures = []
    for number in range(6):
        group, place_in = divmod(number, 4)
        total = jnp.zeros((N_ROW * TH, 128), F32)
        for side in range(3):
            turn = (TW * (side - place_in)) % 128
            moved = pltpu.roll(field[side, group], turn, 1) if turn else field[side, group]
            total = jnp.where((lane >= TW * side) & (lane < TW * side + TW), moved, total)
        pictures.append(jnp.where((lane >= low) & (lane < high), total, 0.0))
    return jnp.concatenate(pictures, axis=0)


def high_dot(a, b):
    return jnp.dot(a, b, precision=HIGH, preferred_element_type=F32)


def thirds(values):
    high = values.astype(BF16).astype(F32)
    rest = values - high
    middle = rest.astype(BF16).astype(F32)
    return jnp.concatenate([high, middle, rest - middle], axis=0)


WINDOW = TH + 16


def picture_bands(place, across, down, down_own):
    across[...] = band(iota((128, 128), 0) - iota((128, 128), 1), True)
    out, source = iota(down.shape, 0), iota(down.shape, 1)
    picture = sum((out >= WINDOW * at).astype(jnp.int32) for at in range(1, 6))
    line = out - WINDOW * picture + (place[1] * TH - 8)
    down[...] = band(line - (source & 31), (picture == (source >> 5)) & (line >= 0) & (line < N_ROW * TH))
    out, source = iota(down_own.shape, 0), iota(down_own.shape, 1)
    picture = sum((source >= WINDOW * at).astype(jnp.int32) for at in range(1, 6))
    down_own[...] = band((out & 7) + 8 - (source - WINDOW * picture), (out >> 3) == picture)


def blurred(maps, across, down):
    rows = maps[0].shape[0]
    wide = high_dot(jnp.concatenate(maps, axis=0), across[...])
    wide = jnp.concatenate([wide[m * rows : (m + 1) * rows] for m in range(len(maps))], axis=1)
    result = high_dot(down[...], wide)
    return [result[:, m * 128 : (m + 1) * 128] for m in range(len(maps))]


def picture_loss(place, x_tile, y_tile, x_packed, x_field, y, mean_y, square_y, bands, spread):
    t, r, c = place
    across, down, down_own = bands
    x = canvas(place, x_packed, x_field)
    mean_x, square_x, cross = blurred([x, x * x, x * y], across, down)
    rows = 6 * WINDOW
    var_x = square_x - mean_x * mean_x
    var_y = square_y - mean_y * mean_y
    covar = cross - mean_x * mean_y
    numer_a = 2.0 * mean_x * mean_y + SSIM_CONST_A
    numer_b = 2.0 * covar + SSIM_CONST_B
    denom_a = mean_x * mean_x + mean_y * mean_y + SSIM_CONST_A
    denom_b = var_x + var_y + SSIM_CONST_B
    denom_all = denom_a * denom_b
    ssim = numer_a * numer_b / denom_all
    slope_mean = (2.0 * mean_y * numer_b - 2.0 * mean_y * numer_a) / denom_all - ssim * (
        2.0 * mean_x / denom_a - 2.0 * mean_x / denom_b
    )
    slope_square = -ssim / denom_b
    slope_cross = 2.0 * numer_a / denom_all
    lane, line = iota((rows, 128), 1), iota((rows, 128), 0)
    line = line - WINDOW * sum((line >= WINDOW * at).astype(jnp.int32) for at in range(1, 6)) + (r * TH - 8)
    low = jnp.where(c == 0, TW, TW - 5)
    high = jnp.where(c == N_COL - 1, 2 * TW, 2 * TW + 5)
    inside = (lane >= low) & (lane < high) & (line >= 0) & (line < N_ROW * TH)
    mine = (lane >= TW) & (lane < 2 * TW) & (line >= r * TH) & (line < r * TH + TH)
    loss = jnp.sum(jnp.where(mine, 1.0 - ssim, 0.0), axis=0, keepdims=True)
    adjoint = [jnp.where(inside, slope * (-1.0 / PIX), 0.0) for slope in (slope_mean, slope_square, slope_cross)]
    pulled = blurred(adjoint, across, down_own)
    x_own = pltpu.roll(x_tile[...].reshape(48, 128), TW, 1)
    y_own = pltpu.roll(y_tile[...].reshape(48, 128), TW, 1)
    lane = iota((48, 128), 1)
    mine = (lane >= TW) & (lane < 2 * TW)
    diff = x_own - y_own
    size = jnp.abs(diff)
    huber = jnp.where(size < HUBER_BETA, 0.5 * diff * diff / HUBER_BETA, size - 0.5 * HUBER_BETA)
    loss = (loss + jnp.sum(jnp.where(mine, huber, 0.0), axis=0, keepdims=True)) / PIX
    grad = jnp.clip(diff / HUBER_BETA, -1.0, 1.0) / PIX + pulled[0] + 2.0 * x_own * pulled[1] + y_own * pulled[2]
    grad = pltpu.roll(jnp.where(mine, grad, 0.0), 128 - TW, 1)
    spread[...] = jnp.zeros(spread.shape, F32)
    for color in range(3):
        for frame in range(FR):
            at = (color * FR + frame) * TH
            spread[pl.ds(frame * 64 + color, TH, stride=8), :] = grad[at : at + TH]
    return loss


def axis_line(place, axis):
    t, r, c = place
    if axis == "z":
        return t, lambda step: (wrap(t, step, N_TM), r, c)
    if axis == "y":
        return r, lambda step: (t, wrap(r, step, N_ROW), c)
    return c >> 1, lambda step: (t, r, wrap(c, 2 * step, N_COL))


class Reduce:
    def __init__(self, s, place, group, result):
        self.s, self.group, self.result = s, group, result
        self.small, self.large = SMALL[group], LARGE[group]
        self.core = place[2] & 1
        self.mate = (place[0], place[1], place[2] + 1 - 2 * self.core)
        self.lines = [[axis_line(place, axis) for axis in AXES[part]] for part in range(PARTS)]

    def at(self, part, phase, step=0):
        return lax.rem(self.lines[part][phase][0] + (step + 4), 4)

    def copy(self, part, phase, stage, step, src, dst):
        sem = ((self.group * PARTS + part) * 5 + stage) * 3 + step - 1
        return pltpu.make_async_remote_copy(
            src_ref=src,
            dst_ref=dst,
            send_sem=self.s.ring_send.at[sem],
            recv_sem=self.s.ring_recv.at[sem],
            device_id=self.lines[part][phase][1](step),
            device_id_type=MESH,
        )

    def base(self, part):
        return START[self.group] + part * SPAN[self.group]

    def lines_of(self, part, step):
        return pl.ds(pl.multiple_of(self.base(part) + self.at(part, 0, step) * self.large, 16), self.large)

    def region(self, part, large, small=None, core=None):
        core = self.core if core is None else core
        base = self.base(part) + self.at(part, 0, large) * self.large
        if small is None:
            return self.result.at[core, pl.ds(pl.multiple_of(base, 16), self.large), :]
        base = base + self.at(part, 1, small) * self.small
        return self.result.at[core, pl.ds(pl.multiple_of(base, 16), self.small), :]

    def send(self, part, stage, step):
        s, group = self.s, self.group
        if stage == 0:
            where = (group, part, step - 1, pl.ds(0, self.large))
            return self.copy(part, 0, 0, step, s.stage0.at[where], s.inbox0.at[where])
        if stage == 1:
            where = (group, part, step - 1, pl.ds(0, self.small))
            return self.copy(part, 1, 1, step, s.stage1.at[where], s.inbox1.at[where])
        if stage == 2:
            block = s.last.at[group, part, self.at(part, 2), pl.ds(0, self.small)]
            return self.copy(part, 2, 2, step, block, block)
        block = self.region(part, 0, 0) if stage == 3 else self.region(part, 0)
        return self.copy(part, 1 if stage == 3 else 0, stage, step, block, block)

    def arrival(self, part, stage, step):
        if stage < 2:
            return self.send(part, stage, step)
        if stage == 2:
            block = self.s.last.at[self.group, part, self.at(part, 2, -step), pl.ds(0, self.small)]
            return self.copy(part, 2, 2, step, block, block)
        block = self.region(part, 0, -step) if stage == 3 else self.region(part, -step)
        return self.copy(part, 1 if stage == 3 else 0, stage, step, block, block)

    def share(self, part, large, arriving=False):
        block = self.region(part, large, core=1 - self.core if arriving else None)
        sem = (self.group * PARTS + part) * 4 + (large + 4) % 4
        return pltpu.make_async_remote_copy(
            src_ref=block,
            dst_ref=block,
            send_sem=self.s.share_send.at[sem],
            recv_sem=self.s.share_recv.at[sem],
            device_id=self.mate,
            device_id_type=MESH,
        )

    def run(self, stage):
        s, group = self.s, self.group
        if stage == 5:
            for earlier in range(4):
                self.left(earlier)
        for part in range(PARTS):
            if stage > 0:
                for step in (1, 3, 2):
                    self.arrival(part, stage - 1, step).wait_recv()
                    if stage == 5:
                        self.share(part, -step).start()
            large, small = pl.ds(0, self.large), pl.ds(0, self.small)
            if stage == 0:
                for step in (2, 1, 3):
                    s.stage0[group, part, step - 1, large, :] = s.flat[self.lines_of(part, step), :].astype(BF16)
                    self.send(part, 0, step).start()
            elif stage == 1:
                total = [s.inbox0[group, part, index, large, :].astype(F32) for index in range(3)]
                s.sum1[group, part, large, :] = s.flat[self.lines_of(part, 0), :] + (total[0] + total[1] + total[2])
                for step in (2, 1, 3):
                    at = pl.ds(pl.multiple_of(self.at(part, 1, step) * self.small, 16), self.small)
                    s.stage1[group, part, step - 1, small, :] = s.sum1[group, part, at, :].astype(BF16)
            elif stage == 2:
                own = s.sum1[group, part, pl.ds(pl.multiple_of(self.at(part, 1) * self.small, 16), self.small), :]
                total = [s.inbox1[group, part, index, small, :].astype(F32) for index in range(3)]
                s.last[group, part, self.at(part, 2), small, :] = (own + (total[0] + total[1] + total[2])).astype(LAST)
            elif stage == 3:
                total = [s.last[group, part, index, small, :].astype(F32) for index in range(4)]
                self.region(part, 0, 0)[...] = ((total[0] + total[1]) + (total[2] + total[3])).astype(BF16)
            if 0 < stage < 5:
                for step in (2, 1, 3):
                    self.send(part, stage, step).start()
            if stage == 4:
                self.share(part, 0).start()

    def left(self, stage):
        for part in range(PARTS):
            for step in (1, 2, 3):
                self.send(part, stage, step).wait_send()

    def settle(self):
        self.left(4)
        for part in range(PARTS):
            for large in range(4):
                self.share(part, large, True).wait_recv()
            for large in range(4):
                self.share(part, large).wait_send()


class Small:
    def __init__(self, s, place):
        self.s = s
        core = place[2] & 1
        self.lines = [axis_line(place, axis) for axis in "zyx"]
        self.lines.append((core, lambda step: (place[0], place[1], place[2] + 1 - 2 * core)))

    def copies(self, stage):
        at, there = self.lines[stage]
        mine = self.s.small.at[stage, at]
        return [
            pltpu.make_async_remote_copy(
                src_ref=mine,
                dst_ref=mine,
                send_sem=self.s.small_send.at[stage * 3 + step - 1],
                recv_sem=self.s.small_recv.at[stage * 3 + step - 1],
                device_id=there(step),
                device_id_type=MESH,
            )
            for step in ((1, 2, 3) if stage < 3 else (1,))
        ]

    def start(self, stage, value):
        self.s.small[stage, self.lines[stage][0]] = value
        for copy in self.copies(stage):
            copy.start()

    def finish(self, stage):
        at, there = self.lines[stage]
        count = 4 if stage < 3 else 2
        for step in range(1, count):
            block = self.s.small.at[stage, lax.rem(at + (count - step), count)]
            pltpu.make_async_remote_copy(
                src_ref=block,
                dst_ref=block,
                send_sem=self.s.small_send.at[stage * 3 + step - 1],
                recv_sem=self.s.small_recv.at[stage * 3 + step - 1],
                device_id=there(step),
                device_id_type=MESH,
            ).wait_recv()
        value = self.s.small[stage, 0]
        for index in range(1, count):
            value = value + self.s.small[stage, index]
        return value

    def settle(self):
        for stage in range(4):
            for copy in self.copies(stage):
                copy.wait_send()


def kernel(feat_hbm, w1_hbm, w2_hbm, ws_hbm, head, targ, result, small_out, *scratch):
    s = types.SimpleNamespace(**dict(zip(SCRATCH_NAMES, scratch)))
    t, r, c = lax.axis_index("tm"), lax.axis_index("row"), lax.axis_index("col")
    place = (t, r, c)

    feat, w1, w2, ws = s.feat, s.w1, s.w2, s.ws
    loads = [
        pltpu.make_async_copy(w1_hbm, w1, s.load.at[0]),
        pltpu.make_async_copy(w2_hbm, w2, s.load.at[1]),
        pltpu.make_async_copy(feat_hbm, feat, s.load.at[2]),
        pltpu.make_async_copy(ws_hbm, ws, s.load.at[3]),
    ]
    loads[2].start()
    barrier = pltpu.get_barrier_semaphore()
    around = [(0, dr, dc) for dr in (-1, 0, 1, 2) for dc in (-1, 0, 1) if (dr, dc) != (0, 0)]
    around += [(-1, 0, 0), (1, 0, 0), (2, 0, 0), (0, 0, -2), (0, 0, 2), (0, 0, 4)]
    for dt, dr, dc in around:
        pl.semaphore_signal(
            barrier,
            inc=1,
            device_id=(wrap(t, dt, N_TM), wrap(r, dr, N_ROW), wrap(c, dc, N_COL)),
            device_id_type=MESH,
        )

    core = c & 1
    mate = (t, r, c + 1 - 2 * core)

    def to_mate(number, src, dst):
        return pltpu.make_async_remote_copy(
            src_ref=src,
            dst_ref=dst,
            send_sem=s.mate_send.at[number],
            recv_sem=s.mate_recv.at[number],
            device_id=mate,
            device_id_type=MESH,
        )

    mates = [
        to_mate(0, feat, s.mate0.at[3, pl.ds(FR, FR), pl.ds(1, TH)]),
        to_mate(1, s.shift0.at[pl.ds(0, 3), pl.ds(FR, FR)], s.mate0.at[pl.ds(0, 3), pl.ds(FR, FR)]),
        to_mate(2, s.shift0.at[pl.ds(0, 3), pl.ds(0, FR)], s.mate0.at[pl.ds(0, 3), pl.ds(0, FR)]),
        to_mate(3, s.shift1.at[:, pl.ds(FR, FR)], s.mate1.at[:, pl.ds(FR, FR)]),
        to_mate(4, s.shift1.at[:, pl.ds(0, FR)], s.mate1.at[:, pl.ds(0, FR)]),
        to_mate(5, s.grads.at[1, :, pl.ds(0, VOX)], s.grads.at[1, :, pl.ds(VOX, VOX)]),
        to_mate(6, s.grads.at[0, :, pl.ds(0, VOX)], s.grads.at[0, :, pl.ds(VOX, VOX)]),
    ]

    def tile_rows(step):
        return divmod(step * (CHUNK // TW), TH)

    def features(step):
        frame, row = tile_rows(step)
        return feat[frame, pl.ds(row, CHUNK // TW)].reshape(CHUNK, C_IN)

    for number in (0, 1, 3):
        loads[number].start()
    loads[2].wait()

    def act(rows, step):
        raw = features(step)
        frame, row = tile_rows(step)
        s.shift0[3, FR + frame, pl.ds(row + 1, CHUNK // TW)] = raw.reshape(CHUNK // TW, TW, C_IN)
        values = silu_forward(raw.astype(F32))
        put_tile(s.own0, s.columns, step, values)

    chunks(act)
    s.target[...] = jnp.zeros(s.target.shape, F32)
    s.target[:, :, 0:TW] = targ[...]
    pack_pictures(s.target, s.y_packed)
    pl.semaphore_wait(barrier, len(around))

    halo0 = Halo(place, 1, C_IN, s.own0, s.other0, s.rims0, s.edges0, s.lines0, s.send0, s.recv0)
    halo1 = Halo(place, 1, C_MID, s.own1, s.other1, s.rims1, s.edges1, s.lines1, s.send1, s.recv1)
    halo2 = Halo(place, -1, C_MID, s.own2, s.other2, s.rims2, s.edges2, s.lines1, s.send2, s.recv2)
    halo0.start(s.columns)
    y_copies = picture_copies(place, s.y_packed, s.y_field, s.send_y, s.recv_y)
    for copy in y_copies:
        copy.start()
    bands = (s.across, s.down, s.down_own)
    picture_bands(place, *bands)

    halo0.arrived(0)
    halo0.shift(0, s.shift0, FR)
    loads[0].wait()
    convolve(s.shift0, w1, s.pre, ([(2, 2)], [(3, 2), (2, 1)]), NT, False, True)
    halo0.arrived(1)
    halo0.shift(1, s.shift0, 0)
    convolve(s.shift0, w1, s.pre, ([(0, 0), (1, 1)], [(1, 0)]), NT, False, False)

    def act_first(rows, step):
        values = silu_forward(s.pre[rows, :])
        put_tile(s.own1, s.columns, step, values)

    chunks(act_first)
    halo1.start(s.columns)
    for number in (0, 1, 2):
        mates[number].start()
    for copy in y_copies:
        copy.wait_recv()
    s.y_full[...] = canvas(place, s.y_packed, s.y_field)
    s.y_blur[0], s.y_blur[1] = blurred([s.y_full[...], s.y_full[...] * s.y_full[...]], s.across, s.down)
    halo1.arrived(0)
    halo1.shift(0, s.shift1, FR)
    loads[1].wait()
    loads[3].wait()
    convolve(s.shift1, w2, s.block, ([(2, 2)], [(3, 2), (2, 1)]), NN, False, True)

    def shortcut(rows, step):
        s.block[rows, :] += lax.dot_general(features(step), ws[...], NT, preferred_element_type=F32)

    chunks(shortcut)
    halo1.arrived(1)
    halo1.shift(1, s.shift1, 0)
    convolve(s.shift1, w2, s.block, ([(0, 0), (1, 1)], [(1, 0)]), NN, False, False)

    s.headf[...] = jnp.zeros(s.headf.shape, F32)
    s.headf[0:3, :] = head[...].astype(F32)

    def act_block(rows, step):
        s.values1[rows, :] = silu_forward(s.block[rows, :]).astype(BF16).astype(F32)

    chunks(act_block)
    lane = iota((8, 128), 1)
    for part in range(4):
        rows = slice(part * 128, part * 128 + 128)
        color = lax.dot_general(
            s.headf[...].astype(BF16), s.values1[rows, :].astype(BF16), NT, preferred_element_type=F32
        )
        for piece in range(4):
            moved = color if piece == 0 else pltpu.roll(color, 128 - TW * piece, 1)
            at = (4 * part + piece) * 8
            s.spread[at : at + 8, :] = jnp.where(lane < TW, moved, 0.0)
    for color in range(3):
        for frame in range(FR):
            s.image[color * FR + frame] = s.spread[pl.ds(frame * 64 + color, TH, stride=8), :]

    pack_pictures(s.image, s.x_packed)
    x_copies = picture_copies(place, s.x_packed, s.x_field, s.send_x, s.recv_x)
    for copy in x_copies:
        copy.start()
    for number in (3, 4):
        mates[number].start()
    for copy in x_copies:
        copy.wait_recv()
    loss = picture_loss(
        place, s.image, s.target, s.x_packed, s.x_field, s.y_full[...], s.y_blur[0], s.y_blur[1], bands, s.spread
    )

    grad_head = None
    for part in range(4):
        rows = slice(part * 128, part * 128 + 128)
        color = None
        for piece in range(4):
            at = (4 * part + piece) * 8
            held = s.spread[at : at + 8, :]
            color = held if piece == 0 else color + pltpu.roll(held, TW * piece, 1)
        split = thirds(color)
        s.colors[part] = jnp.concatenate([split, jnp.zeros((128 - 24, 128), F32)], axis=0).T[:, 0:24].astype(BF16)
        term = jnp.dot(split.astype(BF16), s.values1[rows, :].astype(BF16), preferred_element_type=F32)
        grad_head = term if grad_head is None else grad_head + term
    grad_head = grad_head[0:8] + (grad_head[8:16] + grad_head[16:24])
    heads = jnp.concatenate([s.headf[...]] * 3, axis=0).astype(BF16)
    tail = jnp.concatenate([grad_head[:, 128:], jnp.zeros((8, 64), F32)], axis=1)
    small = Small(s, place)
    small.start(
        0,
        jnp.concatenate([grad_head[0:3, 0:128], tail[0:3], jnp.zeros((1, 128), F32), loss], axis=0),
    )

    def back_block(rows, step):
        grad = jnp.dot(s.colors[step], heads, preferred_element_type=F32)
        values = silu_backward(s.block[rows, :], grad)
        s.values1[rows, :] = values
        put_tile(s.own2, s.columns, step, values)

    chunks(back_block)
    halo2.start(s.columns)
    s.grads[1, :, 0:VOX] = s.values1[...].T.astype(BF16)
    mates[5].start()
    groups = [Reduce(s, place, group, result) for group in range(GROUPS)]
    s.flat[FIRST_FILLED + C_MID : START[2], :] = jnp.zeros((START[2] - FIRST_FILLED - C_MID, 128), F32)
    small.start(1, small.finish(0))
    for number in (3, 4, 5):
        mates[number].wait_recv()

    def patches(mine, theirs, slot):
        extra = (slot == 27).astype(jnp.int32)
        time, row, col = slot // 9 - extra, lax.rem(slot // 3, 3) + extra, lax.rem(slot, 3) + 3 * extra
        where = (col, pl.ds(time, FR), pl.ds(row, TH))
        chan = mine.shape[-1]
        return jnp.concatenate([mine[where].reshape(VOX, chan), theirs[where].reshape(VOX, chan)], axis=0)

    def second(pair, carry):
        halves = []
        for which in range(2):
            slot = jnp.minimum(core * SLOTS + pair * 2 + which, 26)
            data = patches(s.shift1, s.mate1, slot)
            halves.append(lax.dot_general(s.grads[1], data, NN, preferred_element_type=F32).T)
        at = pl.multiple_of(START[2] + pair * (3 * C_MID), 16)
        s.flat[pl.ds(at, C_MID), :] = halves[0][:, 0:128]
        s.flat[pl.ds(at + C_MID, C_MID), :] = halves[1][:, 0:128]
        s.flat[pl.ds(rest_at(pair), C_MID), :] = jnp.concatenate([halves[0][:, 128:], halves[1][:, 128:]], axis=1)
        return carry

    lax.fori_loop(0, 3, second, 0)
    halo2.arrived(0)
    lax.fori_loop(3, SLOTS // 2, second, 0)
    groups[2].run(0)
    halo2.shift(0, s.shift2, 0)
    convolve(s.shift2, w2, s.back, ([(0, 2), (1, 1)], [(1, 2)]), NT, True, True)
    halo2.arrived(1)
    halo2.shift(1, s.shift2, FR)
    convolve(s.shift2, w2, s.back, ([(2, 0)], [(3, 0), (2, 1)]), NT, True, False)

    def back_first(rows, step):
        s.values1[rows, :] = silu_backward(s.pre[rows, :], s.back[rows, :])

    chunks(back_first)
    s.grads[0, :, 0:VOX] = s.values1[...].T.astype(BF16)
    mates[6].start()
    groups[2].run(1)
    small.start(2, small.finish(1))
    for number in (0, 1, 2, 6):
        mates[number].wait_recv()

    def put_slot(step, values):
        at = pl.multiple_of(step * (3 * C_MID), C_MID)
        for block in range(3):
            s.flat[pl.ds(at + block * C_MID, C_MID), :] = values[:, block * 128 : block * 128 + 128]

    def first(pair, carry):
        data = [patches(s.shift0, s.mate0, core * SLOTS + 2 * pair + which) for which in range(2)]
        data = jnp.concatenate(data, axis=1)
        both = lax.dot_general(s.grads[0], data, NN, preferred_element_type=F32)
        put_slot(2 * pair, both[:, 0:C_IN])
        put_slot(2 * pair + 1, both[:, C_IN:])
        return carry

    def first_alone(step):
        slot = core * SLOTS + step
        data = patches(s.shift0, s.mate0, slot)
        grads = s.grads[(slot == 27).astype(jnp.int32)]
        put_slot(step, lax.dot_general(grads, data, NN, preferred_element_type=F32))

    lax.fori_loop(0, EARLY // 2, first, 0)
    groups[0].run(0)
    lax.fori_loop(EARLY // 2, SLOTS // 2 - 1, first, 0)
    first_alone(SLOTS - 2)
    first_alone(SLOTS - 1)
    groups[1].run(0)
    groups[0].run(1)
    groups[2].run(2)
    groups[1].run(1)
    small.start(3, small.finish(2))
    groups[0].run(2)
    groups[2].run(3)
    groups[1].run(2)
    groups[0].run(3)
    small_out[...] = small.finish(3)
    groups[2].run(4)
    groups[1].run(3)
    groups[0].run(4)
    groups[1].run(4)
    for halo in (halo0, halo1, halo2):
        halo.sent()
    for copy in x_copies + y_copies + mates:
        copy.wait_send()
    small.settle()
    groups[0].run(5)
    groups[2].run(5)
    groups[0].settle()
    groups[2].settle()
    groups[1].run(5)
    groups[1].settle()


def halo_scratch(number, chan, copies):
    tile = (FR, TH + 2, TW, chan) if chan % 128 == 0 else (TH + 2, TW, FR * chan)
    return [
        (f"own{number}", pltpu.VMEM(tile, BF16)),
        (f"other{number}", pltpu.VMEM(tile, BF16)),
        (f"rims{number}", pltpu.VMEM((2, 2, 3, FR * TH, chan), BF16)),
        (f"edges{number}", pltpu.VMEM((2, FR * TH, chan), BF16)),
        (f"shift{number}", pltpu.VMEM((copies, 2 * FR, TH + 2, TW, chan), BF16)),
        (f"send{number}", pltpu.SemaphoreType.DMA((12,))),
        (f"recv{number}", pltpu.SemaphoreType.DMA((12,))),
    ]


SCRATCH = (
    halo_scratch(0, C_IN, 4)
    + halo_scratch(1, C_MID, 3)
    + halo_scratch(2, C_MID, 3)
    + [
        ("w1", pltpu.VMEM((27, C_MID, C_IN), BF16)),
        ("w2", pltpu.VMEM((27, C_MID, C_MID), BF16)),
        ("feat", pltpu.VMEM((FR, TH, TW, C_IN), BF16)),
        ("ws", pltpu.VMEM((C_MID, C_IN), BF16)),
        ("load", pltpu.SemaphoreType.DMA((4,))),
        ("lines0", pltpu.VMEM((2, FR, 16, C_IN), F32)),
        ("lines1", pltpu.VMEM((2, FR, 16, C_MID), F32)),
        ("columns", pltpu.VMEM((2, FR * TH, C_IN), F32)),
        ("values1", pltpu.VMEM((VOX, C_MID), F32)),
        ("pre", pltpu.VMEM((VOX, C_MID), F32)),
        ("block", pltpu.VMEM((VOX, C_MID), F32)),
        ("back", pltpu.VMEM((VOX, C_MID), F32)),
        ("grads", pltpu.VMEM((2, C_MID, 2 * VOX), BF16)),
        ("mate0", pltpu.VMEM((4, 2 * FR, TH + 2, TW, C_IN), BF16)),
        ("mate1", pltpu.VMEM((3, 2 * FR, TH + 2, TW, C_MID), BF16)),
        ("mate_send", pltpu.SemaphoreType.DMA((7,))),
        ("mate_recv", pltpu.SemaphoreType.DMA((7,))),
        ("flat", pltpu.VMEM((LINES, 128), F32)),
        ("stage0", pltpu.VMEM((GROUPS, PARTS, 3, max(LARGE), 128), BF16)),
        ("inbox0", pltpu.VMEM((GROUPS, PARTS, 3, max(LARGE), 128), BF16)),
        ("sum1", pltpu.VMEM((GROUPS, PARTS, max(LARGE), 128), F32)),
        ("stage1", pltpu.VMEM((GROUPS, PARTS, 3, max(SMALL), 128), BF16)),
        ("inbox1", pltpu.VMEM((GROUPS, PARTS, 3, max(SMALL), 128), BF16)),
        ("last", pltpu.VMEM((GROUPS, PARTS, 4, max(SMALL), 128), LAST)),
        ("ring_send", pltpu.SemaphoreType.DMA((GROUPS * PARTS * 15,))),
        ("ring_recv", pltpu.SemaphoreType.DMA((GROUPS * PARTS * 15,))),
        ("share_send", pltpu.SemaphoreType.DMA((GROUPS * PARTS * 4,))),
        ("share_recv", pltpu.SemaphoreType.DMA((GROUPS * PARTS * 4,))),
        ("small", pltpu.VMEM((4, 4, 8, 128), F32)),
        ("small_send", pltpu.SemaphoreType.DMA((12,))),
        ("small_recv", pltpu.SemaphoreType.DMA((12,))),
        ("headf", pltpu.VMEM((8, C_MID), F32)),
        ("spread", pltpu.VMEM((128, 128), F32)),
        ("colors", pltpu.VMEM((4, 128, 24), BF16)),
        ("image", pltpu.VMEM((6, TH, 128), F32)),
        ("target", pltpu.VMEM((6, TH, 128), F32)),
        ("x_packed", pltpu.VMEM((2, TH, 128), F32)),
        ("y_packed", pltpu.VMEM((2, TH, 128), F32)),
        ("x_field", pltpu.VMEM((3, 2, N_ROW * TH, 128), F32)),
        ("y_field", pltpu.VMEM((3, 2, N_ROW * TH, 128), F32)),
        ("across", pltpu.VMEM((128, 128), F32)),
        ("down", pltpu.VMEM((6 * WINDOW, 6 * N_ROW * TH), F32)),
        ("down_own", pltpu.VMEM((6 * TH, 6 * WINDOW), F32)),
        ("y_full", pltpu.VMEM((6 * N_ROW * TH, 128), F32)),
        ("y_blur", pltpu.VMEM((2, 6 * WINDOW, 128), F32)),
        ("send_x", pltpu.SemaphoreType.DMA((11,))),
        ("recv_x", pltpu.SemaphoreType.DMA((11,))),
        ("send_y", pltpu.SemaphoreType.DMA((11,))),
        ("recv_y", pltpu.SemaphoreType.DMA((11,))),
    ]
)
SCRATCH_NAMES = [name for name, _ in SCRATCH]


def widen(flat, small_ref, g1, gs, g2, gh, loss, wide1, wide2, sems):
    copies = []

    def one1(slot, carry):
        core, step = slot // SLOTS, lax.rem(slot, SLOTS)
        at = pl.multiple_of(step * (3 * C_MID), C_MID)
        for block in range(3):
            rows = flat[core, pl.ds(at + block * C_MID, C_MID), :]
            wide1[slot, :, block * 128 : block * 128 + 128] = rows.astype(F32)
        return carry

    def one2(pair, carry):
        core, step = pair // (SLOTS // 2), lax.rem(pair, SLOTS // 2)
        at = pl.multiple_of(START[2] + step * (3 * C_MID), 16)
        wide2[2 * pair, :, 0:128] = flat[core, pl.ds(at, C_MID), :].astype(F32)
        wide2[2 * pair + 1, :, 0:128] = flat[core, pl.ds(at + C_MID, C_MID), :].astype(F32)
        rest = flat[core, pl.ds(rest_at(step), C_MID), :].astype(F32)
        wide2[2 * pair, :, 128:] = rest[:, 0:64]
        wide2[2 * pair + 1, :, 128:] = rest[:, 64:]
        return carry

    cuts = (0, 2, 6, 12, 18, 24, 28)
    for low, high in zip(cuts[:-1], cuts[1:]):
        rows = pl.ds(low, min(high, 27) - low)
        lax.fori_loop(low, high, one1, 0)
        copies.append(pltpu.make_async_copy(wide1.at[rows], g1.at[rows], sems.at[len(copies)]))
        copies[-1].start()
        lax.fori_loop(low // 2, high // 2, one2, 0)
        copies.append(pltpu.make_async_copy(wide2.at[rows], g2.at[rows], sems.at[len(copies)]))
        copies[-1].start()
    copies.append(pltpu.make_async_copy(wide1.at[27], gs, sems.at[len(copies)]))
    copies[-1].start()
    gh[:, 0:128] = small_ref[0:3, :]
    gh[:, 128:] = small_ref[3:6, 0:64]
    loss[...] = jnp.sum(small_ref[7:8, :], axis=1, keepdims=True) / (N_TM * N_ROW * N_COL)
    for copy in copies:
        copy.wait()


def body(features, conv_first, conv_second, shortcut_weight, head_weight, target_frames):
    vmem, hbm = pl.BlockSpec(memory_space=pltpu.VMEM), pl.BlockSpec(memory_space=pl.ANY)
    flat, small = pl.pallas_call(
        kernel,
        out_shape=[pltpu.VMEM((2, LINES, 128), BF16), pltpu.VMEM((8, 128), F32)],
        in_specs=[hbm, hbm, hbm, hbm, vmem, vmem],
        out_specs=[vmem] * 2,
        scratch_shapes=[shape for _, shape in SCRATCH],
        compiler_params=pltpu.CompilerParams(
            collective_id=0, has_side_effects=True, vmem_limit_bytes=52 * 1024 * 1024
        ),
    )(
        features,
        conv_first.transpose(0, 1, 2, 4, 3).reshape(27, C_MID, C_IN),
        conv_second.reshape(27, C_MID, C_MID),
        shortcut_weight.T,
        head_weight.T,
        target_frames.reshape(6, TH, TW),
    )
    g1, gs, g2, gh, loss = pl.pallas_call(
        widen,
        out_shape=[
            jax.ShapeDtypeStruct((27, C_MID, C_IN), F32),
            jax.ShapeDtypeStruct((C_MID, C_IN), F32),
            jax.ShapeDtypeStruct((27, C_MID, C_MID), F32),
            jax.ShapeDtypeStruct((3, C_MID), F32),
            jax.ShapeDtypeStruct((1, 1), F32),
        ],
        in_specs=[vmem] * 2,
        out_specs=[hbm] * 3 + [vmem] * 2,
        scratch_shapes=[
            pltpu.VMEM((28, C_MID, C_IN), F32),
            pltpu.VMEM((28, C_MID, C_MID), F32),
            pltpu.SemaphoreType.DMA((15,)),
        ],
        compiler_params=pltpu.CompilerParams(vmem_limit_bytes=40 * 1024 * 1024),
    )(flat, small)
    return (
        g1.reshape(3, 3, 3, C_MID, C_IN).transpose(0, 1, 2, 4, 3),
        g2.reshape(3, 3, 3, C_MID, C_MID),
        gs.T,
        gh.T,
        loss.reshape(()),
    )


def solution(mesh):
    return jax.shard_map(
        body,
        mesh=mesh,
        in_specs=(P("tm", "row", "col", None), P(), P(), P(), P(), P(None, "tm", "row", "col")),
        out_specs=(P(), P(), P(), P(), P()),
        check_vma=False,
    )
```

```python
import functools
import math
import types

import jax
import jax.numpy as jnp
from jax import lax
from jax.experimental import pallas as pl
from jax.experimental.pallas import tpu as pltpu
from jax.sharding import PartitionSpec as P

MESH = pl.DeviceIdType.MESH
F32, BF16 = jnp.float32, jnp.bfloat16
HIGH = lax.Precision.HIGHEST
LAST = BF16
EPSILON = 1e-06
HUBER_BETA = 0.05
SSIM_CONST_A = 0.0004
SSIM_CONST_B = 0.0036
N_TM, N_ROW, N_COL = 4, 4, 8
FR, TH, TW = 2, 8, 32
VOX = FR * TH * TW
C_IN, C_MID = 384, 192
PIX = 1.0 * 3 * VOX
RAW = [math.exp(-o * o / 4.5) for o in range(6)]
TAPS = [v / (RAW[0] + 2.0 * sum(RAW[1:])) for v in RAW]
NT = (((1,), (1,)), ((), ()))
NN = (((1,), (0,)), ((), ()))
TN = (((0,), (0,)), ((), ()))
PARTS, GROUPS = 3, 3
SMALL = (96, 80, 80)
LARGE = tuple(4 * size for size in SMALL)
SPAN = tuple(4 * size for size in LARGE)
AXES = ("yzx", "zxy", "xyz")
SLOTS = 14
START = (0, PARTS * SPAN[0], PARTS * (SPAN[0] + SPAN[1]))
LINES = PARTS * sum(SPAN)
FIRST_FILLED = SLOTS * 3 * C_MID
EARLY = 8
SIDES = [(-1, -1), (0, -1), (1, -1), (-1, 1), (0, 1), (1, 1)]


def band(distance, keep):
    total = jnp.zeros(distance.shape, F32)
    gap = jnp.abs(distance)
    for offset in range(6):
        total = total + jnp.where(gap == offset, TAPS[offset], 0.0)
    return jnp.where(keep, total, 0.0)


def iota(shape, dim):
    return lax.broadcasted_iota(jnp.int32, shape, dim)


def silu_forward(values):
    inverse = lax.rsqrt(jnp.mean(values * values, axis=-1, keepdims=True) + EPSILON)
    unit = values * inverse
    return unit / (1.0 + jnp.exp(-unit))


def silu_backward(values, grad):
    inverse = lax.rsqrt(jnp.mean(values * values, axis=-1, keepdims=True) + EPSILON)
    unit = values * inverse
    gate = 1.0 / (1.0 + jnp.exp(-unit))
    slope = grad * (gate * (1.0 + unit * (1.0 - gate)))
    return inverse * (slope - unit * jnp.mean(slope * unit, axis=-1, keepdims=True))


def rest_at(pair):
    last = SLOTS // 2 - 1
    at = jnp.where(pair == last, FIRST_FILLED, START[2] + pair * (3 * C_MID) + 2 * C_MID)
    return pl.multiple_of(at, 16)


def wrap(index, step, count):
    return lax.rem(index + (step + count), count)


class Halo:
    def __init__(self, place, ahead, chan, own, other, rims, edges, lines, send, recv):
        self.place, self.ahead, self.chan = place, ahead, chan
        self.packed = chan % 128 != 0
        self.tiles, self.rims, self.edges, self.lines = (own, other), rims, edges, lines
        self.send, self.recv = send, recv

    def copy(self, number, src, dst, dt, dr, dc):
        t, r, c = self.place
        return pltpu.make_async_remote_copy(
            src_ref=src,
            dst_ref=dst,
            send_sem=self.send.at[number],
            recv_sem=self.recv.at[number],
            device_id=(wrap(t, dt, N_TM), wrap(r, dr, N_ROW), wrap(c, dc, N_COL)),
            device_id_type=MESH,
        )

    def rows(self, group, at):
        tile = self.tiles[group]
        return tile.at[at] if self.packed else tile.at[:, at]

    def near(self):
        items = [
            self.copy(0, self.rows(0, 1), self.rows(0, TH + 1), 0, -1, 0),
            self.copy(1, self.rows(0, TH), self.rows(0, 0), 0, 1, 0),
        ]
        for number, (dr, dc) in enumerate(SIDES):
            side = 0 if dc == 1 else 1
            items.append(self.copy(2 + number, self.edges.at[1 - side], self.rims.at[0, side, 1 - dr], 0, dr, dc))
        return items

    def far_rows(self, number, at):
        return self.copy(number, self.rows(0, at), self.rows(1, at), self.ahead, 0, 0)

    def far_tile(self):
        return self.far_rows(8, pl.ds(1, TH))

    def far_rim(self):
        rims = self.copy(9, self.rims.at[0], self.rims.at[1], self.ahead, 0, 0)
        return [rims, self.far_rows(10, 0), self.far_rows(11, TH + 1)]

    def start(self, edges_ref):
        self.far_tile().start()
        self.edges[...] = edges_ref[:, :, 0 : self.chan].astype(BF16)
        for copy in self.near():
            copy.start()

    def arrived(self, group):
        for copy in self.near() if group == 0 else [self.far_tile()] + self.far_rim():
            copy.wait_recv()
        if group == 0:
            for copy in self.far_rim():
                copy.start()

    def sent(self):
        for copy in self.near() + [self.far_tile()] + self.far_rim():
            copy.wait_send()

    def shift(self, group, shifted, frame_at):
        t, r, c = self.place
        tile, lines, chan = self.tiles[group], self.lines, self.chan
        for side in (0, 1):
            for frame in range(FR):
                at = slice(frame * TH, frame * TH + TH)
                middle = self.rims[group, side, 1].astype(F32)
                lines[side, frame, 1 : TH + 1] = middle[at]
                lines[side, frame, 0:1] = self.rims[group, side, 0].astype(F32)[frame * TH + TH - 1 : frame * TH + TH]
                lines[side, frame, TH + 1 : TH + 2] = self.rims[group, side, 2].astype(F32)[frame * TH : frame * TH + 1]
        edge_t = jnp.where(self.ahead == 1, t == 0, t == N_TM - 1)
        live = 1.0 if group == 0 else jnp.where(edge_t, 0.0, 1.0)
        top = jnp.where(r == 0, 0.0, 1.0)
        bottom = jnp.where(r == N_ROW - 1, 0.0, 1.0)
        left = jnp.where(c == 0, 0.0, 1.0)
        right = jnp.where(c == N_COL - 1, 0.0, 1.0)
        column = iota((TW, chan), 0)
        for frame in range(FR):

            def one(row, carry, frame=frame):
                scale = live * jnp.where(row == 0, top, jnp.where(row == TH + 1, bottom, 1.0))
                if self.packed:
                    base = tile[row].astype(F32)[:, frame * chan : (frame + 1) * chan] * scale
                else:
                    base = tile[frame, row].astype(F32) * scale
                first = lines[0, frame, pl.ds(row, 1), :] * (scale * left)
                last = lines[1, frame, pl.ds(row, 1), :] * (scale * right)
                before, after = pltpu.roll(base, 1, 0), pltpu.roll(base, TW - 1, 0)
                shifted[0, frame_at + frame, row] = jnp.where(column == 0, first, before).astype(BF16)
                shifted[1, frame_at + frame, row] = base.astype(BF16)
                shifted[2, frame_at + frame, row] = jnp.where(column == TW - 1, last, after).astype(BF16)
                return carry

            lax.fori_loop(0, TH + 2, one, 0)


def convolve(shifted, weights, total, sources, dims, flip, first):
    half, chan = VOX // FR, shifted.shape[-1]
    joined = chan % 128 == 0

    def one(row, carry):
        def tap(time, col):
            if flip:
                return weights[(time * 3 + 2 - row) * 3 + 2 - col]
            return weights[(time * 3 + row) * 3 + col]

        def data(frame, col):
            return shifted[col, frame, pl.ds(row, TH)].reshape(half, chan)

        for out in range(FR):
            terms = [(frame, time, col) for frame, time in sources[out] for col in range(3)]
            if not terms:
                continue
            if joined:
                values = jnp.concatenate([data(frame, col) for frame, _, col in terms], axis=1)
                taps = jnp.concatenate([tap(time, col) for _, time, col in terms], axis=dims[0][1][0])
                result = lax.dot_general(values, taps, dims, preferred_element_type=F32)
            else:
                result = None
                for frame, time, col in terms:
                    term = lax.dot_general(data(frame, col), tap(time, col), dims, preferred_element_type=F32)
                    result = term if result is None else result + term
            total[out * half : (out + 1) * half, :] += result
        return carry

    if first:
        total[...] = jnp.zeros(total.shape, F32)
    lax.fori_loop(0, 3, one, 0)


CHUNK = 128


def chunks(body):
    for step in range(VOX // CHUNK):
        body(slice(step * CHUNK, (step + 1) * CHUNK), step)


def put_tile(tile, edges, step, values):
    rows = CHUNK // TW
    chan = values.shape[-1]
    for at in range(rows):
        line = step * rows + at
        edges[0, line : line + 1, 0:chan] = values[at * TW : at * TW + 1]
        edges[1, line : line + 1, 0:chan] = values[at * TW + TW - 1 : at * TW + TW]
    frame, row = divmod(step * rows, TH)
    values = values.astype(BF16).reshape(rows, TW, chan)
    if len(tile.shape) == 3:
        tile[row + 1 : row + 1 + rows, :, frame * chan : (frame + 1) * chan] = values
    else:
        tile[frame, row + 1 : row + 1 + rows] = values


def picture_copies(place, tile, field, send, recv):
    t, r, c = place
    items = []
    number = 0
    for dr in range(N_ROW):
        for dc in (-1, 0, 1):
            if dr == 0 and dc == 0:
                continue
            items.append(
                pltpu.make_async_remote_copy(
                    src_ref=tile,
                    dst_ref=field.at[1 - dc, :, pl.ds(pl.multiple_of(r * TH, TH), TH), :],
                    send_sem=send.at[number],
                    recv_sem=recv.at[number],
                    device_id=(t, wrap(r, dr, N_ROW), wrap(c, dc, N_COL)),
                    device_id_type=MESH,
                )
            )
            number += 1
    return items


def pack_pictures(tile, packed):
    for group in range(2):
        total = tile[4 * group]
        for number in range(4 * group + 1, min(4 * group + 4, 6)):
            total = total + pltpu.roll(tile[number], TW * (number % 4), 1)
        packed[group] = total


def canvas(place, packed, field):
    t, r, c = place
    field[1, :, pl.ds(pl.multiple_of(r * TH, TH), TH), :] = packed[...]
    lane = iota((N_ROW * TH, 128), 1)
    low = jnp.where(c == 0, TW, 0)
    high = jnp.where(c == N_COL - 1, 2 * TW, 3 * TW)
    pictures = []
    for number in range(6):
        group, place_in = divmod(number, 4)
        total = jnp.zeros((N_ROW * TH, 128), F32)
        for side in range(3):
            turn = (TW * (side - place_in)) % 128
            moved = pltpu.roll(field[side, group], turn, 1) if turn else field[side, group]
            total = jnp.where((lane >= TW * side) & (lane < TW * side + TW), moved, total)
        pictures.append(jnp.where((lane >= low) & (lane < high), total, 0.0))
    return jnp.concatenate(pictures, axis=0)


def high_dot(a, b):
    return jnp.dot(a, b, precision=HIGH, preferred_element_type=F32)


def thirds(values):
    high = values.astype(BF16).astype(F32)
    rest = values - high
    middle = rest.astype(BF16).astype(F32)
    return jnp.concatenate([high, middle, rest - middle], axis=0)


WINDOW = TH + 16


def picture_bands(place, across, down, down_own):
    across[...] = band(iota((128, 128), 0) - iota((128, 128), 1), True)
    out, source = iota(down.shape, 0), iota(down.shape, 1)
    picture = sum((out >= WINDOW * at).astype(jnp.int32) for at in range(1, 6))
    line = out - WINDOW * picture + (place[1] * TH - 8)
    down[...] = band(line - (source & 31), (picture == (source >> 5)) & (line >= 0) & (line < N_ROW * TH))
    out, source = iota(down_own.shape, 0), iota(down_own.shape, 1)
    picture = sum((source >= WINDOW * at).astype(jnp.int32) for at in range(1, 6))
    down_own[...] = band((out & 7) + 8 - (source - WINDOW * picture), (out >> 3) == picture)


def blurred(maps, across, down):
    rows = maps[0].shape[0]
    wide = high_dot(jnp.concatenate(maps, axis=0), across[...])
    wide = jnp.concatenate([wide[m * rows : (m + 1) * rows] for m in range(len(maps))], axis=1)
    result = high_dot(down[...], wide)
    return [result[:, m * 128 : (m + 1) * 128] for m in range(len(maps))]


def picture_loss(place, x_tile, y_tile, x_packed, x_field, y, mean_y, square_y, bands, spread):
    t, r, c = place
    across, down, down_own = bands
    x = canvas(place, x_packed, x_field)
    mean_x, square_x, cross = blurred([x, x * x, x * y], across, down)
    rows = 6 * WINDOW
    var_x = square_x - mean_x * mean_x
    var_y = square_y - mean_y * mean_y
    covar = cross - mean_x * mean_y
    numer_a = 2.0 * mean_x * mean_y + SSIM_CONST_A
    numer_b = 2.0 * covar + SSIM_CONST_B
    denom_a = mean_x * mean_x + mean_y * mean_y + SSIM_CONST_A
    denom_b = var_x + var_y + SSIM_CONST_B
    denom_all = denom_a * denom_b
    ssim = numer_a * numer_b / denom_all
    slope_mean = (2.0 * mean_y * numer_b - 2.0 * mean_y * numer_a) / denom_all - ssim * (
        2.0 * mean_x / denom_a - 2.0 * mean_x / denom_b
    )
    slope_square = -ssim / denom_b
    slope_cross = 2.0 * numer_a / denom_all
    lane, line = iota((rows, 128), 1), iota((rows, 128), 0)
    line = line - WINDOW * sum((line >= WINDOW * at).astype(jnp.int32) for at in range(1, 6)) + (r * TH - 8)
    low = jnp.where(c == 0, TW, TW - 5)
    high = jnp.where(c == N_COL - 1, 2 * TW, 2 * TW + 5)
    inside = (lane >= low) & (lane < high) & (line >= 0) & (line < N_ROW * TH)
    mine = (lane >= TW) & (lane < 2 * TW) & (line >= r * TH) & (line < r * TH + TH)
    loss = jnp.sum(jnp.where(mine, 1.0 - ssim, 0.0), axis=0, keepdims=True)
    adjoint = [jnp.where(inside, slope * (-1.0 / PIX), 0.0) for slope in (slope_mean, slope_square, slope_cross)]
    pulled = blurred(adjoint, across, down_own)
    x_own = pltpu.roll(x_tile[...].reshape(48, 128), TW, 1)
    y_own = pltpu.roll(y_tile[...].reshape(48, 128), TW, 1)
    lane = iota((48, 128), 1)
    mine = (lane >= TW) & (lane < 2 * TW)
    diff = x_own - y_own
    size = jnp.abs(diff)
    huber = jnp.where(size < HUBER_BETA, 0.5 * diff * diff / HUBER_BETA, size - 0.5 * HUBER_BETA)
    loss = (loss + jnp.sum(jnp.where(mine, huber, 0.0), axis=0, keepdims=True)) / PIX
    grad = jnp.clip(diff / HUBER_BETA, -1.0, 1.0) / PIX + pulled[0] + 2.0 * x_own * pulled[1] + y_own * pulled[2]
    grad = pltpu.roll(jnp.where(mine, grad, 0.0), 128 - TW, 1)
    spread[...] = jnp.zeros(spread.shape, F32)
    for color in range(3):
        for frame in range(FR):
            at = (color * FR + frame) * TH
            spread[pl.ds(frame * 64 + color, TH, stride=8), :] = grad[at : at + TH]
    return loss


def axis_line(place, axis):
    t, r, c = place
    if axis == "z":
        return t, lambda step: (wrap(t, step, N_TM), r, c)
    if axis == "y":
        return r, lambda step: (t, wrap(r, step, N_ROW), c)
    return c >> 1, lambda step: (t, r, wrap(c, 2 * step, N_COL))


class Reduce:
    def __init__(self, s, place, group, result):
        self.s, self.group, self.result = s, group, result
        self.small, self.large = SMALL[group], LARGE[group]
        self.core = place[2] & 1
        self.mate = (place[0], place[1], place[2] + 1 - 2 * self.core)
        self.lines = [[axis_line(place, axis) for axis in AXES[part]] for part in range(PARTS)]

    def at(self, part, phase, step=0):
        return lax.rem(self.lines[part][phase][0] + (step + 4), 4)

    def copy(self, part, phase, stage, step, src, dst):
        sem = ((self.group * PARTS + part) * 5 + stage) * 3 + step - 1
        return pltpu.make_async_remote_copy(
            src_ref=src,
            dst_ref=dst,
            send_sem=self.s.ring_send.at[sem],
            recv_sem=self.s.ring_recv.at[sem],
            device_id=self.lines[part][phase][1](step),
            device_id_type=MESH,
        )

    def base(self, part):
        return START[self.group] + part * SPAN[self.group]

    def lines_of(self, part, step):
        return pl.ds(pl.multiple_of(self.base(part) + self.at(part, 0, step) * self.large, 16), self.large)

    def region(self, part, large, small=None, core=None):
        core = self.core if core is None else core
        base = self.base(part) + self.at(part, 0, large) * self.large
        if small is None:
            return self.result.at[core, pl.ds(pl.multiple_of(base, 16), self.large), :]
        base = base + self.at(part, 1, small) * self.small
        return self.result.at[core, pl.ds(pl.multiple_of(base, 16), self.small), :]

    def send(self, part, stage, step):
        s, group = self.s, self.group
        if stage == 0:
            where = (group, part, step - 1, pl.ds(0, self.large))
            return self.copy(part, 0, 0, step, s.stage0.at[where], s.inbox0.at[where])
        if stage == 1:
            where = (group, part, step - 1, pl.ds(0, self.small))
            return self.copy(part, 1, 1, step, s.stage1.at[where], s.inbox1.at[where])
        if stage == 2:
            block = s.last.at[group, part, self.at(part, 2), pl.ds(0, self.small)]
            return self.copy(part, 2, 2, step, block, block)
        block = self.region(part, 0, 0) if stage == 3 else self.region(part, 0)
        return self.copy(part, 1 if stage == 3 else 0, stage, step, block, block)

    def arrival(self, part, stage, step):
        if stage < 2:
            return self.send(part, stage, step)
        if stage == 2:
            block = self.s.last.at[self.group, part, self.at(part, 2, -step), pl.ds(0, self.small)]
            return self.copy(part, 2, 2, step, block, block)
        block = self.region(part, 0, -step) if stage == 3 else self.region(part, -step)
        return self.copy(part, 1 if stage == 3 else 0, stage, step, block, block)

    def share(self, part, large, arriving=False):
        block = self.region(part, large, core=1 - self.core if arriving else None)
        sem = (self.group * PARTS + part) * 4 + (large + 4) % 4
        return pltpu.make_async_remote_copy(
            src_ref=block,
            dst_ref=block,
            send_sem=self.s.share_send.at[sem],
            recv_sem=self.s.share_recv.at[sem],
            device_id=self.mate,
            device_id_type=MESH,
        )

    def run(self, stage):
        s, group = self.s, self.group
        if stage == 5:
            for earlier in range(4):
                self.left(earlier)
        for part in range(PARTS):
            if stage > 0:
                for step in (1, 3, 2):
                    self.arrival(part, stage - 1, step).wait_recv()
                    if stage == 5:
                        self.share(part, -step).start()
            large, small = pl.ds(0, self.large), pl.ds(0, self.small)
            if stage == 0:
                for step in (2, 1, 3):
                    s.stage0[group, part, step - 1, large, :] = s.flat[self.lines_of(part, step), :].astype(BF16)
                    self.send(part, 0, step).start()
            elif stage == 1:
                total = [s.inbox0[group, part, index, large, :].astype(F32) for index in range(3)]
                s.sum1[group, part, large, :] = s.flat[self.lines_of(part, 0), :] + (total[0] + total[1] + total[2])
                for step in (2, 1, 3):
                    at = pl.ds(pl.multiple_of(self.at(part, 1, step) * self.small, 16), self.small)
                    s.stage1[group, part, step - 1, small, :] = s.sum1[group, part, at, :].astype(BF16)
            elif stage == 2:
                own = s.sum1[group, part, pl.ds(pl.multiple_of(self.at(part, 1) * self.small, 16), self.small), :]
                total = [s.inbox1[group, part, index, small, :].astype(F32) for index in range(3)]
                s.last[group, part, self.at(part, 2), small, :] = (own + (total[0] + total[1] + total[2])).astype(LAST)
            elif stage == 3:
                total = [s.last[group, part, index, small, :].astype(F32) for index in range(4)]
                self.region(part, 0, 0)[...] = ((total[0] + total[1]) + (total[2] + total[3])).astype(BF16)
            if 0 < stage < 5:
                for step in (2, 1, 3):
                    self.send(part, stage, step).start()
            if stage == 4:
                self.share(part, 0).start()

    def left(self, stage):
        for part in range(PARTS):
            for step in (1, 2, 3):
                self.send(part, stage, step).wait_send()

    def settle(self):
        self.left(4)
        for part in range(PARTS):
            for large in range(4):
                self.share(part, large, True).wait_recv()
            for large in range(4):
                self.share(part, large).wait_send()


class Small:
    def __init__(self, s, place):
        self.s = s
        core = place[2] & 1
        self.lines = [axis_line(place, axis) for axis in "zyx"]
        self.lines.append((core, lambda step: (place[0], place[1], place[2] + 1 - 2 * core)))

    def copies(self, stage):
        at, there = self.lines[stage]
        mine = self.s.small.at[stage, at]
        return [
            pltpu.make_async_remote_copy(
                src_ref=mine,
                dst_ref=mine,
                send_sem=self.s.small_send.at[stage * 3 + step - 1],
                recv_sem=self.s.small_recv.at[stage * 3 + step - 1],
                device_id=there(step),
                device_id_type=MESH,
            )
            for step in ((1, 2, 3) if stage < 3 else (1,))
        ]

    def start(self, stage, value):
        self.s.small[stage, self.lines[stage][0]] = value
        for copy in self.copies(stage):
            copy.start()

    def finish(self, stage):
        at, there = self.lines[stage]
        count = 4 if stage < 3 else 2
        for step in range(1, count):
            block = self.s.small.at[stage, lax.rem(at + (count - step), count)]
            pltpu.make_async_remote_copy(
                src_ref=block,
                dst_ref=block,
                send_sem=self.s.small_send.at[stage * 3 + step - 1],
                recv_sem=self.s.small_recv.at[stage * 3 + step - 1],
                device_id=there(step),
                device_id_type=MESH,
            ).wait_recv()
        value = self.s.small[stage, 0]
        for index in range(1, count):
            value = value + self.s.small[stage, index]
        return value

    def settle(self):
        for stage in range(4):
            for copy in self.copies(stage):
                copy.wait_send()


def kernel(feat_hbm, w1_hbm, w2_hbm, ws_hbm, head, targ, result, small_out, *scratch):
    s = types.SimpleNamespace(**dict(zip(SCRATCH_NAMES, scratch)))
    t, r, c = lax.axis_index("tm"), lax.axis_index("row"), lax.axis_index("col")
    place = (t, r, c)

    feat, w1, w2, ws = s.feat, s.w1, s.w2, s.ws
    loads = [
        pltpu.make_async_copy(w1_hbm, w1, s.load.at[0]),
        pltpu.make_async_copy(w2_hbm, w2, s.load.at[1]),
        pltpu.make_async_copy(feat_hbm, feat, s.load.at[2]),
        pltpu.make_async_copy(ws_hbm, ws, s.load.at[3]),
    ]
    loads[2].start()
    barrier = pltpu.get_barrier_semaphore()
    around = [(0, dr, dc) for dr in (-1, 0, 1, 2) for dc in (-1, 0, 1) if (dr, dc) != (0, 0)]
    around += [(-1, 0, 0), (1, 0, 0), (2, 0, 0), (0, 0, -2), (0, 0, 2), (0, 0, 4)]
    for dt, dr, dc in around:
        pl.semaphore_signal(
            barrier,
            inc=1,
            device_id=(wrap(t, dt, N_TM), wrap(r, dr, N_ROW), wrap(c, dc, N_COL)),
            device_id_type=MESH,
        )

    core = c & 1
    mate = (t, r, c + 1 - 2 * core)

    def to_mate(number, src, dst):
        return pltpu.make_async_remote_copy(
            src_ref=src,
            dst_ref=dst,
            send_sem=s.mate_send.at[number],
            recv_sem=s.mate_recv.at[number],
            device_id=mate,
            device_id_type=MESH,
        )

    mates = [
        to_mate(0, feat, s.mate0.at[3, pl.ds(FR, FR), pl.ds(1, TH)]),
        to_mate(1, s.shift0.at[pl.ds(0, 3), pl.ds(FR, FR)], s.mate0.at[pl.ds(0, 3), pl.ds(FR, FR)]),
        to_mate(2, s.shift0.at[pl.ds(0, 3), pl.ds(0, FR)], s.mate0.at[pl.ds(0, 3), pl.ds(0, FR)]),
        to_mate(3, s.shift1.at[:, pl.ds(FR, FR)], s.mate1.at[:, pl.ds(FR, FR)]),
        to_mate(4, s.shift1.at[:, pl.ds(0, FR)], s.mate1.at[:, pl.ds(0, FR)]),
        to_mate(5, s.grads.at[1, :, pl.ds(0, VOX)], s.grads.at[1, :, pl.ds(VOX, VOX)]),
        to_mate(6, s.grads.at[0, :, pl.ds(0, VOX)], s.grads.at[0, :, pl.ds(VOX, VOX)]),
    ]

    def tile_rows(step):
        return divmod(step * (CHUNK // TW), TH)

    def features(step):
        frame, row = tile_rows(step)
        return feat[frame, pl.ds(row, CHUNK // TW)].reshape(CHUNK, C_IN)

    for number in (0, 1, 3):
        loads[number].start()
    loads[2].wait()

    def act(rows, step):
        raw = features(step)
        frame, row = tile_rows(step)
        s.shift0[3, FR + frame, pl.ds(row + 1, CHUNK // TW)] = raw.reshape(CHUNK // TW, TW, C_IN)
        values = silu_forward(raw.astype(F32))
        put_tile(s.own0, s.columns, step, values)

    chunks(act)
    s.target[...] = jnp.zeros(s.target.shape, F32)
    s.target[:, :, 0:TW] = targ[...]
    pack_pictures(s.target, s.y_packed)
    pl.semaphore_wait(barrier, len(around))

    halo0 = Halo(place, 1, C_IN, s.own0, s.other0, s.rims0, s.edges0, s.lines0, s.send0, s.recv0)
    halo1 = Halo(place, 1, C_MID, s.own1, s.other1, s.rims1, s.edges1, s.lines1, s.send1, s.recv1)
    halo2 = Halo(place, -1, C_MID, s.own2, s.other2, s.rims2, s.edges2, s.lines1, s.send2, s.recv2)
    halo0.start(s.columns)
    y_copies = picture_copies(place, s.y_packed, s.y_field, s.send_y, s.recv_y)
    for copy in y_copies:
        copy.start()
    bands = (s.across, s.down, s.down_own)
    picture_bands(place, *bands)

    halo0.arrived(0)
    halo0.shift(0, s.shift0, FR)
    loads[0].wait()
    convolve(s.shift0, w1, s.pre, ([(2, 2)], [(3, 2), (2, 1)]), NT, False, True)
    halo0.arrived(1)
    halo0.shift(1, s.shift0, 0)
    convolve(s.shift0, w1, s.pre, ([(0, 0), (1, 1)], [(1, 0)]), NT, False, False)

    def act_first(rows, step):
        values = silu_forward(s.pre[rows, :])
        put_tile(s.own1, s.columns, step, values)

    chunks(act_first)
    halo1.start(s.columns)
    for number in (0, 1, 2):
        mates[number].start()
    for copy in y_copies:
        copy.wait_recv()
    s.y_full[...] = canvas(place, s.y_packed, s.y_field)
    s.y_blur[0], s.y_blur[1] = blurred([s.y_full[...], s.y_full[...] * s.y_full[...]], s.across, s.down)
    halo1.arrived(0)
    halo1.shift(0, s.shift1, FR)
    loads[1].wait()
    loads[3].wait()
    convolve(s.shift1, w2, s.block, ([(2, 2)], [(3, 2), (2, 1)]), NN, False, True)

    def shortcut(rows, step):
        s.block[rows, :] += lax.dot_general(features(step), ws[...], NT, preferred_element_type=F32)

    chunks(shortcut)
    halo1.arrived(1)
    halo1.shift(1, s.shift1, 0)
    convolve(s.shift1, w2, s.block, ([(0, 0), (1, 1)], [(1, 0)]), NN, False, False)

    s.headf[...] = jnp.zeros(s.headf.shape, F32)
    s.headf[0:3, :] = head[...].astype(F32)

    def act_block(rows, step):
        s.values1[rows, :] = silu_forward(s.block[rows, :]).astype(BF16).astype(F32)

    chunks(act_block)
    lane = iota((8, 128), 1)
    for part in range(4):
        rows = slice(part * 128, part * 128 + 128)
        color = lax.dot_general(
            s.headf[...].astype(BF16), s.values1[rows, :].astype(BF16), NT, preferred_element_type=F32
        )
        for piece in range(4):
            moved = color if piece == 0 else pltpu.roll(color, 128 - TW * piece, 1)
            at = (4 * part + piece) * 8
            s.spread[at : at + 8, :] = jnp.where(lane < TW, moved, 0.0)
    for color in range(3):
        for frame in range(FR):
            s.image[color * FR + frame] = s.spread[pl.ds(frame * 64 + color, TH, stride=8), :]

    pack_pictures(s.image, s.x_packed)
    x_copies = picture_copies(place, s.x_packed, s.x_field, s.send_x, s.recv_x)
    for copy in x_copies:
        copy.start()
    for number in (3, 4):
        mates[number].start()
    for copy in x_copies:
        copy.wait_recv()
    loss = picture_loss(
        place, s.image, s.target, s.x_packed, s.x_field, s.y_full[...], s.y_blur[0], s.y_blur[1], bands, s.spread
    )

    grad_head = None
    for part in range(4):
        rows = slice(part * 128, part * 128 + 128)
        color = None
        for piece in range(4):
            at = (4 * part + piece) * 8
            held = s.spread[at : at + 8, :]
            color = held if piece == 0 else color + pltpu.roll(held, TW * piece, 1)
        split = thirds(color)
        s.colors[part] = jnp.concatenate([split, jnp.zeros((128 - 24, 128), F32)], axis=0).T[:, 0:24].astype(BF16)
        term = jnp.dot(split.astype(BF16), s.values1[rows, :].astype(BF16), preferred_element_type=F32)
        grad_head = term if grad_head is None else grad_head + term
    grad_head = grad_head[0:8] + (grad_head[8:16] + grad_head[16:24])
    heads = jnp.concatenate([s.headf[...]] * 3, axis=0).astype(BF16)
    tail = jnp.concatenate([grad_head[:, 128:], jnp.zeros((8, 64), F32)], axis=1)
    small = Small(s, place)
    small.start(
        0,
        jnp.concatenate([grad_head[0:3, 0:128], tail[0:3], jnp.zeros((1, 128), F32), loss], axis=0),
    )

    def back_block(rows, step):
        grad = jnp.dot(s.colors[step], heads, preferred_element_type=F32)
        values = silu_backward(s.block[rows, :], grad)
        s.values1[rows, :] = values
        put_tile(s.own2, s.columns, step, values)

    chunks(back_block)
    halo2.start(s.columns)
    s.grads[1, :, 0:VOX] = s.values1[...].T.astype(BF16)
    mates[5].start()
    groups = [Reduce(s, place, group, result) for group in range(GROUPS)]
    s.flat[FIRST_FILLED + C_MID : START[2], :] = jnp.zeros((START[2] - FIRST_FILLED - C_MID, 128), F32)
    small.start(1, small.finish(0))
    for number in (3, 4, 5):
        mates[number].wait_recv()

    def patches(mine, theirs, slot):
        extra = (slot == 27).astype(jnp.int32)
        time, row, col = slot // 9 - extra, lax.rem(slot // 3, 3) + extra, lax.rem(slot, 3) + 3 * extra
        where = (col, pl.ds(time, FR), pl.ds(row, TH))
        chan = mine.shape[-1]
        return jnp.concatenate([mine[where].reshape(VOX, chan), theirs[where].reshape(VOX, chan)], axis=0)

    def second(pair, carry):
        halves = []
        for which in range(2):
            slot = jnp.minimum(core * SLOTS + pair * 2 + which, 26)
            data = patches(s.shift1, s.mate1, slot)
            halves.append(lax.dot_general(s.grads[1], data, NN, preferred_element_type=F32).T)
        at = pl.multiple_of(START[2] + pair * (3 * C_MID), 16)
        s.flat[pl.ds(at, C_MID), :] = halves[0][:, 0:128]
        s.flat[pl.ds(at + C_MID, C_MID), :] = halves[1][:, 0:128]
        s.flat[pl.ds(rest_at(pair), C_MID), :] = jnp.concatenate([halves[0][:, 128:], halves[1][:, 128:]], axis=1)
        return carry

    lax.fori_loop(0, 2, second, 0)
    halo2.arrived(0)
    lax.fori_loop(2, SLOTS // 2, second, 0)
    groups[2].run(0)
    halo2.shift(0, s.shift2, 0)
    convolve(s.shift2, w2, s.back, ([(0, 2), (1, 1)], [(1, 2)]), NT, True, True)
    halo2.arrived(1)
    halo2.shift(1, s.shift2, FR)
    convolve(s.shift2, w2, s.back, ([(2, 0)], [(3, 0), (2, 1)]), NT, True, False)

    def back_first(rows, step):
        s.values1[rows, :] = silu_backward(s.pre[rows, :], s.back[rows, :])

    chunks(back_first)
    s.grads[0, :, 0:VOX] = s.values1[...].T.astype(BF16)
    mates[6].start()
    groups[2].run(1)
    small.start(2, small.finish(1))
    for number in (0, 1, 2, 6):
        mates[number].wait_recv()

    def put_slot(step, values):
        at = pl.multiple_of(step * (3 * C_MID), C_MID)
        for block in range(3):
            s.flat[pl.ds(at + block * C_MID, C_MID), :] = values[:, block * 128 : block * 128 + 128]

    def first(pair, carry):
        data = [patches(s.shift0, s.mate0, core * SLOTS + 2 * pair + which) for which in range(2)]
        data = jnp.concatenate(data, axis=1)
        both = lax.dot_general(s.grads[0], data, NN, preferred_element_type=F32)
        put_slot(2 * pair, both[:, 0:C_IN])
        put_slot(2 * pair + 1, both[:, C_IN:])
        return carry

    def first_alone(step):
        slot = core * SLOTS + step
        data = patches(s.shift0, s.mate0, slot)
        grads = s.grads[(slot == 27).astype(jnp.int32)]
        put_slot(step, lax.dot_general(grads, data, NN, preferred_element_type=F32))

    lax.fori_loop(0, EARLY // 2, first, 0)
    groups[0].run(0)
    lax.fori_loop(EARLY // 2, SLOTS // 2 - 1, first, 0)
    first_alone(SLOTS - 2)
    first_alone(SLOTS - 1)
    groups[1].run(0)
    groups[0].run(1)
    groups[2].run(2)
    groups[1].run(1)
    small.start(3, small.finish(2))
    groups[0].run(2)
    groups[2].run(3)
    groups[1].run(2)
    groups[0].run(3)
    small_out[...] = small.finish(3)
    groups[2].run(4)
    groups[1].run(3)
    groups[0].run(4)
    groups[1].run(4)
    for halo in (halo0, halo1, halo2):
        halo.sent()
    for copy in x_copies + y_copies + mates:
        copy.wait_send()
    small.settle()
    groups[0].run(5)
    groups[2].run(5)
    groups[0].settle()
    groups[2].settle()
    groups[1].run(5)
    groups[1].settle()


def halo_scratch(number, chan, copies):
    tile = (FR, TH + 2, TW, chan) if chan % 128 == 0 else (TH + 2, TW, FR * chan)
    return [
        (f"own{number}", pltpu.VMEM(tile, BF16)),
        (f"other{number}", pltpu.VMEM(tile, BF16)),
        (f"rims{number}", pltpu.VMEM((2, 2, 3, FR * TH, chan), BF16)),
        (f"edges{number}", pltpu.VMEM((2, FR * TH, chan), BF16)),
        (f"shift{number}", pltpu.VMEM((copies, 2 * FR, TH + 2, TW, chan), BF16)),
        (f"send{number}", pltpu.SemaphoreType.DMA((12,))),
        (f"recv{number}", pltpu.SemaphoreType.DMA((12,))),
    ]


SCRATCH = (
    halo_scratch(0, C_IN, 4)
    + halo_scratch(1, C_MID, 3)
    + halo_scratch(2, C_MID, 3)
    + [
        ("w1", pltpu.VMEM((27, C_MID, C_IN), BF16)),
        ("w2", pltpu.VMEM((27, C_MID, C_MID), BF16)),
        ("feat", pltpu.VMEM((FR, TH, TW, C_IN), BF16)),
        ("ws", pltpu.VMEM((C_MID, C_IN), BF16)),
        ("load", pltpu.SemaphoreType.DMA((4,))),
        ("lines0", pltpu.VMEM((2, FR, 16, C_IN), F32)),
        ("lines1", pltpu.VMEM((2, FR, 16, C_MID), F32)),
        ("columns", pltpu.VMEM((2, FR * TH, C_IN), F32)),
        ("values1", pltpu.VMEM((VOX, C_MID), F32)),
        ("pre", pltpu.VMEM((VOX, C_MID), F32)),
        ("block", pltpu.VMEM((VOX, C_MID), F32)),
        ("back", pltpu.VMEM((VOX, C_MID), F32)),
        ("grads", pltpu.VMEM((2, C_MID, 2 * VOX), BF16)),
        ("mate0", pltpu.VMEM((4, 2 * FR, TH + 2, TW, C_IN), BF16)),
        ("mate1", pltpu.VMEM((3, 2 * FR, TH + 2, TW, C_MID), BF16)),
        ("mate_send", pltpu.SemaphoreType.DMA((7,))),
        ("mate_recv", pltpu.SemaphoreType.DMA((7,))),
        ("flat", pltpu.VMEM((LINES, 128), F32)),
        ("stage0", pltpu.VMEM((GROUPS, PARTS, 3, max(LARGE), 128), BF16)),
        ("inbox0", pltpu.VMEM((GROUPS, PARTS, 3, max(LARGE), 128), BF16)),
        ("sum1", pltpu.VMEM((GROUPS, PARTS, max(LARGE), 128), F32)),
        ("stage1", pltpu.VMEM((GROUPS, PARTS, 3, max(SMALL), 128), BF16)),
        ("inbox1", pltpu.VMEM((GROUPS, PARTS, 3, max(SMALL), 128), BF16)),
        ("last", pltpu.VMEM((GROUPS, PARTS, 4, max(SMALL), 128), LAST)),
        ("ring_send", pltpu.SemaphoreType.DMA((GROUPS * PARTS * 15,))),
        ("ring_recv", pltpu.SemaphoreType.DMA((GROUPS * PARTS * 15,))),
        ("share_send", pltpu.SemaphoreType.DMA((GROUPS * PARTS * 4,))),
        ("share_recv", pltpu.SemaphoreType.DMA((GROUPS * PARTS * 4,))),
        ("small", pltpu.VMEM((4, 4, 8, 128), F32)),
        ("small_send", pltpu.SemaphoreType.DMA((12,))),
        ("small_recv", pltpu.SemaphoreType.DMA((12,))),
        ("headf", pltpu.VMEM((8, C_MID), F32)),
        ("spread", pltpu.VMEM((128, 128), F32)),
        ("colors", pltpu.VMEM((4, 128, 24), BF16)),
        ("image", pltpu.VMEM((6, TH, 128), F32)),
        ("target", pltpu.VMEM((6, TH, 128), F32)),
        ("x_packed", pltpu.VMEM((2, TH, 128), F32)),
        ("y_packed", pltpu.VMEM((2, TH, 128), F32)),
        ("x_field", pltpu.VMEM((3, 2, N_ROW * TH, 128), F32)),
        ("y_field", pltpu.VMEM((3, 2, N_ROW * TH, 128), F32)),
        ("across", pltpu.VMEM((128, 128), F32)),
        ("down", pltpu.VMEM((6 * WINDOW, 6 * N_ROW * TH), F32)),
        ("down_own", pltpu.VMEM((6 * TH, 6 * WINDOW), F32)),
        ("y_full", pltpu.VMEM((6 * N_ROW * TH, 128), F32)),
        ("y_blur", pltpu.VMEM((2, 6 * WINDOW, 128), F32)),
        ("send_x", pltpu.SemaphoreType.DMA((11,))),
        ("recv_x", pltpu.SemaphoreType.DMA((11,))),
        ("send_y", pltpu.SemaphoreType.DMA((11,))),
        ("recv_y", pltpu.SemaphoreType.DMA((11,))),
    ]
)
SCRATCH_NAMES = [name for name, _ in SCRATCH]


def widen(flat, small_ref, g1, gs, g2, gh, loss, wide1, wide2, sems):
    copies = []

    def one1(slot, carry):
        core, step = slot // SLOTS, lax.rem(slot, SLOTS)
        at = pl.multiple_of(step * (3 * C_MID), C_MID)
        for block in range(3):
            rows = flat[core, pl.ds(at + block * C_MID, C_MID), :]
            wide1[slot, :, block * 128 : block * 128 + 128] = rows.astype(F32)
        return carry

    def one2(pair, carry):
        core, step = pair // (SLOTS // 2), lax.rem(pair, SLOTS // 2)
        at = pl.multiple_of(START[2] + step * (3 * C_MID), 16)
        wide2[2 * pair, :, 0:128] = flat[core, pl.ds(at, C_MID), :].astype(F32)
        wide2[2 * pair + 1, :, 0:128] = flat[core, pl.ds(at + C_MID, C_MID), :].astype(F32)
        rest = flat[core, pl.ds(rest_at(step), C_MID), :].astype(F32)
        wide2[2 * pair, :, 128:] = rest[:, 0:64]
        wide2[2 * pair + 1, :, 128:] = rest[:, 64:]
        return carry

    cuts = (0, 2, 6, 12, 18, 24, 28)
    for low, high in zip(cuts[:-1], cuts[1:]):
        rows = pl.ds(low, min(high, 27) - low)
        lax.fori_loop(low, high, one1, 0)
        copies.append(pltpu.make_async_copy(wide1.at[rows], g1.at[rows], sems.at[len(copies)]))
        copies[-1].start()
        lax.fori_loop(low // 2, high // 2, one2, 0)
        copies.append(pltpu.make_async_copy(wide2.at[rows], g2.at[rows], sems.at[len(copies)]))
        copies[-1].start()
    copies.append(pltpu.make_async_copy(wide1.at[27], gs, sems.at[len(copies)]))
    copies[-1].start()
    gh[:, 0:128] = small_ref[0:3, :]
    gh[:, 128:] = small_ref[3:6, 0:64]
    loss[...] = jnp.sum(small_ref[7:8, :], axis=1, keepdims=True) / (N_TM * N_ROW * N_COL)
    for copy in copies:
        copy.wait()


def body(features, conv_first, conv_second, shortcut_weight, head_weight, target_frames):
    vmem, hbm = pl.BlockSpec(memory_space=pltpu.VMEM), pl.BlockSpec(memory_space=pl.ANY)
    flat, small = pl.pallas_call(
        kernel,
        out_shape=[pltpu.VMEM((2, LINES, 128), BF16), pltpu.VMEM((8, 128), F32)],
        in_specs=[hbm, hbm, hbm, hbm, vmem, vmem],
        out_specs=[vmem] * 2,
        scratch_shapes=[shape for _, shape in SCRATCH],
        compiler_params=pltpu.CompilerParams(
            collective_id=0, has_side_effects=True, vmem_limit_bytes=52 * 1024 * 1024
        ),
    )(
        features,
        conv_first.transpose(0, 1, 2, 4, 3).reshape(27, C_MID, C_IN),
        conv_second.reshape(27, C_MID, C_MID),
        shortcut_weight.T,
        head_weight.T,
        target_frames.reshape(6, TH, TW),
    )
    g1, gs, g2, gh, loss = pl.pallas_call(
        widen,
        out_shape=[
            jax.ShapeDtypeStruct((27, C_MID, C_IN), F32),
            jax.ShapeDtypeStruct((C_MID, C_IN), F32),
            jax.ShapeDtypeStruct((27, C_MID, C_MID), F32),
            jax.ShapeDtypeStruct((3, C_MID), F32),
            jax.ShapeDtypeStruct((1, 1), F32),
        ],
        in_specs=[vmem] * 2,
        out_specs=[hbm] * 3 + [vmem] * 2,
        scratch_shapes=[
            pltpu.VMEM((28, C_MID, C_IN), F32),
            pltpu.VMEM((28, C_MID, C_MID), F32),
            pltpu.SemaphoreType.DMA((15,)),
        ],
        compiler_params=pltpu.CompilerParams(vmem_limit_bytes=40 * 1024 * 1024),
    )(flat, small)
    return (
        g1.reshape(3, 3, 3, C_MID, C_IN).transpose(0, 1, 2, 4, 3),
        g2.reshape(3, 3, 3, C_MID, C_MID),
        gs.T,
        gh.T,
        loss.reshape(()),
    )


def solution(mesh):
    return jax.shard_map(
        body,
        mesh=mesh,
        in_specs=(P("tm", "row", "col", None), P(), P(), P(), P(), P(None, "tm", "row", "col")),
        out_specs=(P(), P(), P(), P(), P()),
        check_vma=False,
    )
```

```python
import functools
import math
import types

import jax
import jax.numpy as jnp
from jax import lax
from jax.experimental import pallas as pl
from jax.experimental.pallas import tpu as pltpu
from jax.sharding import PartitionSpec as P

MESH = pl.DeviceIdType.MESH
F32, BF16 = jnp.float32, jnp.bfloat16
HIGH = lax.Precision.HIGHEST
LAST = BF16
EPSILON = 1e-06
HUBER_BETA = 0.05
SSIM_CONST_A = 0.0004
SSIM_CONST_B = 0.0036
N_TM, N_ROW, N_COL = 4, 4, 8
FR, TH, TW = 2, 8, 32
VOX = FR * TH * TW
C_IN, C_MID = 384, 192
PIX = 1.0 * 3 * VOX
RAW = [math.exp(-o * o / 4.5) for o in range(6)]
TAPS = [v / (RAW[0] + 2.0 * sum(RAW[1:])) for v in RAW]
NT = (((1,), (1,)), ((), ()))
NN = (((1,), (0,)), ((), ()))
TN = (((0,), (0,)), ((), ()))
PARTS, GROUPS = 3, 3
SMALL = (96, 80, 80)
LARGE = tuple(4 * size for size in SMALL)
SPAN = tuple(4 * size for size in LARGE)
AXES = ("yzx", "zxy", "xyz")
SLOTS = 14
START = (0, PARTS * SPAN[0], PARTS * (SPAN[0] + SPAN[1]))
LINES = PARTS * sum(SPAN)
FIRST_FILLED = SLOTS * 3 * C_MID
EARLY = 8
SIDES = [(-1, -1), (0, -1), (1, -1), (-1, 1), (0, 1), (1, 1)]


def band(distance, keep):
    total = jnp.zeros(distance.shape, F32)
    gap = jnp.abs(distance)
    for offset in range(6):
        total = total + jnp.where(gap == offset, TAPS[offset], 0.0)
    return jnp.where(keep, total, 0.0)


def iota(shape, dim):
    return lax.broadcasted_iota(jnp.int32, shape, dim)


def silu_forward(values):
    inverse = lax.rsqrt(jnp.mean(values * values, axis=-1, keepdims=True) + EPSILON)
    unit = values * inverse
    return unit / (1.0 + jnp.exp(-unit))


def silu_backward(values, grad):
    inverse = lax.rsqrt(jnp.mean(values * values, axis=-1, keepdims=True) + EPSILON)
    unit = values * inverse
    gate = 1.0 / (1.0 + jnp.exp(-unit))
    slope = grad * (gate * (1.0 + unit * (1.0 - gate)))
    return inverse * (slope - unit * jnp.mean(slope * unit, axis=-1, keepdims=True))


def rest_at(pair):
    last = SLOTS // 2 - 1
    at = jnp.where(pair == last, FIRST_FILLED, START[2] + pair * (3 * C_MID) + 2 * C_MID)
    return pl.multiple_of(at, 16)


def wrap(index, step, count):
    return lax.rem(index + (step + count), count)


class Halo:
    def __init__(self, place, ahead, chan, own, other, rims, edges, lines, send, recv):
        self.place, self.ahead, self.chan = place, ahead, chan
        self.packed = chan % 128 != 0
        self.tiles, self.rims, self.edges, self.lines = (own, other), rims, edges, lines
        self.send, self.recv = send, recv

    def copy(self, number, src, dst, dt, dr, dc):
        t, r, c = self.place
        return pltpu.make_async_remote_copy(
            src_ref=src,
            dst_ref=dst,
            send_sem=self.send.at[number],
            recv_sem=self.recv.at[number],
            device_id=(wrap(t, dt, N_TM), wrap(r, dr, N_ROW), wrap(c, dc, N_COL)),
            device_id_type=MESH,
        )

    def rows(self, group, at):
        tile = self.tiles[group]
        return tile.at[at] if self.packed else tile.at[:, at]

    def near(self):
        items = [
            self.copy(0, self.rows(0, 1), self.rows(0, TH + 1), 0, -1, 0),
            self.copy(1, self.rows(0, TH), self.rows(0, 0), 0, 1, 0),
        ]
        for number, (dr, dc) in enumerate(SIDES):
            side = 0 if dc == 1 else 1
            items.append(self.copy(2 + number, self.edges.at[1 - side], self.rims.at[0, side, 1 - dr], 0, dr, dc))
        return items

    def far_rows(self, number, at):
        return self.copy(number, self.rows(0, at), self.rows(1, at), self.ahead, 0, 0)

    def far_tile(self):
        return self.far_rows(8, pl.ds(1, TH))

    def far_rim(self):
        rims = self.copy(9, self.rims.at[0], self.rims.at[1], self.ahead, 0, 0)
        return [rims, self.far_rows(10, 0), self.far_rows(11, TH + 1)]

    def start(self, edges_ref):
        self.far_tile().start()
        self.edges[...] = edges_ref[:, :, 0 : self.chan].astype(BF16)
        for copy in self.near():
            copy.start()

    def arrived(self, group):
        for copy in self.near() if group == 0 else [self.far_tile()] + self.far_rim():
            copy.wait_recv()
        if group == 0:
            for copy in self.far_rim():
                copy.start()

    def sent(self):
        for copy in self.near() + [self.far_tile()] + self.far_rim():
            copy.wait_send()

    def shift(self, group, shifted, frame_at):
        t, r, c = self.place
        tile, lines, chan = self.tiles[group], self.lines, self.chan
        for side in (0, 1):
            for frame in range(FR):
                at = slice(frame * TH, frame * TH + TH)
                middle = self.rims[group, side, 1].astype(F32)
                lines[side, frame, 1 : TH + 1] = middle[at]
                lines[side, frame, 0:1] = self.rims[group, side, 0].astype(F32)[frame * TH + TH - 1 : frame * TH + TH]
                lines[side, frame, TH + 1 : TH + 2] = self.rims[group, side, 2].astype(F32)[frame * TH : frame * TH + 1]
        edge_t = jnp.where(self.ahead == 1, t == 0, t == N_TM - 1)
        live = 1.0 if group == 0 else jnp.where(edge_t, 0.0, 1.0)
        top = jnp.where(r == 0, 0.0, 1.0)
        bottom = jnp.where(r == N_ROW - 1, 0.0, 1.0)
        left = jnp.where(c == 0, 0.0, 1.0)
        right = jnp.where(c == N_COL - 1, 0.0, 1.0)
        column = iota((TW, chan), 0)
        for frame in range(FR):

            def one(row, carry, frame=frame):
                scale = live * jnp.where(row == 0, top, jnp.where(row == TH + 1, bottom, 1.0))
                if self.packed:
                    base = tile[row].astype(F32)[:, frame * chan : (frame + 1) * chan] * scale
                else:
                    base = tile[frame, row].astype(F32) * scale
                first = lines[0, frame, pl.ds(row, 1), :] * (scale * left)
                last = lines[1, frame, pl.ds(row, 1), :] * (scale * right)
                before, after = pltpu.roll(base, 1, 0), pltpu.roll(base, TW - 1, 0)
                shifted[0, frame_at + frame, row] = jnp.where(column == 0, first, before).astype(BF16)
                shifted[1, frame_at + frame, row] = base.astype(BF16)
                shifted[2, frame_at + frame, row] = jnp.where(column == TW - 1, last, after).astype(BF16)
                return carry

            lax.fori_loop(0, TH + 2, one, 0)


def convolve(shifted, weights, total, sources, dims, flip, first):
    half, chan = VOX // FR, shifted.shape[-1]
    joined = chan % 128 == 0

    def one(row, carry):
        def tap(time, col):
            if flip:
                return weights[(time * 3 + 2 - row) * 3 + 2 - col]
            return weights[(time * 3 + row) * 3 + col]

        def data(frame, col):
            return shifted[col, frame, pl.ds(row, TH)].reshape(half, chan)

        for out in range(FR):
            terms = [(frame, time, col) for frame, time in sources[out] for col in range(3)]
            if not terms:
                continue
            if joined:
                values = jnp.concatenate([data(frame, col) for frame, _, col in terms], axis=1)
                taps = jnp.concatenate([tap(time, col) for _, time, col in terms], axis=dims[0][1][0])
                result = lax.dot_general(values, taps, dims, preferred_element_type=F32)
            else:
                result = None
                for frame, time, col in terms:
                    term = lax.dot_general(data(frame, col), tap(time, col), dims, preferred_element_type=F32)
                    result = term if result is None else result + term
            total[out * half : (out + 1) * half, :] += result
        return carry

    if first:
        total[...] = jnp.zeros(total.shape, F32)
    lax.fori_loop(0, 3, one, 0)


CHUNK = 128


def chunks(body):
    for step in range(VOX // CHUNK):
        body(slice(step * CHUNK, (step + 1) * CHUNK), step)


def put_tile(tile, edges, step, values):
    rows = CHUNK // TW
    chan = values.shape[-1]
    for at in range(rows):
        line = step * rows + at
        edges[0, line : line + 1, 0:chan] = values[at * TW : at * TW + 1]
        edges[1, line : line + 1, 0:chan] = values[at * TW + TW - 1 : at * TW + TW]
    frame, row = divmod(step * rows, TH)
    values = values.astype(BF16).reshape(rows, TW, chan)
    if len(tile.shape) == 3:
        tile[row + 1 : row + 1 + rows, :, frame * chan : (frame + 1) * chan] = values
    else:
        tile[frame, row + 1 : row + 1 + rows] = values


def picture_copies(place, tile, field, send, recv):
    t, r, c = place
    items = []
    number = 0
    for dr in range(N_ROW):
        for dc in (-1, 0, 1):
            if dr == 0 and dc == 0:
                continue
            items.append(
                pltpu.make_async_remote_copy(
                    src_ref=tile,
                    dst_ref=field.at[1 - dc, :, pl.ds(pl.multiple_of(r * TH, TH), TH), :],
                    send_sem=send.at[number],
                    recv_sem=recv.at[number],
                    device_id=(t, wrap(r, dr, N_ROW), wrap(c, dc, N_COL)),
                    device_id_type=MESH,
                )
            )
            number += 1
    return items


def pack_pictures(tile, packed):
    for group in range(2):
        total = tile[4 * group]
        for number in range(4 * group + 1, min(4 * group + 4, 6)):
            total = total + pltpu.roll(tile[number], TW * (number % 4), 1)
        packed[group] = total


def canvas(place, packed, field):
    t, r, c = place
    field[1, :, pl.ds(pl.multiple_of(r * TH, TH), TH), :] = packed[...]
    lane = iota((N_ROW * TH, 128), 1)
    low = jnp.where(c == 0, TW, 0)
    high = jnp.where(c == N_COL - 1, 2 * TW, 3 * TW)
    pictures = []
    for number in range(6):
        group, place_in = divmod(number, 4)
        total = jnp.zeros((N_ROW * TH, 128), F32)
        for side in range(3):
            turn = (TW * (side - place_in)) % 128
            moved = pltpu.roll(field[side, group], turn, 1) if turn else field[side, group]
            total = jnp.where((lane >= TW * side) & (lane < TW * side + TW), moved, total)
        pictures.append(jnp.where((lane >= low) & (lane < high), total, 0.0))
    return jnp.concatenate(pictures, axis=0)


def high_dot(a, b):
    return jnp.dot(a, b, precision=HIGH, preferred_element_type=F32)


def thirds(values):
    high = values.astype(BF16).astype(F32)
    rest = values - high
    middle = rest.astype(BF16).astype(F32)
    return jnp.concatenate([high, middle, rest - middle], axis=0)


WINDOW = TH + 16


def picture_bands(place, across, down, down_own):
    across[...] = band(iota((128, 128), 0) - iota((128, 128), 1), True)
    out, source = iota(down.shape, 0), iota(down.shape, 1)
    picture = sum((out >= WINDOW * at).astype(jnp.int32) for at in range(1, 6))
    line = out - WINDOW * picture + (place[1] * TH - 8)
    down[...] = band(line - (source & 31), (picture == (source >> 5)) & (line >= 0) & (line < N_ROW * TH))
    out, source = iota(down_own.shape, 0), iota(down_own.shape, 1)
    picture = sum((source >= WINDOW * at).astype(jnp.int32) for at in range(1, 6))
    down_own[...] = band((out & 7) + 8 - (source - WINDOW * picture), (out >> 3) == picture)


def blurred(maps, across, down):
    rows = maps[0].shape[0]
    wide = high_dot(jnp.concatenate(maps, axis=0), across[...])
    wide = jnp.concatenate([wide[m * rows : (m + 1) * rows] for m in range(len(maps))], axis=1)
    result = high_dot(down[...], wide)
    return [result[:, m * 128 : (m + 1) * 128] for m in range(len(maps))]


def picture_loss(place, x_tile, y_tile, x_packed, x_field, y, mean_y, square_y, bands, spread):
    t, r, c = place
    across, down, down_own = bands
    x = canvas(place, x_packed, x_field)
    mean_x, square_x, cross = blurred([x, x * x, x * y], across, down)
    rows = 6 * WINDOW
    var_x = square_x - mean_x * mean_x
    var_y = square_y - mean_y * mean_y
    covar = cross - mean_x * mean_y
    numer_a = 2.0 * mean_x * mean_y + SSIM_CONST_A
    numer_b = 2.0 * covar + SSIM_CONST_B
    denom_a = mean_x * mean_x + mean_y * mean_y + SSIM_CONST_A
    denom_b = var_x + var_y + SSIM_CONST_B
    denom_all = denom_a * denom_b
    ssim = numer_a * numer_b / denom_all
    slope_mean = (2.0 * mean_y * numer_b - 2.0 * mean_y * numer_a) / denom_all - ssim * (
        2.0 * mean_x / denom_a - 2.0 * mean_x / denom_b
    )
    slope_square = -ssim / denom_b
    slope_cross = 2.0 * numer_a / denom_all
    lane, line = iota((rows, 128), 1), iota((rows, 128), 0)
    line = line - WINDOW * sum((line >= WINDOW * at).astype(jnp.int32) for at in range(1, 6)) + (r * TH - 8)
    low = jnp.where(c == 0, TW, TW - 5)
    high = jnp.where(c == N_COL - 1, 2 * TW, 2 * TW + 5)
    inside = (lane >= low) & (lane < high) & (line >= 0) & (line < N_ROW * TH)
    mine = (lane >= TW) & (lane < 2 * TW) & (line >= r * TH) & (line < r * TH + TH)
    loss = jnp.sum(jnp.where(mine, 1.0 - ssim, 0.0), axis=0, keepdims=True)
    adjoint = [jnp.where(inside, slope * (-1.0 / PIX), 0.0) for slope in (slope_mean, slope_square, slope_cross)]
    pulled = blurred(adjoint, across, down_own)
    x_own = pltpu.roll(x_tile[...].reshape(48, 128), TW, 1)
    y_own = pltpu.roll(y_tile[...].reshape(48, 128), TW, 1)
    lane = iota((48, 128), 1)
    mine = (lane >= TW) & (lane < 2 * TW)
    diff = x_own - y_own
    size = jnp.abs(diff)
    huber = jnp.where(size < HUBER_BETA, 0.5 * diff * diff / HUBER_BETA, size - 0.5 * HUBER_BETA)
    loss = (loss + jnp.sum(jnp.where(mine, huber, 0.0), axis=0, keepdims=True)) / PIX
    grad = jnp.clip(diff / HUBER_BETA, -1.0, 1.0) / PIX + pulled[0] + 2.0 * x_own * pulled[1] + y_own * pulled[2]
    grad = pltpu.roll(jnp.where(mine, grad, 0.0), 128 - TW, 1)
    spread[...] = jnp.zeros(spread.shape, F32)
    for color in range(3):
        for frame in range(FR):
            at = (color * FR + frame) * TH
            spread[pl.ds(frame * 64 + color, TH, stride=8), :] = grad[at : at + TH]
    return loss


def axis_line(place, axis):
    t, r, c = place
    if axis == "z":
        return t, lambda step: (wrap(t, step, N_TM), r, c)
    if axis == "y":
        return r, lambda step: (t, wrap(r, step, N_ROW), c)
    return c >> 1, lambda step: (t, r, wrap(c, 2 * step, N_COL))


class Reduce:
    def __init__(self, s, place, group, result):
        self.s, self.group, self.result = s, group, result
        self.small, self.large = SMALL[group], LARGE[group]
        self.core = place[2] & 1
        self.mate = (place[0], place[1], place[2] + 1 - 2 * self.core)
        self.lines = [[axis_line(place, axis) for axis in AXES[part]] for part in range(PARTS)]

    def at(self, part, phase, step=0):
        return lax.rem(self.lines[part][phase][0] + (step + 4), 4)

    def copy(self, part, phase, stage, step, src, dst):
        sem = ((self.group * PARTS + part) * 5 + stage) * 3 + step - 1
        return pltpu.make_async_remote_copy(
            src_ref=src,
            dst_ref=dst,
            send_sem=self.s.ring_send.at[sem],
            recv_sem=self.s.ring_recv.at[sem],
            device_id=self.lines[part][phase][1](step),
            device_id_type=MESH,
        )

    def base(self, part):
        return START[self.group] + part * SPAN[self.group]

    def lines_of(self, part, step):
        return pl.ds(pl.multiple_of(self.base(part) + self.at(part, 0, step) * self.large, 16), self.large)

    def region(self, part, large, small=None, core=None):
        core = self.core if core is None else core
        base = self.base(part) + self.at(part, 0, large) * self.large
        if small is None:
            return self.result.at[core, pl.ds(pl.multiple_of(base, 16), self.large), :]
        base = base + self.at(part, 1, small) * self.small
        return self.result.at[core, pl.ds(pl.multiple_of(base, 16), self.small), :]

    def send(self, part, stage, step):
        s, group = self.s, self.group
        if stage == 0:
            where = (group, part, step - 1, pl.ds(0, self.large))
            return self.copy(part, 0, 0, step, s.stage0.at[where], s.inbox0.at[where])
        if stage == 1:
            where = (group, part, step - 1, pl.ds(0, self.small))
            return self.copy(part, 1, 1, step, s.stage1.at[where], s.inbox1.at[where])
        if stage == 2:
            block = s.last.at[group, part, self.at(part, 2), pl.ds(0, self.small)]
            return self.copy(part, 2, 2, step, block, block)
        block = self.region(part, 0, 0) if stage == 3 else self.region(part, 0)
        return self.copy(part, 1 if stage == 3 else 0, stage, step, block, block)

    def arrival(self, part, stage, step):
        if stage < 2:
            return self.send(part, stage, step)
        if stage == 2:
            block = self.s.last.at[self.group, part, self.at(part, 2, -step), pl.ds(0, self.small)]
            return self.copy(part, 2, 2, step, block, block)
        block = self.region(part, 0, -step) if stage == 3 else self.region(part, -step)
        return self.copy(part, 1 if stage == 3 else 0, stage, step, block, block)

    def share(self, part, large, arriving=False):
        block = self.region(part, large, core=1 - self.core if arriving else None)
        sem = (self.group * PARTS + part) * 4 + (large + 4) % 4
        return pltpu.make_async_remote_copy(
            src_ref=block,
            dst_ref=block,
            send_sem=self.s.share_send.at[sem],
            recv_sem=self.s.share_recv.at[sem],
            device_id=self.mate,
            device_id_type=MESH,
        )

    def run(self, stage):
        s, group = self.s, self.group
        if stage == 5:
            for earlier in range(4):
                self.left(earlier)
        for part in range(PARTS):
            if stage > 0:
                for step in (1, 3, 2):
                    self.arrival(part, stage - 1, step).wait_recv()
                    if stage == 5:
                        self.share(part, -step).start()
            large, small = pl.ds(0, self.large), pl.ds(0, self.small)
            if stage == 0:
                for step in (2, 1, 3):
                    s.stage0[group, part, step - 1, large, :] = s.flat[self.lines_of(part, step), :].astype(BF16)
                    self.send(part, 0, step).start()
            elif stage == 1:
                total = [s.inbox0[group, part, index, large, :].astype(F32) for index in range(3)]
                s.sum1[group, part, large, :] = s.flat[self.lines_of(part, 0), :] + (total[0] + total[1] + total[2])
                for step in (2, 1, 3):
                    at = pl.ds(pl.multiple_of(self.at(part, 1, step) * self.small, 16), self.small)
                    s.stage1[group, part, step - 1, small, :] = s.sum1[group, part, at, :].astype(BF16)
            elif stage == 2:
                own = s.sum1[group, part, pl.ds(pl.multiple_of(self.at(part, 1) * self.small, 16), self.small), :]
                total = [s.inbox1[group, part, index, small, :].astype(F32) for index in range(3)]
                s.last[group, part, self.at(part, 2), small, :] = (own + (total[0] + total[1] + total[2])).astype(LAST)
            elif stage == 3:
                total = [s.last[group, part, index, small, :].astype(F32) for index in range(4)]
                self.region(part, 0, 0)[...] = ((total[0] + total[1]) + (total[2] + total[3])).astype(BF16)
            if 0 < stage < 5:
                for step in (2, 1, 3):
                    self.send(part, stage, step).start()
            if stage == 4:
                self.share(part, 0).start()

    def left(self, stage):
        for part in range(PARTS):
            for step in (1, 2, 3):
                self.send(part, stage, step).wait_send()

    def settle(self):
        self.left(4)
        for part in range(PARTS):
            for large in range(4):
                self.share(part, large, True).wait_recv()
            for large in range(4):
                self.share(part, large).wait_send()


class Small:
    def __init__(self, s, place):
        self.s = s
        core = place[2] & 1
        self.lines = [axis_line(place, axis) for axis in "zyx"]
        self.lines.append((core, lambda step: (place[0], place[1], place[2] + 1 - 2 * core)))

    def copies(self, stage):
        at, there = self.lines[stage]
        mine = self.s.small.at[stage, at]
        return [
            pltpu.make_async_remote_copy(
                src_ref=mine,
                dst_ref=mine,
                send_sem=self.s.small_send.at[stage * 3 + step - 1],
                recv_sem=self.s.small_recv.at[stage * 3 + step - 1],
                device_id=there(step),
                device_id_type=MESH,
            )
            for step in ((1, 2, 3) if stage < 3 else (1,))
        ]

    def start(self, stage, value):
        self.s.small[stage, self.lines[stage][0]] = value
        for copy in self.copies(stage):
            copy.start()

    def finish(self, stage):
        at, there = self.lines[stage]
        count = 4 if stage < 3 else 2
        for step in range(1, count):
            block = self.s.small.at[stage, lax.rem(at + (count - step), count)]
            pltpu.make_async_remote_copy(
                src_ref=block,
                dst_ref=block,
                send_sem=self.s.small_send.at[stage * 3 + step - 1],
                recv_sem=self.s.small_recv.at[stage * 3 + step - 1],
                device_id=there(step),
                device_id_type=MESH,
            ).wait_recv()
        value = self.s.small[stage, 0]
        for index in range(1, count):
            value = value + self.s.small[stage, index]
        return value

    def settle(self):
        for stage in range(4):
            for copy in self.copies(stage):
                copy.wait_send()


def kernel(feat_hbm, w1_hbm, w2_hbm, ws_hbm, head, targ, result, small_out, *scratch):
    s = types.SimpleNamespace(**dict(zip(SCRATCH_NAMES, scratch)))
    t, r, c = lax.axis_index("tm"), lax.axis_index("row"), lax.axis_index("col")
    place = (t, r, c)

    feat, w1, w2, ws = s.feat, s.w1, s.w2, s.ws
    loads = [
        pltpu.make_async_copy(w1_hbm, w1, s.load.at[0]),
        pltpu.make_async_copy(w2_hbm, w2, s.load.at[1]),
        pltpu.make_async_copy(feat_hbm, feat, s.load.at[2]),
        pltpu.make_async_copy(ws_hbm, ws, s.load.at[3]),
    ]
    loads[2].start()
    barrier = pltpu.get_barrier_semaphore()
    around = [(0, dr, dc) for dr in (-1, 0, 1, 2) for dc in (-1, 0, 1) if (dr, dc) != (0, 0)]
    around += [(-1, 0, 0), (1, 0, 0), (2, 0, 0), (0, 0, -2), (0, 0, 2), (0, 0, 4)]
    for dt, dr, dc in around:
        pl.semaphore_signal(
            barrier,
            inc=1,
            device_id=(wrap(t, dt, N_TM), wrap(r, dr, N_ROW), wrap(c, dc, N_COL)),
            device_id_type=MESH,
        )

    core = c & 1
    mate = (t, r, c + 1 - 2 * core)

    def to_mate(number, src, dst):
        return pltpu.make_async_remote_copy(
            src_ref=src,
            dst_ref=dst,
            send_sem=s.mate_send.at[number],
            recv_sem=s.mate_recv.at[number],
            device_id=mate,
            device_id_type=MESH,
        )

    mates = [
        to_mate(0, feat, s.mate0.at[3, pl.ds(FR, FR), pl.ds(1, TH)]),
        to_mate(1, s.shift0.at[pl.ds(0, 3), pl.ds(FR, FR)], s.mate0.at[pl.ds(0, 3), pl.ds(FR, FR)]),
        to_mate(2, s.shift0.at[pl.ds(0, 3), pl.ds(0, FR)], s.mate0.at[pl.ds(0, 3), pl.ds(0, FR)]),
        to_mate(3, s.shift1.at[:, pl.ds(FR, FR)], s.mate1.at[:, pl.ds(FR, FR)]),
        to_mate(4, s.shift1.at[:, pl.ds(0, FR)], s.mate1.at[:, pl.ds(0, FR)]),
        to_mate(5, s.grads.at[1, :, pl.ds(0, VOX)], s.grads.at[1, :, pl.ds(VOX, VOX)]),
        to_mate(6, s.grads.at[0, :, pl.ds(0, VOX)], s.grads.at[0, :, pl.ds(VOX, VOX)]),
    ]

    def tile_rows(step):
        return divmod(step * (CHUNK // TW), TH)

    def features(step):
        frame, row = tile_rows(step)
        return feat[frame, pl.ds(row, CHUNK // TW)].reshape(CHUNK, C_IN)

    for number in (0, 1, 3):
        loads[number].start()
    loads[2].wait()

    def act(rows, step):
        raw = features(step)
        frame, row = tile_rows(step)
        s.shift0[3, FR + frame, pl.ds(row + 1, CHUNK // TW)] = raw.reshape(CHUNK // TW, TW, C_IN)
        values = silu_forward(raw.astype(F32))
        put_tile(s.own0, s.columns, step, values)

    chunks(act)
    s.target[...] = jnp.zeros(s.target.shape, F32)
    s.target[:, :, 0:TW] = targ[...]
    pack_pictures(s.target, s.y_packed)
    pl.semaphore_wait(barrier, len(around))

    halo0 = Halo(place, 1, C_IN, s.own0, s.other0, s.rims0, s.edges0, s.lines0, s.send0, s.recv0)
    halo1 = Halo(place, 1, C_MID, s.own1, s.other1, s.rims1, s.edges1, s.lines1, s.send1, s.recv1)
    halo2 = Halo(place, -1, C_MID, s.own2, s.other2, s.rims2, s.edges2, s.lines1, s.send2, s.recv2)
    halo0.start(s.columns)
    y_copies = picture_copies(place, s.y_packed, s.y_field, s.send_y, s.recv_y)
    for copy in y_copies:
        copy.start()
    bands = (s.across, s.down, s.down_own)
    picture_bands(place, *bands)

    halo0.arrived(0)
    halo0.shift(0, s.shift0, FR)
    loads[0].wait()
    convolve(s.shift0, w1, s.pre, ([(2, 2)], [(3, 2), (2, 1)]), NT, False, True)
    halo0.arrived(1)
    halo0.shift(1, s.shift0, 0)
    convolve(s.shift0, w1, s.pre, ([(0, 0), (1, 1)], [(1, 0)]), NT, False, False)

    def act_first(rows, step):
        values = silu_forward(s.pre[rows, :])
        put_tile(s.own1, s.columns, step, values)

    chunks(act_first)
    halo1.start(s.columns)
    for number in (0, 1, 2):
        mates[number].start()
    for copy in y_copies:
        copy.wait_recv()
    s.y_full[...] = canvas(place, s.y_packed, s.y_field)
    s.y_blur[0], s.y_blur[1] = blurred([s.y_full[...], s.y_full[...] * s.y_full[...]], s.across, s.down)
    halo1.arrived(0)
    halo1.shift(0, s.shift1, FR)
    loads[1].wait()
    loads[3].wait()
    convolve(s.shift1, w2, s.block, ([(2, 2)], [(3, 2), (2, 1)]), NN, False, True)

    def shortcut(rows, step):
        s.block[rows, :] += lax.dot_general(features(step), ws[...], NT, preferred_element_type=F32)

    chunks(shortcut)
    halo1.arrived(1)
    halo1.shift(1, s.shift1, 0)
    convolve(s.shift1, w2, s.block, ([(0, 0), (1, 1)], [(1, 0)]), NN, False, False)

    s.headf[...] = jnp.zeros(s.headf.shape, F32)
    s.headf[0:3, :] = head[...].astype(F32)

    def act_block(rows, step):
        s.values1[rows, :] = silu_forward(s.block[rows, :]).astype(BF16).astype(F32)

    chunks(act_block)
    lane = iota((8, 128), 1)
    for part in range(4):
        rows = slice(part * 128, part * 128 + 128)
        color = lax.dot_general(
            s.headf[...].astype(BF16), s.values1[rows, :].astype(BF16), NT, preferred_element_type=F32
        )
        for piece in range(4):
            moved = color if piece == 0 else pltpu.roll(color, 128 - TW * piece, 1)
            at = (4 * part + piece) * 8
            s.spread[at : at + 8, :] = jnp.where(lane < TW, moved, 0.0)
    for color in range(3):
        for frame in range(FR):
            s.image[color * FR + frame] = s.spread[pl.ds(frame * 64 + color, TH, stride=8), :]

    pack_pictures(s.image, s.x_packed)
    x_copies = picture_copies(place, s.x_packed, s.x_field, s.send_x, s.recv_x)
    for copy in x_copies:
        copy.start()
    for number in (3, 4):
        mates[number].start()
    for copy in x_copies:
        copy.wait_recv()
    loss = picture_loss(
        place, s.image, s.target, s.x_packed, s.x_field, s.y_full[...], s.y_blur[0], s.y_blur[1], bands, s.spread
    )

    grad_head = None
    for part in range(4):
        rows = slice(part * 128, part * 128 + 128)
        color = None
        for piece in range(4):
            at = (4 * part + piece) * 8
            held = s.spread[at : at + 8, :]
            color = held if piece == 0 else color + pltpu.roll(held, TW * piece, 1)
        split = thirds(color)
        s.colors[part] = jnp.concatenate([split, jnp.zeros((128 - 24, 128), F32)], axis=0).T[:, 0:24].astype(BF16)
        term = jnp.dot(split.astype(BF16), s.values1[rows, :].astype(BF16), preferred_element_type=F32)
        grad_head = term if grad_head is None else grad_head + term
    grad_head = grad_head[0:8] + (grad_head[8:16] + grad_head[16:24])
    heads = jnp.concatenate([s.headf[...]] * 3, axis=0).astype(BF16)
    tail = jnp.concatenate([grad_head[:, 128:], jnp.zeros((8, 64), F32)], axis=1)
    small = Small(s, place)
    small.start(
        0,
        jnp.concatenate([grad_head[0:3, 0:128], tail[0:3], jnp.zeros((1, 128), F32), loss], axis=0),
    )

    def back_block(rows, step):
        grad = jnp.dot(s.colors[step], heads, preferred_element_type=F32)
        values = silu_backward(s.block[rows, :], grad)
        s.values1[rows, :] = values
        put_tile(s.own2, s.columns, step, values)

    chunks(back_block)
    halo2.start(s.columns)
    s.grads[1, :, 0:VOX] = s.values1[...].T.astype(BF16)
    mates[5].start()
    groups = [Reduce(s, place, group, result) for group in range(GROUPS)]
    s.flat[FIRST_FILLED + C_MID : START[2], :] = jnp.zeros((START[2] - FIRST_FILLED - C_MID, 128), F32)
    small.start(1, small.finish(0))
    for number in (3, 4, 5):
        mates[number].wait_recv()

    def patches(mine, theirs, slot):
        extra = (slot == 27).astype(jnp.int32)
        time, row, col = slot // 9 - extra, lax.rem(slot // 3, 3) + extra, lax.rem(slot, 3) + 3 * extra
        where = (col, pl.ds(time, FR), pl.ds(row, TH))
        chan = mine.shape[-1]
        return jnp.concatenate([mine[where].reshape(VOX, chan), theirs[where].reshape(VOX, chan)], axis=0)

    def second(pair, carry):
        halves = []
        for which in range(2):
            slot = jnp.minimum(core * SLOTS + pair * 2 + which, 26)
            data = patches(s.shift1, s.mate1, slot)
            halves.append(lax.dot_general(s.grads[1], data, NN, preferred_element_type=F32).T)
        at = pl.multiple_of(START[2] + pair * (3 * C_MID), 16)
        s.flat[pl.ds(at, C_MID), :] = halves[0][:, 0:128]
        s.flat[pl.ds(at + C_MID, C_MID), :] = halves[1][:, 0:128]
        s.flat[pl.ds(rest_at(pair), C_MID), :] = jnp.concatenate([halves[0][:, 128:], halves[1][:, 128:]], axis=1)
        return carry

    lax.fori_loop(0, 2, second, 0)
    halo2.arrived(0)
    lax.fori_loop(2, SLOTS // 2, second, 0)
    groups[2].run(0)
    halo2.shift(0, s.shift2, 0)
    convolve(s.shift2, w2, s.back, ([(0, 2), (1, 1)], [(1, 2)]), NT, True, True)
    halo2.arrived(1)
    halo2.shift(1, s.shift2, FR)
    convolve(s.shift2, w2, s.back, ([(2, 0)], [(3, 0), (2, 1)]), NT, True, False)

    def back_first(rows, step):
        s.values1[rows, :] = silu_backward(s.pre[rows, :], s.back[rows, :])

    chunks(back_first)
    s.grads[0, :, 0:VOX] = s.values1[...].T.astype(BF16)
    mates[6].start()
    groups[2].run(1)
    small.start(2, small.finish(1))
    for number in (0, 1, 2, 6):
        mates[number].wait_recv()

    def put_slot(step, values):
        at = pl.multiple_of(step * (3 * C_MID), C_MID)
        for block in range(3):
            s.flat[pl.ds(at + block * C_MID, C_MID), :] = values[:, block * 128 : block * 128 + 128]

    def first(pair, carry):
        data = [patches(s.shift0, s.mate0, core * SLOTS + 2 * pair + which) for which in range(2)]
        data = jnp.concatenate(data, axis=1)
        both = lax.dot_general(s.grads[0], data, NN, preferred_element_type=F32)
        put_slot(2 * pair, both[:, 0:C_IN])
        put_slot(2 * pair + 1, both[:, C_IN:])
        return carry

    def first_alone(step):
        slot = core * SLOTS + step
        data = patches(s.shift0, s.mate0, slot)
        grads = s.grads[(slot == 27).astype(jnp.int32)]
        put_slot(step, lax.dot_general(grads, data, NN, preferred_element_type=F32))

    lax.fori_loop(0, EARLY // 2, first, 0)
    groups[0].run(0)
    lax.fori_loop(EARLY // 2, SLOTS // 2 - 1, first, 0)
    first_alone(SLOTS - 2)
    first_alone(SLOTS - 1)
    groups[1].run(0)
    groups[0].run(1)
    groups[2].run(2)
    groups[1].run(1)
    small.start(3, small.finish(2))
    groups[0].run(2)
    groups[2].run(3)
    groups[1].run(2)
    groups[0].run(3)
    small_out[...] = small.finish(3)
    groups[2].run(4)
    groups[1].run(3)
    groups[0].run(4)
    groups[1].run(4)
    for halo in (halo0, halo1, halo2):
        halo.sent()
    for copy in x_copies + y_copies + mates:
        copy.wait_send()
    small.settle()
    groups[0].run(5)
    groups[2].run(5)
    groups[0].settle()
    groups[2].settle()
    groups[1].run(5)
    groups[1].settle()


def halo_scratch(number, chan, copies):
    tile = (FR, TH + 2, TW, chan) if chan % 128 == 0 else (TH + 2, TW, FR * chan)
    return [
        (f"own{number}", pltpu.VMEM(tile, BF16)),
        (f"other{number}", pltpu.VMEM(tile, BF16)),
        (f"rims{number}", pltpu.VMEM((2, 2, 3, FR * TH, chan), BF16)),
        (f"edges{number}", pltpu.VMEM((2, FR * TH, chan), BF16)),
        (f"shift{number}", pltpu.VMEM((copies, 2 * FR, TH + 2, TW, chan), BF16)),
        (f"send{number}", pltpu.SemaphoreType.DMA((12,))),
        (f"recv{number}", pltpu.SemaphoreType.DMA((12,))),
    ]


SCRATCH = (
    halo_scratch(0, C_IN, 4)
    + halo_scratch(1, C_MID, 3)
    + halo_scratch(2, C_MID, 3)
    + [
        ("w1", pltpu.VMEM((27, C_MID, C_IN), BF16)),
        ("w2", pltpu.VMEM((27, C_MID, C_MID), BF16)),
        ("feat", pltpu.VMEM((FR, TH, TW, C_IN), BF16)),
        ("ws", pltpu.VMEM((C_MID, C_IN), BF16)),
        ("load", pltpu.SemaphoreType.DMA((4,))),
        ("lines0", pltpu.VMEM((2, FR, 16, C_IN), F32)),
        ("lines1", pltpu.VMEM((2, FR, 16, C_MID), F32)),
        ("columns", pltpu.VMEM((2, FR * TH, C_IN), F32)),
        ("values1", pltpu.VMEM((VOX, C_MID), F32)),
        ("pre", pltpu.VMEM((VOX, C_MID), F32)),
        ("block", pltpu.VMEM((VOX, C_MID), F32)),
        ("back", pltpu.VMEM((VOX, C_MID), F32)),
        ("grads", pltpu.VMEM((2, C_MID, 2 * VOX), BF16)),
        ("mate0", pltpu.VMEM((4, 2 * FR, TH + 2, TW, C_IN), BF16)),
        ("mate1", pltpu.VMEM((3, 2 * FR, TH + 2, TW, C_MID), BF16)),
        ("mate_send", pltpu.SemaphoreType.DMA((7,))),
        ("mate_recv", pltpu.SemaphoreType.DMA((7,))),
        ("flat", pltpu.VMEM((LINES, 128), F32)),
        ("stage0", pltpu.VMEM((GROUPS, PARTS, 3, max(LARGE), 128), BF16)),
        ("inbox0", pltpu.VMEM((GROUPS, PARTS, 3, max(LARGE), 128), BF16)),
        ("sum1", pltpu.VMEM((GROUPS, PARTS, max(LARGE), 128), F32)),
        ("stage1", pltpu.VMEM((GROUPS, PARTS, 3, max(SMALL), 128), BF16)),
        ("inbox1", pltpu.VMEM((GROUPS, PARTS, 3, max(SMALL), 128), BF16)),
        ("last", pltpu.VMEM((GROUPS, PARTS, 4, max(SMALL), 128), LAST)),
        ("ring_send", pltpu.SemaphoreType.DMA((GROUPS * PARTS * 15,))),
        ("ring_recv", pltpu.SemaphoreType.DMA((GROUPS * PARTS * 15,))),
        ("share_send", pltpu.SemaphoreType.DMA((GROUPS * PARTS * 4,))),
        ("share_recv", pltpu.SemaphoreType.DMA((GROUPS * PARTS * 4,))),
        ("small", pltpu.VMEM((4, 4, 8, 128), F32)),
        ("small_send", pltpu.SemaphoreType.DMA((12,))),
        ("small_recv", pltpu.SemaphoreType.DMA((12,))),
        ("headf", pltpu.VMEM((8, C_MID), F32)),
        ("spread", pltpu.VMEM((136, 128), F32)),
        ("colors", pltpu.VMEM((4, 128, 24), BF16)),
        ("image", pltpu.VMEM((6, TH, 128), F32)),
        ("target", pltpu.VMEM((6, TH, 128), F32)),
        ("x_packed", pltpu.VMEM((2, TH, 128), F32)),
        ("y_packed", pltpu.VMEM((2, TH, 128), F32)),
        ("x_field", pltpu.VMEM((3, 2, N_ROW * TH, 128), F32)),
        ("y_field", pltpu.VMEM((3, 2, N_ROW * TH, 128), F32)),
        ("across", pltpu.VMEM((128, 128), F32)),
        ("down", pltpu.VMEM((6 * WINDOW, 6 * N_ROW * TH), F32)),
        ("down_own", pltpu.VMEM((6 * TH, 6 * WINDOW), F32)),
        ("y_full", pltpu.VMEM((6 * N_ROW * TH, 128), F32)),
        ("y_blur", pltpu.VMEM((2, 6 * WINDOW, 128), F32)),
        ("send_x", pltpu.SemaphoreType.DMA((11,))),
        ("recv_x", pltpu.SemaphoreType.DMA((11,))),
        ("send_y", pltpu.SemaphoreType.DMA((11,))),
        ("recv_y", pltpu.SemaphoreType.DMA((11,))),
    ]
)
SCRATCH_NAMES = [name for name, _ in SCRATCH]


def widen(flat, small_ref, g1, gs, g2, gh, loss, wide1, wide2, sems):
    copies = []

    def one1(slot, carry):
        core, step = slot // SLOTS, lax.rem(slot, SLOTS)
        at = pl.multiple_of(step * (3 * C_MID), C_MID)
        for block in range(3):
            rows = flat[core, pl.ds(at + block * C_MID, C_MID), :]
            wide1[slot, :, block * 128 : block * 128 + 128] = rows.astype(F32)
        return carry

    def one2(pair, carry):
        core, step = pair // (SLOTS // 2), lax.rem(pair, SLOTS // 2)
        at = pl.multiple_of(START[2] + step * (3 * C_MID), 16)
        wide2[2 * pair, :, 0:128] = flat[core, pl.ds(at, C_MID), :].astype(F32)
        wide2[2 * pair + 1, :, 0:128] = flat[core, pl.ds(at + C_MID, C_MID), :].astype(F32)
        rest = flat[core, pl.ds(rest_at(step), C_MID), :].astype(F32)
        wide2[2 * pair, :, 128:] = rest[:, 0:64]
        wide2[2 * pair + 1, :, 128:] = rest[:, 64:]
        return carry

    cuts = (0, 2, 6, 12, 18, 24, 28)
    for low, high in zip(cuts[:-1], cuts[1:]):
        rows = pl.ds(low, min(high, 27) - low)
        lax.fori_loop(low, high, one1, 0)
        copies.append(pltpu.make_async_copy(wide1.at[rows], g1.at[rows], sems.at[len(copies)]))
        copies[-1].start()
        lax.fori_loop(low // 2, high // 2, one2, 0)
        copies.append(pltpu.make_async_copy(wide2.at[rows], g2.at[rows], sems.at[len(copies)]))
        copies[-1].start()
    copies.append(pltpu.make_async_copy(wide1.at[27], gs, sems.at[len(copies)]))
    copies[-1].start()
    gh[:, 0:128] = small_ref[0:3, :]
    gh[:, 128:] = small_ref[3:6, 0:64]
    loss[...] = jnp.sum(small_ref[7:8, :], axis=1, keepdims=True) / (N_TM * N_ROW * N_COL)
    for copy in copies:
        copy.wait()


def body(features, conv_first, conv_second, shortcut_weight, head_weight, target_frames):
    vmem, hbm = pl.BlockSpec(memory_space=pltpu.VMEM), pl.BlockSpec(memory_space=pl.ANY)
    flat, small = pl.pallas_call(
        kernel,
        out_shape=[pltpu.VMEM((2, LINES, 128), BF16), pltpu.VMEM((8, 128), F32)],
        in_specs=[hbm, hbm, hbm, hbm, vmem, vmem],
        out_specs=[vmem] * 2,
        scratch_shapes=[shape for _, shape in SCRATCH],
        compiler_params=pltpu.CompilerParams(
            collective_id=0, has_side_effects=True, vmem_limit_bytes=52 * 1024 * 1024
        ),
    )(
        features,
        conv_first.transpose(0, 1, 2, 4, 3).reshape(27, C_MID, C_IN),
        conv_second.reshape(27, C_MID, C_MID),
        shortcut_weight.T,
        head_weight.T,
        target_frames.reshape(6, TH, TW),
    )
    g1, gs, g2, gh, loss = pl.pallas_call(
        widen,
        out_shape=[
            jax.ShapeDtypeStruct((27, C_MID, C_IN), F32),
            jax.ShapeDtypeStruct((C_MID, C_IN), F32),
            jax.ShapeDtypeStruct((27, C_MID, C_MID), F32),
            jax.ShapeDtypeStruct((3, C_MID), F32),
            jax.ShapeDtypeStruct((1, 1), F32),
        ],
        in_specs=[vmem] * 2,
        out_specs=[hbm] * 3 + [vmem] * 2,
        scratch_shapes=[
            pltpu.VMEM((28, C_MID, C_IN), F32),
            pltpu.VMEM((28, C_MID, C_MID), F32),
            pltpu.SemaphoreType.DMA((15,)),
        ],
        compiler_params=pltpu.CompilerParams(vmem_limit_bytes=40 * 1024 * 1024),
    )(flat, small)
    return (
        g1.reshape(3, 3, 3, C_MID, C_IN).transpose(0, 1, 2, 4, 3),
        g2.reshape(3, 3, 3, C_MID, C_MID),
        gs.T,
        gh.T,
        loss.reshape(()),
    )


def solution(mesh):
    return jax.shard_map(
        body,
        mesh=mesh,
        in_specs=(P("tm", "row", "col", None), P(), P(), P(), P(), P(None, "tm", "row", "col")),
        out_specs=(P(), P(), P(), P(), P()),
        check_vma=False,
    )
```
